128 devices in a mesh: tile: 32 (over z, x, core), frame: 4 (over y).
Axes of the slice: x: 4, y: 4, z: 4, core: 2. Of those that a mesh axis runs over, the one named last changes fastest.
Arguments:
- cells: bfloat16 [4, 65536, 128], P('frame', 'tile'), may hold values from -24 to 24
- vectors: bfloat16 [8, 128], replicated, may hold values from -6 to 6
- weights: bfloat16 [4, 128, 128], replicated, may hold values from -0.5 to 0.5
- cuboid_shift: int32 [1], replicated, may hold values from 0 to 2047
- cell_upstream: bfloat16 [4, 65536, 128], P('frame', 'tile'), may hold values from -6 to 6
- vector_upstream: float32 [8, 128], replicated, may hold values from -6 to 6
Outputs:
- cell_grad: bfloat16 [4, 65536, 128], P('frame', 'tile')
- weight_grad: float32 [4, 128, 128], replicated
- vector_grad: float32 [8, 128], replicated
The draws below stay inside these ranges and needn't reach their ends.
All inputs are finite; a program needn't handle non-finite values.
Results may differ from the reference program's by a relative error of at most 0.008.
The reference program's roundings to bfloat16 on the way count: a program that leaves them out, or rounds other values in their place, can miss the bound.
Values may be sent and summed in bfloat16 or wider, within the bound.
No kernel may reach another device: no remote copies, remote signals or barrier semaphores. Data moves between devices by JAX's collectives and lax.ppermute only.
A program may use at most 64 MiB of HBM per device.

```python
import math
import jax
import jax.numpy as jnp
from jax import lax

CH = 128
HEADS = 4
HDIM = 32
GLOBALS = 8
FRAMES = 4
SPAN = 4
CELLS_DEV = 2048
CELLS = 65536
CUBOID_LEN = 512
N_TILE = 32
N_FRAME = 4


def draw_cells(key, part):
    key = jax.random.fold_in(key, 11)
    base_key, scale_key = jax.random.split(key, 2)
    values = jax.random.normal(base_key, (FRAMES, CELLS, CH), jnp.float32)
    row_scale = jnp.exp(jax.random.uniform(scale_key, (FRAMES, CELLS, 1), jnp.float32, 0.0, math.log(2.0)))
    values = values * row_scale
    return jnp.clip(values, -24.0, 24.0).astype(jnp.bfloat16)


def draw_vectors(key, part):
    key = jax.random.fold_in(key, 13)
    base_key = jax.random.fold_in(key, 0)
    values = jax.random.normal(base_key, (GLOBALS, CH), jnp.float32)
    return jnp.clip(values, -6.0, 6.0).astype(jnp.bfloat16)


def draw_weights(key, part):
    key = jax.random.fold_in(key, 17)
    base_key = jax.random.fold_in(key, 0)
    values = jax.random.normal(base_key, (4, CH, CH), jnp.float32) / math.sqrt(CH)
    return jnp.clip(values, -0.5, 0.5).astype(jnp.bfloat16)


def levels(own_key, shape, cuts, low, largest):
    factor_of, own = 1.0, jax.random.fold_in(own_key, 6)
    for position, parts in cuts:
        heights = jnp.exp(jax.random.uniform(jax.random.fold_in(own, position), (parts,), jnp.float32, low / len(cuts), largest / len(cuts)))
        factor_of = factor_of * jnp.repeat(heights, shape[position] // parts).reshape([-1 if axis == position else 1 for axis in range(len(shape))])
    return factor_of


def gaussian(stream_key, extent, width, limit, pieces=(), kind=jnp.bfloat16):
    gain = levels(stream_key, extent, pieces, -0.22, 0.18) if pieces else 1.0
    drawn = jax.random.normal(stream_key, extent, jnp.float32) * width * gain
    return jnp.minimum(jnp.maximum(drawn, -limit), limit).astype(kind)


def setup_inputs(seed: int = 0) -> dict:
    key_of = jax.random.split(jax.random.key(seed), 7)
    return {
        "cells": draw_cells(jax.random.fold_in(key_of[6], 71), 0),
        "vectors": draw_vectors(jax.random.fold_in(key_of[6], 71), 0),
        "weights": draw_weights(jax.random.fold_in(key_of[6], 71), 0),
        "cuboid_shift": jax.random.randint(key_of[3], (1,), 0, CELLS_DEV).astype(jnp.int32),
        "cell_upstream": gaussian(key_of[4], (FRAMES, CELLS, CH), 1.0, 6.0, ((0, 4), (1, 32))),
        "vector_upstream": gaussian(key_of[5], (GLOBALS, CH), 1.0, 6.0, (), jnp.float32),
    }


highest_precision = lax.Precision.HIGHEST


def lowered(value):
    return lax.optimization_barrier(value.astype(jnp.bfloat16)).astype(jnp.float32)


def cuboid_pass(query_rows, key_matrix, value_matrix, upstream, global_key, global_value, w_out):
    logit_scale = HDIM ** -0.5
    local_score_rows = jnp.einsum('qnc,inc->nqi', query_rows, key_matrix, precision=highest_precision) * logit_scale
    s_global = jnp.einsum('lhd,ghd->hlg', query_rows, global_key, precision=highest_precision) * logit_scale
    row_top = jnp.maximum(jnp.max(local_score_rows, -1, keepdims=True), jnp.max(s_global, -1, keepdims=True))
    e_local = jnp.exp(local_score_rows - row_top)
    e_global = jnp.exp(s_global - row_top)
    row_total = jnp.sum(e_local, -1, keepdims=True) + jnp.sum(e_global, -1, keepdims=True)
    p_local = e_local / row_total
    p_global = e_global / row_total
    local_probability_rows = lowered(p_local)
    pb_global = lowered(p_global)
    attended_output = jnp.einsum('ofb,bow->fow', local_probability_rows, value_matrix, precision=highest_precision)
    attended_output = attended_output + jnp.einsum('hlg,ghd->lhd', pb_global, global_value, precision=highest_precision)
    attended_output = attended_output.reshape(attended_output.shape[0], -1).astype(jnp.bfloat16)
    attention_gradient = jnp.dot(upstream, w_out.T, preferred_element_type=jnp.float32)
    attention_gradient = lowered(attention_gradient).reshape(query_rows.shape)
    local_probability_gradient = jnp.einsum('qnc,inc->nqi', attention_gradient, value_matrix, precision=highest_precision)
    dprob_global = jnp.einsum('lhd,ghd->hlg', attention_gradient, global_value, precision=highest_precision)
    row_dot = jnp.sum(p_local * local_probability_gradient, -1, keepdims=True) + jnp.sum(p_global * dprob_global, -1, keepdims=True)
    local_score_gradient = lowered(p_local * (local_probability_gradient - row_dot) * logit_scale)
    ds_global = lowered(p_global * (dprob_global - row_dot) * logit_scale)
    query_gradient = jnp.einsum('ofb,bow->fow', local_score_gradient, key_matrix, precision=highest_precision)
    query_gradient = query_gradient + jnp.einsum('hlg,ghd->lhd', ds_global, global_key, precision=highest_precision)
    key_gradient = jnp.einsum('yqn,qyk->nyk', local_score_gradient, query_rows, precision=highest_precision)
    value_gradient = jnp.einsum('yqn,qyk->nyk', local_probability_rows, attention_gradient, precision=highest_precision)
    grad_gkey = jnp.einsum('hlg,lhd->ghd', ds_global, query_rows, precision=highest_precision)
    grad_gvalue = jnp.einsum('hlg,lhd->ghd', pb_global, attention_gradient, precision=highest_precision)
    return attended_output, query_gradient.astype(jnp.bfloat16), key_gradient, value_gradient, grad_gkey, grad_gvalue


def reference(cells, vectors, weights, cuboid_shift, cell_upstream, vector_upstream):
    owners = N_TILE * N_FRAME
    offset = cuboid_shift[0].astype(jnp.int32)
    w_qkv = weights[:3].transpose(1, 0, 2).reshape(CH, 3 * CH)
    w_out = weights[3]
    tile_ids = jnp.arange(N_TILE, dtype=jnp.int32)[:, None]
    cell_ids = jnp.arange(CELLS_DEV, dtype=jnp.int32)[None, :]
    forward_pos = ((cell_ids + offset * (tile_ids + 1)) % CELLS_DEV).astype(jnp.int32)
    backward_pos = ((cell_ids - offset * (tile_ids + 1)) % CELLS_DEV).astype(jnp.int32)

    def group(table):
        columns = table.shape[-1]
        table = table.reshape(FRAMES, N_TILE, CELLS_DEV, columns)
        table = table[:, tile_ids, forward_pos, :]
        table = table.reshape(FRAMES, N_TILE, owners, CELLS_DEV // owners // SPAN, SPAN, columns)
        return table.transpose(2, 3, 1, 0, 4, 5).reshape(-1, CUBOID_LEN, columns)

    def ungroup(table):
        columns = table.shape[-1]
        table = table.reshape(owners, -1, N_TILE, FRAMES, SPAN, columns).transpose(3, 2, 0, 1, 4, 5)
        table = table.reshape(FRAMES, N_TILE, CELLS_DEV, columns)
        table = table[:, tile_ids, backward_pos, :]
        return table.reshape(FRAMES, -1, columns)

    grouped = group(cells)
    upstream = group(cell_upstream)
    cub_count = grouped.shape[0]
    projected = jnp.dot(grouped.reshape(-1, CH), w_qkv, preferred_element_type=jnp.float32)
    projected = projected.astype(jnp.bfloat16).reshape(cub_count, CUBOID_LEN, 3 * CH)
    proj_single = lax.optimization_barrier(projected).astype(jnp.float32)
    query_rows = proj_single[..., :CH].reshape(cub_count, CUBOID_LEN, HEADS, HDIM)
    key_matrix = proj_single[..., CH:2 * CH].reshape(cub_count, CUBOID_LEN, HEADS, HDIM)
    value_matrix = proj_single[..., 2 * CH:].reshape(cub_count, CUBOID_LEN, HEADS, HDIM)
    global_proj = lowered(jnp.dot(vectors, w_qkv, preferred_element_type=jnp.float32)).reshape(GLOBALS, 3, HEADS, HDIM)
    global_query = global_proj[:, 0]
    global_key = global_proj[:, 1]
    global_value = global_proj[:, 2]

    key_flat = key_matrix.reshape(-1, HEADS, HDIM)
    value_flat = value_matrix.reshape(-1, HEADS, HDIM)
    logit_scale = HDIM ** -0.5
    global_score = jnp.einsum('ghd,nhd->hgn', global_query, key_flat, precision=highest_precision) * logit_scale
    global_top = jnp.max(global_score, -1)
    global_exp = jnp.exp(global_score - global_top[..., None])
    global_total = jnp.sum(global_exp, -1)
    global_numer = jnp.einsum('hgn,nhd->hgd', global_exp, value_flat, precision=highest_precision)
    global_att = global_numer / global_total[..., None]
    global_prob = global_exp / global_total[..., None]

    def one_cuboid(items):
        return cuboid_pass(items[0], items[1], items[2], items[3], global_key, global_value, w_out)

    attended_output, query_gradient, key_gradient, value_gradient, grad_gkey, grad_gvalue = lax.map(one_cuboid, (query_rows, key_matrix, value_matrix, upstream))

    grad_global = jnp.dot(vector_upstream, w_out.T.astype(jnp.float32), precision=highest_precision)
    grad_global = grad_global.reshape(GLOBALS, HEADS, HDIM).transpose(1, 0, 2)
    global_dprob = jnp.einsum('hgd,nhd->hgn', grad_global, value_flat, precision=highest_precision)
    global_row = jnp.sum(grad_global * global_att, -1)
    global_dscore = global_prob * (global_dprob - global_row[..., None]) * logit_scale
    key_extra = jnp.einsum('hgn,ghd->nhd', global_dscore, global_query, precision=highest_precision)
    value_extra = jnp.einsum('hgn,hgd->nhd', global_prob, grad_global, precision=highest_precision)
    grad_gquery = jnp.einsum('hgn,nhd->hgd', global_dscore, key_flat, precision=highest_precision)

    grad_qkv = jnp.concatenate([
        query_gradient.reshape(cub_count, CUBOID_LEN, CH),
        (key_gradient + key_extra.reshape(key_gradient.shape)).astype(jnp.bfloat16).reshape(cub_count, CUBOID_LEN, CH),
        (value_gradient + value_extra.reshape(value_gradient.shape)).astype(jnp.bfloat16).reshape(cub_count, CUBOID_LEN, CH)], axis=-1)
    flat_grad = grad_qkv.reshape(-1, 3 * CH)
    cell_delta = jnp.dot(flat_grad, w_qkv.T, preferred_element_type=jnp.float32).astype(jnp.bfloat16)
    cell_grad = ungroup(cell_delta.reshape(cub_count, CUBOID_LEN, CH))
    weight_part = jnp.dot(grouped.reshape(-1, CH).T, flat_grad, preferred_element_type=jnp.float32)
    out_part = jnp.dot(attended_output.reshape(-1, CH).T, upstream.reshape(-1, CH), preferred_element_type=jnp.float32)
    flat_gq = grad_gquery.transpose(1, 0, 2).reshape(GLOBALS, CH)
    flat_gk = jnp.sum(grad_gkey, 0).reshape(GLOBALS, CH)
    flat_gv = jnp.sum(grad_gvalue, 0).reshape(GLOBALS, CH)
    summed_g = jnp.stack([flat_gq, flat_gk, flat_gv])
    vector_single = vectors.astype(jnp.float32)
    global_extra = jnp.einsum('gc,sgd->scd', vector_single, summed_g, precision=highest_precision)
    att_flat = global_att.transpose(1, 0, 2).reshape(GLOBALS, CH)
    out_extra = jnp.dot(att_flat.T, vector_upstream, precision=highest_precision)
    summed_w = jnp.concatenate([weight_part, out_part], axis=1)
    weight_grad = summed_w.reshape(CH, 4, CH).transpose(1, 0, 2) + jnp.concatenate([global_extra, out_extra[None]], 0)
    vector_grad = jnp.einsum('sgd,scd->gc', summed_g, weights[:3].astype(jnp.float32), precision=highest_precision)
    return cell_grad, weight_grad, vector_grad
```

```python
import math

import jax
import jax.numpy as jnp
from jax import lax
from jax.experimental import pallas as pl
from jax.experimental.pallas import tpu as pltpu
from jax.sharding import PartitionSpec as P

CH = 128
HEADS = 4
HDIM = 32
GLOBALS = 8
PAIRS = HEADS * GLOBALS
SPAN = 4
CELLS_DEV = 2048
PEERS = 128
PEER_ROWS = CELLS_DEV // PEERS
CUBOIDS = PEER_ROWS // SPAN
TOKENS = 512
GROUP = 16
GROUP_ROWS = GROUP * PEER_ROWS
WINDOW = GROUP_ROWS + 16
MSG_ROWS = 40
SCALE = HDIM**-0.5
LOG2E = math.log2(math.e)
BF = jnp.bfloat16
F32 = jnp.float32
HIGHEST = lax.Precision.HIGHEST
NT = (((1,), (1,)), ((), ()))


def dot(a, b):
    return jnp.dot(a, b, preferred_element_type=F32)


def dot_nt(a, b):
    return lax.dot_general(a, b, NT, preferred_element_type=F32)


def iota(shape, axis):
    return lax.broadcasted_iota(jnp.int32, shape, axis)


def split3(x):
    hi = x.astype(BF)
    rest = x - hi.astype(F32)
    mid = rest.astype(BF)
    low = (rest - mid.astype(F32)).astype(BF)
    return hi, mid, low


def head_blocks(rows):
    head = iota((GLOBALS, CH), 1) // HDIM
    return jnp.concatenate([jnp.where(head == h, rows, 0.0) for h in range(HEADS)], axis=0)


def head_diagonal(blocks):
    head = iota((GLOBALS, CH), 1) // HDIM
    total = jnp.zeros((GLOBALS, CH), F32)
    for h in range(HEADS):
        total += jnp.where(head == h, blocks[h * GLOBALS : (h + 1) * GLOBALS], 0.0)
    return total


def global_rows(vectors, weight):
    return dot(vectors.astype(BF), weight).astype(BF).astype(F32)


def global_upstream(vector_upstream, w_out):
    hi, mid, low = split3(vector_upstream)
    return dot_nt(hi, w_out) + dot_nt(mid, w_out) + dot_nt(low, w_out)


def tile_offset(shift_ref):
    return (shift_ref[0] * (lax.axis_index("tile") + 1)) % CELLS_DEV


def shift_matrix(step):
    return (iota((GROUP_ROWS, WINDOW), 1) == iota((GROUP_ROWS, WINDOW), 0) + step).astype(BF)


def pack_kernel(
    shift_ref, cells_ref, up_ref, vectors_ref, weights_ref, vup_ref, msg_ref, held
):
    held[:CELLS_DEV, :CH] = cells_ref[...]
    held[:CELLS_DEV, CH:] = up_ref[...]
    held[CELLS_DEV:, :CH] = cells_ref[:WINDOW]
    held[CELLS_DEV:, CH:] = up_ref[:WINDOW]
    offset = tile_offset(shift_ref)
    mover = shift_matrix(offset % 16)
    base = offset - offset % 16
    for i in range(CELLS_DEV // GROUP_ROWS):
        start = pl.multiple_of((base + i * GROUP_ROWS) % CELLS_DEV, 16)
        moved = dot(mover, held[pl.ds(start, WINDOW), :]).astype(BF)
        peers = pl.ds(i * GROUP, GROUP)
        msg_ref[peers, 0:PEER_ROWS, :] = moved[:, :CH].reshape(GROUP, PEER_ROWS, CH)
        msg_ref[peers, PEER_ROWS : 2 * PEER_ROWS, :] = moved[:, CH:].reshape(GROUP, PEER_ROWS, CH)
    vectors = vectors_ref[...]
    query = head_blocks(global_rows(vectors, weights_ref[0])).astype(BF)
    upstream = head_blocks(global_upstream(vup_ref[...], weights_ref[3]))
    up_parts = jnp.concatenate([part.astype(F32) for part in split3(upstream)], axis=0).astype(BF)
    keys = dot(cells_ref[...], weights_ref[1]).astype(BF)
    values = dot(cells_ref[...], weights_ref[2]).astype(BF)
    score = dot_nt(query, keys) * SCALE
    dprob = dot_nt(up_parts, values)
    dprob = dprob[:PAIRS] + dprob[PAIRS : 2 * PAIRS] + dprob[2 * PAIRS :]
    top = jnp.max(score, axis=1, keepdims=True)
    weight = jnp.exp(score - top)
    total = jnp.sum(weight, axis=1, keepdims=True)
    inner = jnp.sum(weight * dprob, axis=1, keepdims=True)
    lane = iota((PAIRS, CH), 1)
    stats = jnp.where(lane == 0, top, jnp.where(lane == 1, total, jnp.where(lane == 2, inner, 0.0)))
    parts = [part.astype(F32) for part in split3(stats)] + [jnp.zeros((PAIRS, CH), F32)]
    rows = jnp.concatenate(parts, axis=0).T[:GLOBALS].astype(BF)
    msg_ref[:, 2 * PEER_ROWS :, :] = jnp.broadcast_to(rows[None], (PEERS, GLOBALS, CH))


def regroup_matrix():
    row = iota((GROUP_ROWS, GROUP_ROWS), 0)
    column = iota((GROUP_ROWS, GROUP_ROWS), 1)
    source = (row // SPAN) % GROUP * PEER_ROWS + row // (GROUP * SPAN) * SPAN + row % SPAN
    return (column == source).astype(BF)


def back_matrix():
    row = iota((GROUP_ROWS, GROUP_ROWS), 0)
    column = iota((GROUP_ROWS, GROUP_ROWS), 1)
    source = (row // SPAN) % CUBOIDS * (GROUP * SPAN) + row // PEER_ROWS * SPAN + row % SPAN
    return (column == source).astype(BF)


def owner_kernel(
    recv_ref,
    vectors_ref,
    weights_ref,
    vup_ref,
    msg_ref,
    cells_ref,
    up_ref,
    delta_ref,
    weights_t_ref,
    query_m,
    grad_m,
    w_sum,
    g_sum,
    part_ref,
):
    group_tokens = GROUP * SPAN
    mover = regroup_matrix()
    for i in range(PEERS // GROUP):
        peers = pl.ds(i * GROUP, GROUP)
        rows = jnp.concatenate(
            [
                recv_ref[peers, 0:PEER_ROWS, :].reshape(GROUP_ROWS, CH),
                recv_ref[peers, PEER_ROWS : 2 * PEER_ROWS, :].reshape(GROUP_ROWS, CH),
            ],
            axis=1,
        )
        moved = dot(mover, rows).astype(BF)
        for u in range(CUBOIDS):
            piece = moved[u * group_tokens : (u + 1) * group_tokens]
            cells_ref[u, pl.ds(i * group_tokens, group_tokens), :] = piece[:, :CH]
            up_ref[u, pl.ds(i * group_tokens, group_tokens), :] = piece[:, CH:]

    stats = recv_ref[:, 2 * PEER_ROWS :, :].astype(F32).reshape(PEERS * GLOBALS, CH)
    stats = stats + pltpu.roll(stats, CH - PAIRS, 1) + pltpu.roll(stats, CH - 2 * PAIRS, 1)
    stats = stats.reshape(PEERS, GLOBALS, CH)
    tops = stats[:, 0:1, :]
    top = jnp.max(tops, axis=0)
    summed = jnp.sum(jnp.exp(tops - top[None]) * stats, axis=0)
    row = iota((GLOBALS, CH), 0)
    lanes = jnp.where(row == 0, top, summed)
    columns = jnp.concatenate([lanes, jnp.zeros((CH - GLOBALS, CH), F32)], axis=0).T
    g_top = columns[:PAIRS, 0:1]
    g_inv = 1.0 / columns[:PAIRS, 1:2]
    g_row = columns[:PAIRS, 2:3] * g_inv

    vectors = vectors_ref[...]
    w_q, w_k, w_v, w_o = (weights_ref[i] for i in range(4))
    for i in range(3):
        weights_t_ref[i] = weights_ref[i].astype(F32).T.astype(BF)
    gq = head_blocks(global_rows(vectors, w_q))
    gk = head_blocks(global_rows(vectors, w_k))
    gv = head_blocks(global_rows(vectors, w_v))
    gg = head_blocks(global_upstream(vup_ref[...], w_o))

    def wide_t(blocks):
        return jnp.concatenate([blocks, jnp.zeros((CH - PAIRS, CH), F32)], axis=0).T

    gq_b, gk_b, gv_b = (x.astype(BF) for x in (gq, gk, gv))
    gk_t = wide_t(gk)[:, :PAIRS].astype(BF)
    gv_t = wide_t(gv)[:, :PAIRS].astype(BF)
    gg3 = [part.astype(F32) for part in split3(gg)]
    gg_parts = jnp.concatenate(gg3, axis=0).astype(BF)
    zero = jnp.zeros((PAIRS, CH), F32)
    gq_t3 = jnp.concatenate([gq, gq, gq, zero], axis=0).T.astype(BF)
    gg_t6a = jnp.concatenate([gg3[0], gg3[0], gg3[0], gg3[1]], axis=0).T.astype(BF)
    gg_t6b = jnp.concatenate([gg3[1], gg3[2], zero, zero], axis=0).T.astype(BF)

    query_m[...] = jnp.zeros_like(query_m)
    grad_m[...] = jnp.zeros_like(grad_m)
    w_sum[...] = jnp.zeros_like(w_sum)
    g_sum[...] = jnp.zeros_like(g_sum)

    def one_cuboid(u, carry):
        cells = cells_ref[u]
        upstream = up_ref[u]
        query_t = dot_nt(weights_t_ref[0], cells).astype(BF)
        key_t = dot_nt(weights_t_ref[1], cells).astype(BF)
        value_t = dot_nt(weights_t_ref[2], cells).astype(BF)
        grad_t = dot_nt(w_o, upstream).astype(BF)
        query = dot(cells, w_q).astype(BF)
        key = dot(cells, w_k).astype(BF)
        value = dot(cells, w_v).astype(BF)
        grad = dot_nt(upstream, w_o).astype(BF)
        for h in range(HEADS):
            part = slice(h * HDIM, (h + 1) * HDIM)
            query_m[h, part, :] = query_t[part]
            grad_m[h, part, :] = grad_t[part]
        s_global = dot(gk_b, query_t)
        d_global = dot(gv_b, grad_t)
        p_rows, ds_rows, out_t, dq_t, dk_t, dv_t = [], [], [], [], [], []
        for h in range(HEADS):
            part = slice(h * HDIM, (h + 1) * HDIM)
            pair = slice(h * GLOBALS, (h + 1) * GLOBALS)
            score = dot(key, query_m[h])
            dprob = dot(value, grad_m[h])
            top = jnp.maximum(
                jnp.max(score, axis=0, keepdims=True),
                jnp.max(s_global[pair], axis=0, keepdims=True),
            )
            e_local = jnp.exp2((score - top) * (SCALE * LOG2E))
            e_global = jnp.exp2((s_global[pair] - top) * (SCALE * LOG2E))
            total = jnp.sum(e_local, axis=0, keepdims=True) + jnp.sum(
                e_global, axis=0, keepdims=True
            )
            inv = 1.0 / total
            p_local = e_local * inv
            p_global = e_global * inv
            inner = jnp.sum(p_local * dprob, axis=0, keepdims=True) + jnp.sum(
                p_global * d_global[pair], axis=0, keepdims=True
            )
            p_low = p_local.astype(BF)
            ds_low = (p_local * (dprob - inner) * SCALE).astype(BF)
            p_rows.append(p_global)
            ds_rows.append(p_global * (d_global[pair] - inner) * SCALE)
            out_t.append(dot(value_t[part], p_low))
            dq_t.append(dot(key_t[part], ds_low))
            dv_t.append(dot_nt(grad_t[part], p_low))
            dk_t.append(dot_nt(query_t[part], ds_low))
        p_rows = jnp.concatenate(p_rows, axis=0).astype(BF)
        ds_rows = jnp.concatenate(ds_rows, axis=0).astype(BF)
        out_t = (jnp.concatenate(out_t, axis=0) + dot(gv_t, p_rows)).astype(BF)
        dq_t = (jnp.concatenate(dq_t, axis=0) + dot(gk_t, ds_rows)).astype(BF)

        prob = jnp.exp(dot(gq_b, key_t) * SCALE - g_top) * g_inv
        g_dprob = dot(gg_parts, value_t)
        g_dprob = g_dprob[:PAIRS] + g_dprob[PAIRS : 2 * PAIRS] + g_dprob[2 * PAIRS :]
        dscore = prob * (g_dprob - g_row) * SCALE
        none = jnp.zeros((PAIRS, TOKENS), BF)
        p_hi, p_mid, p_low3 = split3(prob)
        d_hi, d_mid, d_low3 = split3(dscore)
        d_parts = jnp.concatenate([d_hi, d_mid, d_low3, none], axis=0)
        p_parts = jnp.concatenate([p_hi, p_mid, p_low3, p_hi], axis=0)
        p_more = jnp.concatenate([p_mid, p_hi, none, none], axis=0)
        dk_t = (jnp.concatenate(dk_t, axis=0) + dot(gq_t3, d_parts)).astype(BF)
        dv_t = (
            jnp.concatenate(dv_t, axis=0) + (dot(gg_t6a, p_parts) + dot(gg_t6b, p_more))
        ).astype(BF)
        g_query = dot(d_parts[: 3 * PAIRS], key)
        g_att = dot(p_parts[: 3 * PAIRS], value)
        g_sum[0] += g_query[:PAIRS] + g_query[PAIRS : 2 * PAIRS] + g_query[2 * PAIRS :]
        g_sum[1] += dot(ds_rows, query)
        g_sum[2] += dot(p_rows, grad)
        g_sum[3] += g_att[:PAIRS] + g_att[PAIRS : 2 * PAIRS] + g_att[2 * PAIRS :]
        w_sum[0] += dot(dq_t, cells)
        w_sum[1] += dot(dk_t, cells)
        w_sum[2] += dot(dv_t, cells)
        w_sum[3] += dot(out_t, upstream)
        delta = dot(w_q, dq_t) + dot(w_k, dk_t) + dot(w_v, dv_t)
        delta_ref[u] = delta.T.astype(BF)
        return carry

    lax.fori_loop(0, CUBOIDS, one_cuboid, 0)

    def outer(a, b):
        a = jnp.concatenate([a, jnp.zeros((CH - GLOBALS, CH), F32)], axis=0).T
        b = jnp.concatenate([b, jnp.zeros((CH - GLOBALS, CH), F32)], axis=0)
        return jnp.dot(a, b, precision=HIGHEST, preferred_element_type=F32)

    vec = jnp.zeros((GLOBALS, CH), F32)
    for i in range(4):
        g_part = head_diagonal(g_sum[i])
        if i < 3:
            total = w_sum[i].T + outer(vectors, g_part)
            hi, mid, low = split3(g_part)
            weight = weights_ref[i]
            vec += dot_nt(hi, weight) + dot_nt(mid, weight) + dot_nt(low, weight)
        else:
            total = w_sum[3] + outer(g_part, vup_ref[...])
        hi, mid, low = split3(total)
        rows = pl.ds(i * CH, CH)
        part_ref[0, rows, :] = hi
        part_ref[1, rows, :] = mid
        part_ref[2, rows, :] = low
    vec_parts = jnp.concatenate(
        [x.astype(F32) for x in split3(vec)] + [jnp.zeros((CH - 3 * GLOBALS, CH), F32)], axis=0
    ).T.astype(BF)
    spread = (iota((TOKENS, CH), 0) // SPAN == iota((TOKENS, CH), 1)).astype(BF)
    part_ref[3] = dot(spread, vec_parts).astype(BF)

    back = back_matrix()
    for i in range(PEERS // GROUP):
        peers = pl.ds(i * GROUP, GROUP)
        tokens = pl.ds(i * group_tokens, group_tokens)
        rows = jnp.concatenate(
            [
                jnp.concatenate([delta_ref[u, tokens, :] for u in range(CUBOIDS)], axis=0),
                jnp.concatenate([part_ref[u, tokens, :] for u in range(CUBOIDS)], axis=0),
            ],
            axis=1,
        )
        moved = dot(back, rows).astype(BF)
        msg_ref[peers, 0:PEER_ROWS, :] = moved[:, :CH].reshape(GROUP, PEER_ROWS, CH)
        msg_ref[peers, PEER_ROWS:, :] = moved[:, CH:].reshape(GROUP, PEER_ROWS, CH)


def sum_kernel(recv_ref, piece_ref):
    summed = jnp.sum(recv_ref[:, PEER_ROWS:, :].astype(F32), axis=0)
    weight = summed[0:SPAN] + summed[SPAN : 2 * SPAN] + summed[2 * SPAN : 3 * SPAN]
    last = summed[3 * SPAN :]
    last = last + pltpu.roll(last, CH - GLOBALS, 1) + pltpu.roll(last, CH - 2 * GLOBALS, 1)
    piece = jnp.concatenate([weight, last], axis=0)
    piece_ref[...] = jnp.broadcast_to(piece[None], piece_ref.shape)


def place_kernel(shift_ref, recv_ref, out_ref, held):
    for i in range(PEERS // GROUP):
        held[pl.ds(i * GROUP_ROWS, GROUP_ROWS), :] = recv_ref[
            pl.ds(i * GROUP, GROUP), 0:PEER_ROWS, :
        ].reshape(GROUP_ROWS, CH)
    held[CELLS_DEV:, :] = held[:WINDOW, :]
    offset = (CELLS_DEV - tile_offset(shift_ref)) % CELLS_DEV
    mover = shift_matrix(offset % 16)
    base = offset - offset % 16
    for i in range(CELLS_DEV // GROUP_ROWS):
        start = pl.multiple_of((base + i * GROUP_ROWS) % CELLS_DEV, 16)
        moved = dot(mover, held[pl.ds(start, WINDOW), :]).astype(BF)
        out_ref[pl.ds(i * GROUP_ROWS, GROUP_ROWS), :] = moved


VMEM = pl.BlockSpec(memory_space=pltpu.VMEM)
SMEM = pl.BlockSpec(memory_space=pltpu.SMEM)
PARAMS = pltpu.CompilerParams(vmem_limit_bytes=48 * 1024 * 1024)


def exchange(rows):
    return lax.all_to_all(rows, ("tile", "frame"), split_axis=0, concat_axis=0, tiled=True)


def body(cells, vectors, weights, cuboid_shift, cell_upstream, vector_upstream):
    vectors = vectors.astype(F32)
    message = pl.pallas_call(
        pack_kernel,
        out_shape=jax.ShapeDtypeStruct((PEERS, MSG_ROWS, CH), BF),
        in_specs=[SMEM] + [VMEM] * 5,
        out_specs=VMEM,
        scratch_shapes=[pltpu.VMEM((CELLS_DEV + WINDOW, 2 * CH), BF)],
        compiler_params=PARAMS,
        name="pack",
    )(cuboid_shift, cells[0], cell_upstream[0], vectors, weights, vector_upstream)
    received = exchange(message)
    message = pl.pallas_call(
        owner_kernel,
        out_shape=jax.ShapeDtypeStruct((PEERS, 2 * PEER_ROWS, CH), BF),
        in_specs=[VMEM] * 4,
        out_specs=VMEM,
        scratch_shapes=[
            pltpu.VMEM((CUBOIDS, TOKENS, CH), BF),
            pltpu.VMEM((CUBOIDS, TOKENS, CH), BF),
            pltpu.VMEM((CUBOIDS, TOKENS, CH), BF),
            pltpu.VMEM((3, CH, CH), BF),
            pltpu.VMEM((HEADS, CH, TOKENS), BF),
            pltpu.VMEM((HEADS, CH, TOKENS), BF),
            pltpu.VMEM((4, CH, CH), F32),
            pltpu.VMEM((4, PAIRS, CH), F32),
            pltpu.VMEM((4, TOKENS, CH), BF),
        ],
        compiler_params=PARAMS,
        name="owner",
    )(received, vectors, weights, vector_upstream)
    received = exchange(message)
    pieces = pl.pallas_call(
        sum_kernel,
        out_shape=jax.ShapeDtypeStruct((PEERS, GLOBALS, CH), F32),
        in_specs=[VMEM],
        out_specs=VMEM,
        compiler_params=PARAMS,
        name="sum_pieces",
    )(received)
    pieces = exchange(pieces)
    cell_grad = pl.pallas_call(
        place_kernel,
        out_shape=jax.ShapeDtypeStruct((CELLS_DEV, CH), BF),
        in_specs=[SMEM, VMEM],
        out_specs=VMEM,
        scratch_shapes=[pltpu.VMEM((CELLS_DEV + WINDOW, CH), BF)],
        compiler_params=PARAMS,
        name="place",
    )(cuboid_shift, received)
    weight_grad = pieces[:, :SPAN, :].reshape(4, CH, CH)
    vector_grad = pieces[:, SPAN, :GLOBALS].T
    return cell_grad[None], weight_grad, vector_grad


def solution(mesh):
    in_specs = (P("frame", "tile", None), P(), P(), P(), P("frame", "tile", None), P())
    out_specs = (P("frame", "tile", None), P(), P())
    return jax.shard_map(body, mesh=mesh, in_specs=in_specs, out_specs=out_specs, check_vma=False)
```

```python
import math

import jax
import jax.numpy as jnp
from jax import lax
from jax.experimental import pallas as pl
from jax.experimental.pallas import tpu as pltpu
from jax.sharding import PartitionSpec as P

CH = 128
HEADS = 4
HDIM = 32
GLOBALS = 8
PAIRS = HEADS * GLOBALS
SPAN = 4
CELLS_DEV = 2048
PEERS = 128
PEER_ROWS = CELLS_DEV // PEERS
CUBOIDS = PEER_ROWS // SPAN
TOKENS = 512
GROUP = 16
GROUP_ROWS = GROUP * PEER_ROWS
WINDOW = GROUP_ROWS + 16
MSG_ROWS = 40
PIECE_ROWS = 2 * SPAN
PIECE_GROUP = 32
VEC_LANES = 2 * GLOBALS
SCALE = HDIM**-0.5
LOG2E = math.log2(math.e)
BF = jnp.bfloat16
F32 = jnp.float32
HIGHEST = lax.Precision.HIGHEST
NT = (((1,), (1,)), ((), ()))


def dot(a, b):
    return jnp.dot(a, b, preferred_element_type=F32)


def dot_nt(a, b):
    return lax.dot_general(a, b, NT, preferred_element_type=F32)


def iota(shape, axis):
    return lax.broadcasted_iota(jnp.int32, shape, axis)


def split3(x):
    hi = x.astype(BF)
    rest = x - hi.astype(F32)
    mid = rest.astype(BF)
    low = (rest - mid.astype(F32)).astype(BF)
    return hi, mid, low


def head_blocks(rows):
    head = iota((GLOBALS, CH), 1) // HDIM
    return jnp.concatenate([jnp.where(head == h, rows, 0.0) for h in range(HEADS)], axis=0)


def head_diagonal(blocks):
    head = iota((GLOBALS, CH), 1) // HDIM
    total = jnp.zeros((GLOBALS, CH), F32)
    for h in range(HEADS):
        total += jnp.where(head == h, blocks[h * GLOBALS : (h + 1) * GLOBALS], 0.0)
    return total


def global_rows(vectors, weight):
    return dot(vectors.astype(BF), weight).astype(BF).astype(F32)


def global_upstream(vector_upstream, w_out):
    hi, mid, low = split3(vector_upstream)
    return dot_nt(hi, w_out) + dot_nt(mid, w_out) + dot_nt(low, w_out)


def tile_offset(shift_ref):
    return (shift_ref[0] * (lax.axis_index("tile") + 1)) % CELLS_DEV


def shift_matrix(step):
    return (iota((GROUP_ROWS, WINDOW), 1) == iota((GROUP_ROWS, WINDOW), 0) + step).astype(BF)


def pack_kernel(
    shift_ref,
    cells_hbm,
    up_hbm,
    vectors_hbm,
    weights_hbm,
    vup_hbm,
    msg_ref,
    held,
    vectors_ref,
    weights_ref,
    vup_ref,
    sems,
):
    whole, wrap = pl.ds(0, CELLS_DEV), pl.ds(CELLS_DEV, WINDOW)
    left, right = pl.ds(0, CH), pl.ds(CH, CH)
    copies = [
        pltpu.make_async_copy(source, target, sems.at[i])
        for i, (source, target) in enumerate(
            [
                (vectors_hbm, vectors_ref),
                (weights_hbm, weights_ref),
                (vup_hbm, vup_ref),
                (cells_hbm, held.at[whole, left]),
                (cells_hbm.at[pl.ds(0, WINDOW)], held.at[wrap, left]),
                (up_hbm, held.at[whole, right]),
                (up_hbm.at[pl.ds(0, WINDOW)], held.at[wrap, right]),
            ]
        )
    ]
    for copy in copies:
        copy.start()
    for copy in copies:
        copy.wait()
    offset = tile_offset(shift_ref)
    mover = shift_matrix(offset % 16)
    base = offset - offset % 16
    for i in range(CELLS_DEV // GROUP_ROWS):
        start = pl.multiple_of((base + i * GROUP_ROWS) % CELLS_DEV, 16)
        moved = dot(mover, held[pl.ds(start, WINDOW), :]).astype(BF)
        peers = pl.ds(i * GROUP, GROUP)
        msg_ref[peers, 0:PEER_ROWS, :] = moved[:, :CH].reshape(GROUP, PEER_ROWS, CH)
        msg_ref[peers, PEER_ROWS : 2 * PEER_ROWS, :] = moved[:, CH:].reshape(GROUP, PEER_ROWS, CH)
    vectors = vectors_ref[...].astype(F32)
    cells = held[:CELLS_DEV, :CH]
    query = head_blocks(global_rows(vectors, weights_ref[0])).astype(BF)
    upstream = head_blocks(global_upstream(vup_ref[...], weights_ref[3]))
    up_parts = jnp.concatenate([part.astype(F32) for part in split3(upstream)], axis=0).astype(BF)
    keys = dot(cells, weights_ref[1]).astype(BF)
    values = dot(cells, weights_ref[2]).astype(BF)
    score = dot_nt(query, keys) * SCALE
    dprob = dot_nt(up_parts, values)
    dprob = dprob[:PAIRS] + dprob[PAIRS : 2 * PAIRS] + dprob[2 * PAIRS :]
    top = jnp.max(score, axis=1, keepdims=True)
    weight = jnp.exp(score - top)
    total = jnp.sum(weight, axis=1, keepdims=True)
    inner = jnp.sum(weight * dprob, axis=1, keepdims=True)
    lane = iota((PAIRS, CH), 1)
    stats = jnp.where(lane == 0, top, jnp.where(lane == 1, total, jnp.where(lane == 2, inner, 0.0)))
    parts = [part.astype(F32) for part in split3(stats)] + [jnp.zeros((PAIRS, CH), F32)]
    rows = jnp.concatenate(parts, axis=0).T[:GLOBALS].astype(BF)
    msg_ref[:, 2 * PEER_ROWS :, :] = jnp.broadcast_to(rows[None], (PEERS, GLOBALS, CH))


def regroup_matrix():
    row = iota((GROUP_ROWS, GROUP_ROWS), 0)
    column = iota((GROUP_ROWS, GROUP_ROWS), 1)
    source = (row // SPAN) % GROUP * PEER_ROWS + row // (GROUP * SPAN) * SPAN + row % SPAN
    return (column == source).astype(BF)


def piece_matrix():
    rows = PIECE_GROUP * PIECE_ROWS
    row = iota((rows, rows), 0)
    source = row // SPAN % 2 * CH + row // PIECE_ROWS * SPAN + row % SPAN
    return (iota((rows, rows), 1) == source).astype(BF)


def vec_slots(rows):
    row, lane = iota((rows, CH), 0), iota((rows, CH), 1)
    return row, (row % SPAN == SPAN - 1) & (lane < VEC_LANES)


def back_matrix():
    row = iota((GROUP_ROWS, GROUP_ROWS), 0)
    column = iota((GROUP_ROWS, GROUP_ROWS), 1)
    source = (row // SPAN) % CUBOIDS * (GROUP * SPAN) + row // PEER_ROWS * SPAN + row % SPAN
    return (column == source).astype(BF)


def owner_kernel(
    recv_ref,
    vectors_ref,
    weights_ref,
    vup_ref,
    msg_ref,
    cells_ref,
    up_ref,
    delta_ref,
    weights_t_ref,
    query_m,
    grad_m,
    w_sum,
    g_sum,
    part_ref,
    low_ref,
):
    group_tokens = GROUP * SPAN
    mover = regroup_matrix()
    for i in range(PEERS // GROUP):
        peers = pl.ds(i * GROUP, GROUP)
        rows = jnp.concatenate(
            [
                recv_ref[peers, 0:PEER_ROWS, :].reshape(GROUP_ROWS, CH),
                recv_ref[peers, PEER_ROWS : 2 * PEER_ROWS, :].reshape(GROUP_ROWS, CH),
            ],
            axis=1,
        )
        moved = dot(mover, rows).astype(BF)
        for u in range(CUBOIDS):
            piece = moved[u * group_tokens : (u + 1) * group_tokens]
            cells_ref[u, pl.ds(i * group_tokens, group_tokens), :] = piece[:, :CH]
            up_ref[u, pl.ds(i * group_tokens, group_tokens), :] = piece[:, CH:]

    stats = recv_ref[:, 2 * PEER_ROWS :, :].astype(F32).reshape(PEERS * GLOBALS, CH)
    stats = stats + pltpu.roll(stats, CH - PAIRS, 1) + pltpu.roll(stats, CH - 2 * PAIRS, 1)
    stats = stats.reshape(PEERS, GLOBALS, CH)
    tops = stats[:, 0:1, :]
    top = jnp.max(tops, axis=0)
    summed = jnp.sum(jnp.exp(tops - top[None]) * stats, axis=0)
    row = iota((GLOBALS, CH), 0)
    lanes = jnp.where(row == 0, top, summed)
    columns = jnp.concatenate([lanes, jnp.zeros((CH - GLOBALS, CH), F32)], axis=0).T
    g_top = columns[:PAIRS, 0:1]
    g_inv = 1.0 / columns[:PAIRS, 1:2]
    g_row = columns[:PAIRS, 2:3] * g_inv

    vectors = vectors_ref[...].astype(F32)
    w_q, w_k, w_v, w_o = (weights_ref[i] for i in range(4))
    for i in range(3):
        weights_t_ref[i] = weights_ref[i].astype(F32).T.astype(BF)
    gq = head_blocks(global_rows(vectors, w_q))
    gk = head_blocks(global_rows(vectors, w_k))
    gv = head_blocks(global_rows(vectors, w_v))
    gg = head_blocks(global_upstream(vup_ref[...], w_o))

    def wide_t(blocks):
        return jnp.concatenate([blocks, jnp.zeros((CH - PAIRS, CH), F32)], axis=0).T

    gq_b, gk_b, gv_b = (x.astype(BF) for x in (gq, gk, gv))
    gk_t = wide_t(gk)[:, :PAIRS].astype(BF)
    gv_t = wide_t(gv)[:, :PAIRS].astype(BF)
    gg3 = [part.astype(F32) for part in split3(gg)]
    gg_parts = jnp.concatenate(gg3, axis=0).astype(BF)
    zero = jnp.zeros((PAIRS, CH), F32)
    gq_t3 = jnp.concatenate([gq, gq, gq, zero], axis=0).T.astype(BF)
    gg_t6a = jnp.concatenate([gg3[0], gg3[0], gg3[0], gg3[1]], axis=0).T.astype(BF)
    gg_t6b = jnp.concatenate([gg3[1], gg3[2], zero, zero], axis=0).T.astype(BF)

    query_m[...] = jnp.zeros_like(query_m)
    grad_m[...] = jnp.zeros_like(grad_m)
    w_sum[...] = jnp.zeros_like(w_sum)
    g_sum[...] = jnp.zeros_like(g_sum)

    def one_cuboid(u, carry):
        cells = cells_ref[u]
        upstream = up_ref[u]
        query_t = dot_nt(weights_t_ref[0], cells).astype(BF)
        key_t = dot_nt(weights_t_ref[1], cells).astype(BF)
        value_t = dot_nt(weights_t_ref[2], cells).astype(BF)
        grad_t = dot_nt(w_o, upstream).astype(BF)
        query = dot(cells, w_q).astype(BF)
        key = dot(cells, w_k).astype(BF)
        value = dot(cells, w_v).astype(BF)
        grad = dot_nt(upstream, w_o).astype(BF)
        for h in range(HEADS):
            part = slice(h * HDIM, (h + 1) * HDIM)
            query_m[h, part, :] = query_t[part]
            grad_m[h, part, :] = grad_t[part]
        s_global = dot(gk_b, query_t)
        d_global = dot(gv_b, grad_t)
        p_rows, ds_rows, out_t, dq_t, dk_t, dv_t = [], [], [], [], [], []
        for h in range(HEADS):
            part = slice(h * HDIM, (h + 1) * HDIM)
            pair = slice(h * GLOBALS, (h + 1) * GLOBALS)
            score = dot(key, query_m[h])
            dprob = dot(value, grad_m[h])
            top = jnp.maximum(
                jnp.max(score, axis=0, keepdims=True),
                jnp.max(s_global[pair], axis=0, keepdims=True),
            )
            e_local = jnp.exp2((score - top) * (SCALE * LOG2E))
            e_global = jnp.exp2((s_global[pair] - top) * (SCALE * LOG2E))
            total = jnp.sum(e_local, axis=0, keepdims=True) + jnp.sum(
                e_global, axis=0, keepdims=True
            )
            inv = 1.0 / total
            p_local = e_local * inv
            p_global = e_global * inv
            inner = jnp.sum(p_local * dprob, axis=0, keepdims=True) + jnp.sum(
                p_global * d_global[pair], axis=0, keepdims=True
            )
            p_low = p_local.astype(BF)
            ds_low = (p_local * (dprob - inner) * SCALE).astype(BF)
            p_rows.append(p_global)
            ds_rows.append(p_global * (d_global[pair] - inner) * SCALE)
            out_t.append(dot(value_t[part], p_low))
            dq_t.append(dot(key_t[part], ds_low))
            dv_t.append(dot_nt(grad_t[part], p_low))
            dk_t.append(dot_nt(query_t[part], ds_low))
        p_rows = jnp.concatenate(p_rows, axis=0).astype(BF)
        ds_rows = jnp.concatenate(ds_rows, axis=0).astype(BF)
        out_t = (jnp.concatenate(out_t, axis=0) + dot(gv_t, p_rows)).astype(BF)
        dq_t = (jnp.concatenate(dq_t, axis=0) + dot(gk_t, ds_rows)).astype(BF)

        prob = jnp.exp(dot(gq_b, key_t) * SCALE - g_top) * g_inv
        g_dprob = dot(gg_parts, value_t)
        g_dprob = g_dprob[:PAIRS] + g_dprob[PAIRS : 2 * PAIRS] + g_dprob[2 * PAIRS :]
        dscore = prob * (g_dprob - g_row) * SCALE
        none = jnp.zeros((PAIRS, TOKENS), BF)
        p_hi, p_mid, p_low3 = split3(prob)
        d_hi, d_mid, d_low3 = split3(dscore)
        d_parts = jnp.concatenate([d_hi, d_mid, d_low3, none], axis=0)
        p_parts = jnp.concatenate([p_hi, p_mid, p_low3, p_hi], axis=0)
        p_more = jnp.concatenate([p_mid, p_hi, none, none], axis=0)
        dk_t = (jnp.concatenate(dk_t, axis=0) + dot(gq_t3, d_parts)).astype(BF)
        dv_t = (
            jnp.concatenate(dv_t, axis=0) + (dot(gg_t6a, p_parts) + dot(gg_t6b, p_more))
        ).astype(BF)
        g_query = dot(d_parts[: 3 * PAIRS], key)
        g_att = dot(p_parts[: 3 * PAIRS], value)
        g_sum[0] += g_query[:PAIRS] + g_query[PAIRS : 2 * PAIRS] + g_query[2 * PAIRS :]
        g_sum[1] += dot(ds_rows, query)
        g_sum[2] += dot(p_rows, grad)
        g_sum[3] += g_att[:PAIRS] + g_att[PAIRS : 2 * PAIRS] + g_att[2 * PAIRS :]
        w_sum[0] += dot(dq_t, cells)
        w_sum[1] += dot(dk_t, cells)
        w_sum[2] += dot(dv_t, cells)
        w_sum[3] += dot(out_t, upstream)
        delta = dot(w_q, dq_t) + dot(w_k, dk_t) + dot(w_v, dv_t)
        delta_ref[u] = delta.T.astype(BF)
        return carry

    lax.fori_loop(0, CUBOIDS, one_cuboid, 0)

    def outer(a, b):
        a = jnp.concatenate([a, jnp.zeros((CH - GLOBALS, CH), F32)], axis=0).T
        b = jnp.concatenate([b, jnp.zeros((CH - GLOBALS, CH), F32)], axis=0)
        return jnp.dot(a, b, precision=HIGHEST, preferred_element_type=F32)

    vec = jnp.zeros((GLOBALS, CH), F32)
    for i in range(4):
        g_part = head_diagonal(g_sum[i])
        if i < 3:
            total = w_sum[i].T + outer(vectors, g_part)
            hi, mid, low = split3(g_part)
            weight = weights_ref[i]
            vec += dot_nt(hi, weight) + dot_nt(mid, weight) + dot_nt(low, weight)
        else:
            total = w_sum[3] + outer(g_part, vup_ref[...])
        high = total.astype(BF)
        rows = pl.ds(i * CH, CH)
        part_ref[0, rows, :] = high
        low_ref[rows, :] = total - high.astype(F32)
    hi, mid, _ = split3(vec)
    vec_parts = jnp.concatenate(
        [hi.astype(F32), mid.astype(F32), jnp.zeros((CH - VEC_LANES, CH), F32)], axis=0
    ).T.astype(BF)
    row, slots = vec_slots(TOKENS)
    spread = (iota((TOKENS, CH), 0) // SPAN == iota((TOKENS, CH), 1)).astype(BF)
    part_ref[1] = jnp.where(slots, dot(spread, vec_parts), low_ref[...]).astype(BF)

    back = back_matrix()
    for i in range(PEERS // GROUP):
        tokens = pl.ds(i * group_tokens, group_tokens)
        rows = jnp.concatenate([delta_ref[u, tokens, :] for u in range(CUBOIDS)], axis=0)
        moved = dot(back, rows).astype(BF)
        msg_ref[pl.ds(i * GROUP, GROUP), 0:PEER_ROWS, :] = moved.reshape(GROUP, PEER_ROWS, CH)
    back = piece_matrix()
    for i in range(PEERS // PIECE_GROUP):
        tokens = pl.ds(i * CH, CH)
        rows = jnp.concatenate([part_ref[0, tokens, :], part_ref[1, tokens, :]], axis=0)
        moved = dot(back, rows).astype(BF)
        msg_ref[pl.ds(i * PIECE_GROUP, PIECE_GROUP), PEER_ROWS:, :] = moved.reshape(
            PIECE_GROUP, PIECE_ROWS, CH
        )


def sum_kernel(recv_ref, piece_ref):
    summed = jnp.sum(recv_ref[:, PEER_ROWS:, :].astype(F32), axis=0)
    row, slots = vec_slots(PIECE_ROWS)
    slots = slots & (row >= SPAN)
    vec = summed + pltpu.roll(summed, CH - GLOBALS, 1)
    low = jnp.where(slots, 0.0, summed)
    weight = summed[:SPAN] + low[SPAN:]
    high = weight.astype(BF).astype(F32)
    vec_high = vec.astype(BF).astype(F32)
    vec_low = pltpu.roll(vec - vec_high, GLOBALS, 1)
    vec = jnp.where(iota((PIECE_ROWS, CH), 1) < GLOBALS, vec_high, vec_low)
    piece = jnp.where(slots, vec, jnp.concatenate([high, weight - high], axis=0)).astype(BF)
    piece_ref[...] = jnp.broadcast_to(piece[None], piece_ref.shape)


def spread_kernel(recv_ref, weight_ref, vec_ref):
    rows = PIECE_GROUP * PIECE_ROWS
    row, slots = vec_slots(rows)
    slots = slots & (row % PIECE_ROWS >= SPAN)
    target, source = iota((CH, rows), 0), iota((CH, rows), 1)
    joins = (source // PIECE_ROWS == target // SPAN) & (source % SPAN == target % SPAN)
    joins = joins.astype(BF)
    target, source = iota((PIECE_GROUP, rows), 0), iota((PIECE_GROUP, rows), 1)
    last = (source == target * PIECE_ROWS + PIECE_ROWS - 1).astype(BF)
    vec = []
    for i in range(PEERS // PIECE_GROUP):
        piece = recv_ref[pl.ds(i * PIECE_GROUP, PIECE_GROUP)].reshape(rows, CH)
        vec.append(dot(last, piece))
        piece = jnp.where(slots, 0.0, piece.astype(F32)).astype(BF)
        weight_ref[i] = dot(joins, piece)
    vec = jnp.concatenate(vec, axis=0).T
    vec_ref[...] = vec[:GLOBALS] + vec[GLOBALS : 2 * GLOBALS]


def place_kernel(shift_ref, recv_ref, out_ref, held):
    for i in range(PEERS // GROUP):
        held[pl.ds(i * GROUP_ROWS, GROUP_ROWS), :] = recv_ref[
            pl.ds(i * GROUP, GROUP), 0:PEER_ROWS, :
        ].reshape(GROUP_ROWS, CH)
    held[CELLS_DEV:, :] = held[:WINDOW, :]
    offset = (CELLS_DEV - tile_offset(shift_ref)) % CELLS_DEV
    mover = shift_matrix(offset % 16)
    base = offset - offset % 16
    for i in range(CELLS_DEV // GROUP_ROWS):
        start = pl.multiple_of((base + i * GROUP_ROWS) % CELLS_DEV, 16)
        moved = dot(mover, held[pl.ds(start, WINDOW), :]).astype(BF)
        out_ref[pl.ds(i * GROUP_ROWS, GROUP_ROWS), :] = moved


VMEM = pl.BlockSpec(memory_space=pltpu.VMEM)
SMEM = pl.BlockSpec(memory_space=pltpu.SMEM)
HBM = pl.BlockSpec(memory_space=pltpu.HBM)
PARAMS = pltpu.CompilerParams(vmem_limit_bytes=48 * 1024 * 1024)


def exchange(rows):
    return lax.all_to_all(rows, ("tile", "frame"), split_axis=0, concat_axis=0, tiled=True)


def body(cells, vectors, weights, cuboid_shift, cell_upstream, vector_upstream):
    message = pl.pallas_call(
        pack_kernel,
        out_shape=jax.ShapeDtypeStruct((PEERS, MSG_ROWS, CH), BF),
        in_specs=[SMEM] + [HBM] * 5,
        out_specs=VMEM,
        scratch_shapes=[
            pltpu.VMEM((CELLS_DEV + WINDOW, 2 * CH), BF),
            pltpu.VMEM((GLOBALS, CH), BF),
            pltpu.VMEM((4, CH, CH), BF),
            pltpu.VMEM((GLOBALS, CH), F32),
            pltpu.SemaphoreType.DMA((7,)),
        ],
        compiler_params=PARAMS,
        name="pack",
    )(cuboid_shift, cells[0], cell_upstream[0], vectors, weights, vector_upstream)
    received = exchange(message)
    message = pl.pallas_call(
        owner_kernel,
        out_shape=jax.ShapeDtypeStruct((PEERS, PEER_ROWS + PIECE_ROWS, CH), BF),
        in_specs=[VMEM] * 4,
        out_specs=VMEM,
        scratch_shapes=[
            pltpu.VMEM((CUBOIDS, TOKENS, CH), BF),
            pltpu.VMEM((CUBOIDS, TOKENS, CH), BF),
            pltpu.VMEM((CUBOIDS, TOKENS, CH), BF),
            pltpu.VMEM((3, CH, CH), BF),
            pltpu.VMEM((HEADS, CH, TOKENS), BF),
            pltpu.VMEM((HEADS, CH, TOKENS), BF),
            pltpu.VMEM((4, CH, CH), F32),
            pltpu.VMEM((4, PAIRS, CH), F32),
            pltpu.VMEM((2, TOKENS, CH), BF),
            pltpu.VMEM((TOKENS, CH), F32),
        ],
        compiler_params=PARAMS,
        name="owner",
    )(received, vectors, weights, vector_upstream)
    received = exchange(message)
    pieces = pl.pallas_call(
        sum_kernel,
        out_shape=jax.ShapeDtypeStruct((PEERS, PIECE_ROWS, CH), BF),
        in_specs=[VMEM],
        out_specs=VMEM,
        compiler_params=PARAMS,
        name="sum_pieces",
    )(received)
    pieces = exchange(pieces)
    cell_grad = pl.pallas_call(
        place_kernel,
        out_shape=jax.ShapeDtypeStruct((CELLS_DEV, CH), BF),
        in_specs=[SMEM, VMEM],
        out_specs=VMEM,
        scratch_shapes=[pltpu.VMEM((CELLS_DEV + WINDOW, CH), BF)],
        compiler_params=PARAMS,
        name="place",
    )(cuboid_shift, received)
    weight_grad, vector_grad = pl.pallas_call(
        spread_kernel,
        out_shape=[
            jax.ShapeDtypeStruct((4, CH, CH), F32),
            jax.ShapeDtypeStruct((GLOBALS, CH), F32),
        ],
        in_specs=[VMEM],
        out_specs=[VMEM, VMEM],
        compiler_params=PARAMS,
        name="spread",
    )(pieces)
    return cell_grad[None], weight_grad, vector_grad


def solution(mesh):
    in_specs = (P("frame", "tile", None), P(), P(), P(), P("frame", "tile", None), P())
    out_specs = (P("frame", "tile", None), P(), P())
    return jax.shard_map(body, mesh=mesh, in_specs=in_specs, out_specs=out_specs, check_vma=False)
```

```python
import math

import jax
import jax.numpy as jnp
from jax import lax
from jax.experimental import pallas as pl
from jax.experimental.pallas import tpu as pltpu
from jax.sharding import PartitionSpec as P

CH = 128
HEADS = 4
HDIM = 32
GLOBALS = 8
PAIRS = HEADS * GLOBALS
SPAN = 4
CELLS_DEV = 2048
PEERS = 128
PEER_ROWS = CELLS_DEV // PEERS
CUBOIDS = PEER_ROWS // SPAN
TOKENS = 512
QUERIES = 256
UNROLL = 1
GROUP = 16
GROUP_ROWS = GROUP * PEER_ROWS
WINDOW = GROUP_ROWS + 16
MSG_ROWS = 40
PIECE_ROWS = 2 * SPAN
PIECE_GROUP = 32
VEC_LANES = 2 * GLOBALS
SCALE = HDIM**-0.5
LOG2E = math.log2(math.e)
BF = jnp.bfloat16
F32 = jnp.float32
HIGHEST = lax.Precision.HIGHEST
NT = (((1,), (1,)), ((), ()))


def dot(a, b):
    return jnp.dot(a, b, preferred_element_type=F32)


def dot_nt(a, b):
    return lax.dot_general(a, b, NT, preferred_element_type=F32)


def iota(shape, axis):
    return lax.broadcasted_iota(jnp.int32, shape, axis)


def split3(x):
    hi = x.astype(BF)
    rest = x - hi.astype(F32)
    mid = rest.astype(BF)
    low = (rest - mid.astype(F32)).astype(BF)
    return hi, mid, low


def head_blocks(rows):
    head = iota((GLOBALS, CH), 1) // HDIM
    return jnp.concatenate([jnp.where(head == h, rows, 0.0) for h in range(HEADS)], axis=0)


def head_diagonal(blocks):
    head = iota((GLOBALS, CH), 1) // HDIM
    total = jnp.zeros((GLOBALS, CH), F32)
    for h in range(HEADS):
        total += jnp.where(head == h, blocks[h * GLOBALS : (h + 1) * GLOBALS], 0.0)
    return total


def global_rows(vectors, weight):
    return dot(vectors.astype(BF), weight).astype(BF).astype(F32)


def global_upstream(vector_upstream, w_out):
    hi, mid, low = split3(vector_upstream)
    return dot_nt(hi, w_out) + dot_nt(mid, w_out) + dot_nt(low, w_out)


def tile_offset(shift_ref):
    return (shift_ref[0] * (lax.axis_index("tile") + 1)) % CELLS_DEV


def shift_matrix(step):
    return (iota((GROUP_ROWS, WINDOW), 1) == iota((GROUP_ROWS, WINDOW), 0) + step).astype(BF)


def pack_kernel(
    shift_ref,
    cells_hbm,
    up_hbm,
    vectors_hbm,
    weights_hbm,
    vup_hbm,
    msg_ref,
    held,
    vectors_ref,
    weights_ref,
    vup_ref,
    sems,
):
    whole, wrap = pl.ds(0, CELLS_DEV), pl.ds(CELLS_DEV, WINDOW)
    left, right = pl.ds(0, CH), pl.ds(CH, CH)
    copies = [
        pltpu.make_async_copy(source, target, sems.at[i])
        for i, (source, target) in enumerate(
            [
                (vectors_hbm, vectors_ref),
                (weights_hbm, weights_ref),
                (vup_hbm, vup_ref),
                (cells_hbm, held.at[whole, left]),
                (cells_hbm.at[pl.ds(0, WINDOW)], held.at[wrap, left]),
                (up_hbm, held.at[whole, right]),
                (up_hbm.at[pl.ds(0, WINDOW)], held.at[wrap, right]),
            ]
        )
    ]
    for copy in copies:
        copy.start()
    for copy in copies:
        copy.wait()
    offset = tile_offset(shift_ref)
    mover = shift_matrix(offset % 16)
    base = offset - offset % 16
    for i in range(CELLS_DEV // GROUP_ROWS):
        start = pl.multiple_of((base + i * GROUP_ROWS) % CELLS_DEV, 16)
        moved = dot(mover, held[pl.ds(start, WINDOW), :]).astype(BF)
        peers = pl.ds(i * GROUP, GROUP)
        msg_ref[peers, 0:PEER_ROWS, :] = moved[:, :CH].reshape(GROUP, PEER_ROWS, CH)
        msg_ref[peers, PEER_ROWS : 2 * PEER_ROWS, :] = moved[:, CH:].reshape(GROUP, PEER_ROWS, CH)
    vectors = vectors_ref[...].astype(F32)
    cells = held[:CELLS_DEV, :CH]
    query = head_blocks(global_rows(vectors, weights_ref[0])).astype(BF)
    upstream = head_blocks(global_upstream(vup_ref[...], weights_ref[3]))
    up_parts = jnp.concatenate([part.astype(F32) for part in split3(upstream)], axis=0).astype(BF)
    keys = dot(cells, weights_ref[1]).astype(BF)
    values = dot(cells, weights_ref[2]).astype(BF)
    score = dot_nt(query, keys) * SCALE
    dprob = dot_nt(up_parts, values)
    dprob = dprob[:PAIRS] + dprob[PAIRS : 2 * PAIRS] + dprob[2 * PAIRS :]
    top = jnp.max(score, axis=1, keepdims=True)
    weight = jnp.exp(score - top)
    total = jnp.sum(weight, axis=1, keepdims=True)
    inner = jnp.sum(weight * dprob, axis=1, keepdims=True)
    lane = iota((PAIRS, CH), 1)
    stats = jnp.where(lane == 0, top, jnp.where(lane == 1, total, jnp.where(lane == 2, inner, 0.0)))
    parts = [part.astype(F32) for part in split3(stats)] + [jnp.zeros((PAIRS, CH), F32)]
    rows = jnp.concatenate(parts, axis=0).T[:GLOBALS].astype(BF)
    msg_ref[:, 2 * PEER_ROWS :, :] = jnp.broadcast_to(rows[None], (PEERS, GLOBALS, CH))


def regroup_matrix():
    row = iota((GROUP_ROWS, GROUP_ROWS), 0)
    column = iota((GROUP_ROWS, GROUP_ROWS), 1)
    source = (row // SPAN) % GROUP * PEER_ROWS + row // (GROUP * SPAN) * SPAN + row % SPAN
    return (column == source).astype(BF)


def piece_matrix():
    rows = PIECE_GROUP * PIECE_ROWS
    row = iota((rows, rows), 0)
    source = row // SPAN % 2 * CH + row // PIECE_ROWS * SPAN + row % SPAN
    return (iota((rows, rows), 1) == source).astype(BF)


def vec_slots(rows):
    row, lane = iota((rows, CH), 0), iota((rows, CH), 1)
    return row, (row % SPAN == SPAN - 1) & (lane < VEC_LANES)


def back_matrix():
    row = iota((GROUP_ROWS, GROUP_ROWS), 0)
    column = iota((GROUP_ROWS, GROUP_ROWS), 1)
    source = (row // SPAN) % CUBOIDS * (GROUP * SPAN) + row // PEER_ROWS * SPAN + row % SPAN
    return (column == source).astype(BF)


def owner_kernel(
    recv_ref,
    vectors_ref,
    weights_ref,
    vup_ref,
    msg_ref,
    cells_ref,
    up_ref,
    delta_ref,
    weights_t_ref,
    query_m,
    grad_m,
    w_sum,
    g_sum,
    part_ref,
    low_ref,
    dk_ref,
    dv_ref,
):
    group_tokens = GROUP * SPAN
    mover = regroup_matrix()
    for i in range(PEERS // GROUP):
        peers = pl.ds(i * GROUP, GROUP)
        rows = jnp.concatenate(
            [
                recv_ref[peers, 0:PEER_ROWS, :].reshape(GROUP_ROWS, CH),
                recv_ref[peers, PEER_ROWS : 2 * PEER_ROWS, :].reshape(GROUP_ROWS, CH),
            ],
            axis=1,
        )
        moved = dot(mover, rows).astype(BF)
        for u in range(CUBOIDS):
            piece = moved[u * group_tokens : (u + 1) * group_tokens]
            cells_ref[u, pl.ds(i * group_tokens, group_tokens), :] = piece[:, :CH]
            up_ref[u, pl.ds(i * group_tokens, group_tokens), :] = piece[:, CH:]

    stats = recv_ref[:, 2 * PEER_ROWS :, :].astype(F32).reshape(PEERS * GLOBALS, CH)
    stats = stats + pltpu.roll(stats, CH - PAIRS, 1) + pltpu.roll(stats, CH - 2 * PAIRS, 1)
    stats = stats.reshape(PEERS, GLOBALS, CH)
    tops = stats[:, 0:1, :]
    top = jnp.max(tops, axis=0)
    summed = jnp.sum(jnp.exp(tops - top[None]) * stats, axis=0)
    row = iota((GLOBALS, CH), 0)
    lanes = jnp.where(row == 0, top, summed)
    columns = jnp.concatenate([lanes, jnp.zeros((CH - GLOBALS, CH), F32)], axis=0).T
    g_top = columns[:PAIRS, 0:1]
    g_inv = 1.0 / columns[:PAIRS, 1:2]
    g_row = columns[:PAIRS, 2:3] * g_inv

    vectors = vectors_ref[...].astype(F32)
    w_q, w_k, w_v, w_o = (weights_ref[i] for i in range(4))
    for i in range(3):
        weights_t_ref[i] = weights_ref[i].astype(F32).T.astype(BF)
    gq = head_blocks(global_rows(vectors, w_q))
    gk = head_blocks(global_rows(vectors, w_k))
    gv = head_blocks(global_rows(vectors, w_v))
    gg = head_blocks(global_upstream(vup_ref[...], w_o))

    def wide_t(blocks):
        return jnp.concatenate([blocks, jnp.zeros((CH - PAIRS, CH), F32)], axis=0).T

    gq_b, gk_b, gv_b = (x.astype(BF) for x in (gq, gk, gv))
    gk_t = wide_t(gk)[:, :PAIRS].astype(BF)
    gv_t = wide_t(gv)[:, :PAIRS].astype(BF)
    gg3 = [part.astype(F32) for part in split3(gg)]
    gg_parts = jnp.concatenate(gg3, axis=0).astype(BF)
    zero = jnp.zeros((PAIRS, CH), F32)
    gq_t3 = jnp.concatenate([gq, gq, gq, zero], axis=0).T.astype(BF)
    gg_t6a = jnp.concatenate([gg3[0], gg3[0], gg3[0], gg3[1]], axis=0).T.astype(BF)
    gg_t6b = jnp.concatenate([gg3[1], gg3[2], zero, zero], axis=0).T.astype(BF)

    query_m[...] = jnp.zeros_like(query_m)
    grad_m[...] = jnp.zeros_like(grad_m)
    w_sum[...] = jnp.zeros_like(w_sum)
    g_sum[...] = jnp.zeros_like(g_sum)

    def one_cuboid(u, carry):
        cells = cells_ref[u]
        upstream = up_ref[u]
        query_t = dot_nt(weights_t_ref[0], cells).astype(BF)
        key_t = dot_nt(weights_t_ref[1], cells).astype(BF)
        value_t = dot_nt(weights_t_ref[2], cells).astype(BF)
        grad_t = dot_nt(w_o, upstream).astype(BF)
        query = dot(cells, w_q).astype(BF)
        key = dot(cells, w_k).astype(BF)
        value = dot(cells, w_v).astype(BF)
        grad = dot_nt(upstream, w_o).astype(BF)
        for h in range(HEADS):
            part = slice(h * HDIM, (h + 1) * HDIM)
            query_m[h, part, :] = query_t[part]
            grad_m[h, part, :] = grad_t[part]
        s_global = dot(gk_b, query_t)
        d_global = dot(gv_b, grad_t)
        steps = [(h, q) for h in range(HEADS) for q in range(0, TOKENS, QUERIES)]

        def scores(step):
            h, q = step
            columns = pl.ds(q, QUERIES)
            return dot(key, query_m[h, :, columns]), dot(value, grad_m[h, :, columns])

        def softmax(step, score, dprob):
            h, q = step
            rows = slice(h * GLOBALS, (h + 1) * GLOBALS)
            s_glob = s_global[rows, q : q + QUERIES]
            d_glob = d_global[rows, q : q + QUERIES]
            top = jnp.maximum(
                jnp.max(score, axis=0, keepdims=True), jnp.max(s_glob, axis=0, keepdims=True)
            )
            e_local = jnp.exp2((score - top) * (SCALE * LOG2E))
            e_global = jnp.exp2((s_glob - top) * (SCALE * LOG2E))
            total = jnp.sum(e_local, axis=0, keepdims=True) + jnp.sum(
                e_global, axis=0, keepdims=True
            )
            inv = 1.0 / total
            p_local = e_local * inv
            p_global = e_global * inv
            inner = jnp.sum(p_local * dprob, axis=0, keepdims=True) + jnp.sum(
                p_global * d_glob, axis=0, keepdims=True
            )
            p_row[h].append(p_global)
            ds_row[h].append(p_global * (d_glob - inner) * SCALE)
            return p_local.astype(BF), (p_local * (dprob - inner) * SCALE).astype(BF)

        def products(step, p_low, ds_low):
            h, q = step
            part = slice(h * HDIM, (h + 1) * HDIM)
            out_row[h].append(dot(value_t[part], p_low))
            dq_row[h].append(dot(key_t[part], ds_low))
            d_value = dot(p_low, grad[q : q + QUERIES])
            d_key = dot(ds_low, query[q : q + QUERIES])
            if q == 0:
                dv_ref[:, part] = d_value[:, part]
                dk_ref[:, part] = d_key[:, part]
            else:
                dv_ref[:, part] += d_value[:, part]
                dk_ref[:, part] += d_key[:, part]

        p_row, ds_row, out_row, dq_row = ([[] for _ in range(HEADS)] for _ in range(4))
        ready = scores(steps[0])
        low = None
        for i, step in enumerate(steps):
            following = scores(steps[i + 1]) if i + 1 < len(steps) else None
            if low is not None:
                products(steps[i - 1], *low)
            low = softmax(step, *ready)
            ready = following
        products(steps[-1], *low)

        def whole(pieces):
            return jnp.concatenate([jnp.concatenate(row, axis=1) for row in pieces], axis=0)

        p_rows, ds_rows, out_t, dq_t = (whole(x) for x in (p_row, ds_row, out_row, dq_row))
        p_rows, ds_rows = p_rows.astype(BF), ds_rows.astype(BF)
        out_t = (out_t + dot(gv_t, p_rows)).astype(BF)
        dq_t = (dq_t + dot(gk_t, ds_rows)).astype(BF)

        prob = jnp.exp(dot(gq_b, key_t) * SCALE - g_top) * g_inv
        g_dprob = dot(gg_parts, value_t)
        g_dprob = g_dprob[:PAIRS] + g_dprob[PAIRS : 2 * PAIRS] + g_dprob[2 * PAIRS :]
        dscore = prob * (g_dprob - g_row) * SCALE
        none = jnp.zeros((PAIRS, TOKENS), BF)
        p_hi, p_mid, p_low3 = split3(prob)
        d_hi, d_mid, d_low3 = split3(dscore)
        d_parts = jnp.concatenate([d_hi, d_mid, d_low3, none], axis=0)
        p_parts = jnp.concatenate([p_hi, p_mid, p_low3, p_hi], axis=0)
        p_more = jnp.concatenate([p_mid, p_hi, none, none], axis=0)
        dk_t = (dk_ref[...].T + dot(gq_t3, d_parts)).astype(BF)
        dv_t = (dv_ref[...].T + (dot(gg_t6a, p_parts) + dot(gg_t6b, p_more))).astype(BF)
        g_query = dot(d_parts[: 3 * PAIRS], key)
        g_att = dot(p_parts[: 3 * PAIRS], value)
        g_sum[0] += g_query[:PAIRS] + g_query[PAIRS : 2 * PAIRS] + g_query[2 * PAIRS :]
        g_sum[1] += dot(ds_rows, query)
        g_sum[2] += dot(p_rows, grad)
        g_sum[3] += g_att[:PAIRS] + g_att[PAIRS : 2 * PAIRS] + g_att[2 * PAIRS :]
        w_sum[0] += dot(dq_t, cells)
        w_sum[1] += dot(dk_t, cells)
        w_sum[2] += dot(dv_t, cells)
        w_sum[3] += dot(out_t, upstream)
        delta = dot(w_q, dq_t) + dot(w_k, dk_t) + dot(w_v, dv_t)
        delta_ref[u] = delta.T.astype(BF)
        return carry

    lax.fori_loop(0, CUBOIDS, one_cuboid, 0, unroll=UNROLL)

    def outer(a, b):
        a = jnp.concatenate([a, jnp.zeros((CH - GLOBALS, CH), F32)], axis=0).T
        b = jnp.concatenate([b, jnp.zeros((CH - GLOBALS, CH), F32)], axis=0)
        return jnp.dot(a, b, precision=HIGHEST, preferred_element_type=F32)

    vec = jnp.zeros((GLOBALS, CH), F32)
    for i in range(4):
        g_part = head_diagonal(g_sum[i])
        if i < 3:
            total = w_sum[i].T + outer(vectors, g_part)
            hi, mid, low = split3(g_part)
            weight = weights_ref[i]
            vec += dot_nt(hi, weight) + dot_nt(mid, weight) + dot_nt(low, weight)
        else:
            total = w_sum[3] + outer(g_part, vup_ref[...])
        high = total.astype(BF)
        rows = pl.ds(i * CH, CH)
        part_ref[0, rows, :] = high
        low_ref[rows, :] = total - high.astype(F32)
    hi, mid, _ = split3(vec)
    vec_parts = jnp.concatenate(
        [hi.astype(F32), mid.astype(F32), jnp.zeros((CH - VEC_LANES, CH), F32)], axis=0
    ).T.astype(BF)
    row, slots = vec_slots(TOKENS)
    spread = (iota((TOKENS, CH), 0) // SPAN == iota((TOKENS, CH), 1)).astype(BF)
    part_ref[1] = jnp.where(slots, dot(spread, vec_parts), low_ref[...]).astype(BF)

    back = back_matrix()
    for i in range(PEERS // GROUP):
        tokens = pl.ds(i * group_tokens, group_tokens)
        rows = jnp.concatenate([delta_ref[u, tokens, :] for u in range(CUBOIDS)], axis=0)
        moved = dot(back, rows).astype(BF)
        msg_ref[pl.ds(i * GROUP, GROUP), 0:PEER_ROWS, :] = moved.reshape(GROUP, PEER_ROWS, CH)
    back = piece_matrix()
    for i in range(PEERS // PIECE_GROUP):
        tokens = pl.ds(i * CH, CH)
        rows = jnp.concatenate([part_ref[0, tokens, :], part_ref[1, tokens, :]], axis=0)
        moved = dot(back, rows).astype(BF)
        msg_ref[pl.ds(i * PIECE_GROUP, PIECE_GROUP), PEER_ROWS:, :] = moved.reshape(
            PIECE_GROUP, PIECE_ROWS, CH
        )


def sum_kernel(recv_ref, piece_ref):
    summed = jnp.sum(recv_ref[:, PEER_ROWS:, :].astype(F32), axis=0)
    row, slots = vec_slots(PIECE_ROWS)
    slots = slots & (row >= SPAN)
    vec = summed + pltpu.roll(summed, CH - GLOBALS, 1)
    low = jnp.where(slots, 0.0, summed)
    weight = summed[:SPAN] + low[SPAN:]
    high = weight.astype(BF).astype(F32)
    vec_high = vec.astype(BF).astype(F32)
    vec_low = pltpu.roll(vec - vec_high, GLOBALS, 1)
    vec = jnp.where(iota((PIECE_ROWS, CH), 1) < GLOBALS, vec_high, vec_low)
    piece = jnp.where(slots, vec, jnp.concatenate([high, weight - high], axis=0)).astype(BF)
    piece_ref[...] = jnp.broadcast_to(piece[None], piece_ref.shape)


def spread_kernel(recv_ref, weight_ref, vec_ref):
    rows = PIECE_GROUP * PIECE_ROWS
    row, slots = vec_slots(rows)
    slots = slots & (row % PIECE_ROWS >= SPAN)
    target, source = iota((CH, rows), 0), iota((CH, rows), 1)
    joins = (source // PIECE_ROWS == target // SPAN) & (source % SPAN == target % SPAN)
    joins = joins.astype(BF)
    target, source = iota((PIECE_GROUP, rows), 0), iota((PIECE_GROUP, rows), 1)
    last = (source == target * PIECE_ROWS + PIECE_ROWS - 1).astype(BF)
    vec = []
    for i in range(PEERS // PIECE_GROUP):
        piece = recv_ref[pl.ds(i * PIECE_GROUP, PIECE_GROUP)].reshape(rows, CH)
        vec.append(dot(last, piece))
        piece = jnp.where(slots, 0.0, piece.astype(F32)).astype(BF)
        weight_ref[i] = dot(joins, piece)
    vec = jnp.concatenate(vec, axis=0).T
    vec_ref[...] = vec[:GLOBALS] + vec[GLOBALS : 2 * GLOBALS]


def place_kernel(shift_ref, recv_ref, out_ref, held):
    for i in range(PEERS // GROUP):
        held[pl.ds(i * GROUP_ROWS, GROUP_ROWS), :] = recv_ref[
            pl.ds(i * GROUP, GROUP), 0:PEER_ROWS, :
        ].reshape(GROUP_ROWS, CH)
    held[CELLS_DEV:, :] = held[:WINDOW, :]
    offset = (CELLS_DEV - tile_offset(shift_ref)) % CELLS_DEV
    mover = shift_matrix(offset % 16)
    base = offset - offset % 16
    for i in range(CELLS_DEV // GROUP_ROWS):
        start = pl.multiple_of((base + i * GROUP_ROWS) % CELLS_DEV, 16)
        moved = dot(mover, held[pl.ds(start, WINDOW), :]).astype(BF)
        out_ref[pl.ds(i * GROUP_ROWS, GROUP_ROWS), :] = moved


VMEM = pl.BlockSpec(memory_space=pltpu.VMEM)
SMEM = pl.BlockSpec(memory_space=pltpu.SMEM)
HBM = pl.BlockSpec(memory_space=pltpu.HBM)
PACK_PARAMS = pltpu.CompilerParams(vmem_limit_bytes=60 * 1024 * 1024)
PARAMS = pltpu.CompilerParams(vmem_limit_bytes=48 * 1024 * 1024)


def exchange(rows):
    return lax.all_to_all(rows, ("tile", "frame"), split_axis=0, concat_axis=0, tiled=True)


def body(cells, vectors, weights, cuboid_shift, cell_upstream, vector_upstream):
    message = pl.pallas_call(
        pack_kernel,
        out_shape=jax.ShapeDtypeStruct((PEERS, MSG_ROWS, CH), BF),
        in_specs=[SMEM] + [HBM] * 5,
        out_specs=VMEM,
        scratch_shapes=[
            pltpu.VMEM((CELLS_DEV + WINDOW, 2 * CH), BF),
            pltpu.VMEM((GLOBALS, CH), BF),
            pltpu.VMEM((4, CH, CH), BF),
            pltpu.VMEM((GLOBALS, CH), F32),
            pltpu.SemaphoreType.DMA((7,)),
        ],
        compiler_params=PACK_PARAMS,
        name="pack",
    )(cuboid_shift, cells[0], cell_upstream[0], vectors, weights, vector_upstream)
    received = exchange(message)
    message = pl.pallas_call(
        owner_kernel,
        out_shape=jax.ShapeDtypeStruct((PEERS, PEER_ROWS + PIECE_ROWS, CH), BF),
        in_specs=[VMEM] * 4,
        out_specs=VMEM,
        scratch_shapes=[
            pltpu.VMEM((CUBOIDS, TOKENS, CH), BF),
            pltpu.VMEM((CUBOIDS, TOKENS, CH), BF),
            pltpu.VMEM((CUBOIDS, TOKENS, CH), BF),
            pltpu.VMEM((3, CH, CH), BF),
            pltpu.VMEM((HEADS, CH, TOKENS), BF),
            pltpu.VMEM((HEADS, CH, TOKENS), BF),
            pltpu.VMEM((4, CH, CH), F32),
            pltpu.VMEM((4, PAIRS, CH), F32),
            pltpu.VMEM((2, TOKENS, CH), BF),
            pltpu.VMEM((TOKENS, CH), F32),
            pltpu.VMEM((TOKENS, CH), F32),
            pltpu.VMEM((TOKENS, CH), F32),
        ],
        compiler_params=PARAMS,
        name="owner",
    )(received, vectors, weights, vector_upstream)
    received = exchange(message)
    pieces = pl.pallas_call(
        sum_kernel,
        out_shape=jax.ShapeDtypeStruct((PEERS, PIECE_ROWS, CH), BF),
        in_specs=[VMEM],
        out_specs=VMEM,
        compiler_params=PARAMS,
        name="sum_pieces",
    )(received)
    pieces = exchange(pieces)
    cell_grad = pl.pallas_call(
        place_kernel,
        out_shape=jax.ShapeDtypeStruct((CELLS_DEV, CH), BF),
        in_specs=[SMEM, VMEM],
        out_specs=VMEM,
        scratch_shapes=[pltpu.VMEM((CELLS_DEV + WINDOW, CH), BF)],
        compiler_params=PARAMS,
        name="place",
    )(cuboid_shift, received)
    weight_grad, vector_grad = pl.pallas_call(
        spread_kernel,
        out_shape=[
            jax.ShapeDtypeStruct((4, CH, CH), F32),
            jax.ShapeDtypeStruct((GLOBALS, CH), F32),
        ],
        in_specs=[VMEM],
        out_specs=[VMEM, VMEM],
        compiler_params=PARAMS,
        name="spread",
    )(pieces)
    return cell_grad[None], weight_grad, vector_grad


def solution(mesh):
    in_specs = (P("frame", "tile", None), P(), P(), P(), P("frame", "tile", None), P())
    out_specs = (P("frame", "tile", None), P(), P())
    return jax.shard_map(body, mesh=mesh, in_specs=in_specs, out_specs=out_specs, check_vma=False)
```

```python
import math

import jax
import jax.numpy as jnp
from jax import lax
from jax.experimental import pallas as pl
from jax.experimental.pallas import tpu as pltpu
from jax.sharding import PartitionSpec as P

CH = 128
HEADS = 4
HDIM = 32
GLOBALS = 8
PAIRS = HEADS * GLOBALS
SPAN = 4
CELLS_DEV = 2048
PEERS = 128
PEER_ROWS = CELLS_DEV // PEERS
CUBOIDS = PEER_ROWS // SPAN
TOKENS = 512
QUERIES = 256
GROUP = 16
GROUP_ROWS = GROUP * PEER_ROWS
WINDOW = GROUP_ROWS + 16
MSG_ROWS = 40
PIECE_ROWS = 2 * SPAN
PIECE_GROUP = 32
VEC_LANES = 2 * GLOBALS
SCALE = HDIM**-0.5
LOG2E = math.log2(math.e)
BF = jnp.bfloat16
F32 = jnp.float32
HIGHEST = lax.Precision.HIGHEST
NT = (((1,), (1,)), ((), ()))


def dot(a, b):
    return jnp.dot(a, b, preferred_element_type=F32)


def dot_nt(a, b):
    return lax.dot_general(a, b, NT, preferred_element_type=F32)


def iota(shape, axis):
    return lax.broadcasted_iota(jnp.int32, shape, axis)


def split3(x):
    hi = x.astype(BF)
    rest = x - hi.astype(F32)
    mid = rest.astype(BF)
    low = (rest - mid.astype(F32)).astype(BF)
    return hi, mid, low


def head_blocks(rows):
    head = iota((GLOBALS, CH), 1) // HDIM
    return jnp.concatenate([jnp.where(head == h, rows, 0.0) for h in range(HEADS)], axis=0)


def head_diagonal(blocks):
    head = iota((GLOBALS, CH), 1) // HDIM
    total = jnp.zeros((GLOBALS, CH), F32)
    for h in range(HEADS):
        total += jnp.where(head == h, blocks[h * GLOBALS : (h + 1) * GLOBALS], 0.0)
    return total


def global_rows(vectors, weight):
    return dot(vectors.astype(BF), weight).astype(BF).astype(F32)


def global_upstream(vector_upstream, w_out):
    hi, mid, low = split3(vector_upstream)
    return dot_nt(hi, w_out) + dot_nt(mid, w_out) + dot_nt(low, w_out)


def tile_offset(shift_ref):
    return (shift_ref[0] * (lax.axis_index("tile") + 1)) % CELLS_DEV


def shift_matrix(step):
    return (iota((GROUP_ROWS, WINDOW), 1) == iota((GROUP_ROWS, WINDOW), 0) + step).astype(BF)


def pack_kernel(
    shift_ref,
    cells_hbm,
    up_hbm,
    vectors_hbm,
    weights_hbm,
    vup_hbm,
    msg_ref,
    held,
    vectors_ref,
    weights_ref,
    vup_ref,
    sems,
):
    whole, wrap = pl.ds(0, CELLS_DEV), pl.ds(CELLS_DEV, WINDOW)
    left, right = pl.ds(0, CH), pl.ds(CH, CH)
    copies = [
        pltpu.make_async_copy(source, target, sems.at[i])
        for i, (source, target) in enumerate(
            [
                (vectors_hbm, vectors_ref),
                (weights_hbm, weights_ref),
                (vup_hbm, vup_ref),
                (cells_hbm, held.at[whole, left]),
                (cells_hbm.at[pl.ds(0, WINDOW)], held.at[wrap, left]),
                (up_hbm, held.at[whole, right]),
                (up_hbm.at[pl.ds(0, WINDOW)], held.at[wrap, right]),
            ]
        )
    ]
    for copy in copies:
        copy.start()
    for copy in copies[:5]:
        copy.wait()
    vectors = vectors_ref[...].astype(F32)
    cells = held[:CELLS_DEV, :CH]
    query = head_blocks(global_rows(vectors, weights_ref[0])).astype(BF)
    upstream = head_blocks(global_upstream(vup_ref[...], weights_ref[3]))
    up_parts = jnp.concatenate([part.astype(F32) for part in split3(upstream)], axis=0).astype(BF)
    keys = dot(cells, weights_ref[1]).astype(BF)
    values = dot(cells, weights_ref[2]).astype(BF)
    score = dot_nt(query, keys) * SCALE
    dprob = dot_nt(up_parts, values)
    dprob = dprob[:PAIRS] + dprob[PAIRS : 2 * PAIRS] + dprob[2 * PAIRS :]
    top = jnp.max(score, axis=1, keepdims=True)
    weight = jnp.exp(score - top)
    total = jnp.sum(weight, axis=1, keepdims=True)
    inner = jnp.sum(weight * dprob, axis=1, keepdims=True)
    lane = iota((PAIRS, CH), 1)
    stats = jnp.where(lane == 0, top, jnp.where(lane == 1, total, jnp.where(lane == 2, inner, 0.0)))
    parts = [part.astype(F32) for part in split3(stats)] + [jnp.zeros((PAIRS, CH), F32)]
    rows = jnp.concatenate(parts, axis=0).T[:GLOBALS].astype(BF)
    msg_ref[:, 2 * PEER_ROWS :, :] = jnp.broadcast_to(rows[None], (PEERS, GLOBALS, CH))
    for copy in copies[5:]:
        copy.wait()
    offset = tile_offset(shift_ref)
    mover = shift_matrix(offset % 16)
    base = offset - offset % 16
    for i in range(CELLS_DEV // GROUP_ROWS):
        start = pl.multiple_of((base + i * GROUP_ROWS) % CELLS_DEV, 16)
        moved = dot(mover, held[pl.ds(start, WINDOW), :]).astype(BF)
        peers = pl.ds(i * GROUP, GROUP)
        msg_ref[peers, 0:PEER_ROWS, :] = moved[:, :CH].reshape(GROUP, PEER_ROWS, CH)
        msg_ref[peers, PEER_ROWS : 2 * PEER_ROWS, :] = moved[:, CH:].reshape(GROUP, PEER_ROWS, CH)


def regroup_matrix():
    row = iota((GROUP_ROWS, GROUP_ROWS), 0)
    column = iota((GROUP_ROWS, GROUP_ROWS), 1)
    source = (row // SPAN) % GROUP * PEER_ROWS + row // (GROUP * SPAN) * SPAN + row % SPAN
    return (column == source).astype(BF)


def piece_matrix():
    rows = PIECE_GROUP * PIECE_ROWS
    row = iota((rows, rows), 0)
    source = row // SPAN % 2 * CH + row // PIECE_ROWS * SPAN + row % SPAN
    return (iota((rows, rows), 1) == source).astype(BF)


def vec_slots(rows):
    row, lane = iota((rows, CH), 0), iota((rows, CH), 1)
    return row, (row % SPAN == SPAN - 1) & (lane < VEC_LANES)


def back_matrix():
    row = iota((GROUP_ROWS, GROUP_ROWS), 0)
    column = iota((GROUP_ROWS, GROUP_ROWS), 1)
    source = (row // SPAN) % CUBOIDS * (GROUP * SPAN) + row // PEER_ROWS * SPAN + row % SPAN
    return (column == source).astype(BF)


def owner_kernel(
    recv_ref,
    vectors_ref,
    weights_ref,
    vup_ref,
    msg_ref,
    cells_ref,
    up_ref,
    delta_ref,
    weights_t_ref,
    query_m,
    grad_m,
    w_sum,
    g_sum,
    part_ref,
    low_ref,
    dk_ref,
    dv_ref,
):
    group_tokens = GROUP * SPAN
    mover = regroup_matrix()
    for i in range(PEERS // GROUP):
        peers = pl.ds(i * GROUP, GROUP)
        rows = jnp.concatenate(
            [
                recv_ref[peers, 0:PEER_ROWS, :].reshape(GROUP_ROWS, CH),
                recv_ref[peers, PEER_ROWS : 2 * PEER_ROWS, :].reshape(GROUP_ROWS, CH),
            ],
            axis=1,
        )
        moved = dot(mover, rows).astype(BF)
        for u in range(CUBOIDS):
            piece = moved[u * group_tokens : (u + 1) * group_tokens]
            cells_ref[u, pl.ds(i * group_tokens, group_tokens), :] = piece[:, :CH]
            up_ref[u, pl.ds(i * group_tokens, group_tokens), :] = piece[:, CH:]

    vectors = vectors_ref[...].astype(F32)
    w_q, w_k, w_v, w_o = (weights_ref[i] for i in range(4))
    for i in range(3):
        weights_t_ref[i] = weights_ref[i].astype(F32).T.astype(BF)
    gk = head_blocks(global_rows(vectors, w_k))
    gv = head_blocks(global_rows(vectors, w_v))
    gk_b, gv_b = gk.astype(BF), gv.astype(BF)
    zero = jnp.zeros((PAIRS, CH), F32)
    shared = {}

    def global_operands():
        gq = head_blocks(global_rows(vectors, w_q))
        gg = head_blocks(global_upstream(vup_ref[...], w_o))
        gg3 = [part.astype(F32) for part in split3(gg)]
        shared["gq_b"] = gq.astype(BF)
        for name, blocks in (("gk_t", gk), ("gv_t", gv)):
            wide = jnp.concatenate([blocks, zero, zero, zero], axis=0)
            shared[name] = wide.T[:, :PAIRS].astype(BF)
        shared["gg_parts"] = jnp.concatenate(gg3, axis=0).astype(BF)
        shared["gq_t3"] = jnp.concatenate([gq, gq, gq, zero], axis=0).T.astype(BF)
        first = [gg3[0], gg3[0], gg3[0], gg3[1]]
        shared["gg_t6a"] = jnp.concatenate(first, axis=0).T.astype(BF)
        second = [gg3[1], gg3[2], zero, zero]
        shared["gg_t6b"] = jnp.concatenate(second, axis=0).T.astype(BF)

    def global_softmax():
        stats = recv_ref[:, 2 * PEER_ROWS :, :].astype(F32).reshape(PEERS * GLOBALS, CH)
        stats = stats + pltpu.roll(stats, CH - PAIRS, 1) + pltpu.roll(stats, CH - 2 * PAIRS, 1)
        stats = stats.reshape(PEERS, GLOBALS, CH)
        tops = stats[:, 0:1, :]
        top = jnp.max(tops, axis=0)
        summed = jnp.sum(jnp.exp(tops - top[None]) * stats, axis=0)
        lanes = jnp.where(iota((GLOBALS, CH), 0) == 0, top, summed)
        columns = jnp.concatenate([lanes, jnp.zeros((CH - GLOBALS, CH), F32)], axis=0).T
        shared["g_top"] = columns[:PAIRS, 0:1]
        shared["g_inv"] = 1.0 / columns[:PAIRS, 1:2]
        shared["g_row"] = columns[:PAIRS, 2:3] * shared["g_inv"]

    query_m[...] = jnp.zeros_like(query_m)
    grad_m[...] = jnp.zeros_like(grad_m)
    w_sum[...] = jnp.zeros_like(w_sum)
    g_sum[...] = jnp.zeros_like(g_sum)

    def heads(h):
        return slice(h * HDIM, (h + 1) * HDIM)

    class Cuboid:
        def __init__(self, u):
            self.u, self.slot = u, u % 2
            self.rows = {n: [[] for _ in range(HEADS)] for n in ("p", "ds", "out", "dq")}

        def project_query(self):
            cells = cells_ref[self.u]
            self.query_t = dot_nt(weights_t_ref[0], cells).astype(BF)
            for h in range(HEADS):
                query_m[self.slot, h, heads(h), :] = self.query_t[heads(h)]
            self.key = dot(cells, w_k).astype(BF)

        def project_grad(self):
            self.grad_t = dot_nt(w_o, up_ref[self.u]).astype(BF)
            for h in range(HEADS):
                grad_m[self.slot, h, heads(h), :] = self.grad_t[heads(h)]
            self.value = dot(cells_ref[self.u], w_v).astype(BF)

        def project_global(self):
            self.s_global = dot(gk_b, self.query_t)
            self.d_global = dot(gv_b, self.grad_t)

        def project_transposed(self):
            cells = cells_ref[self.u]
            self.key_t = dot_nt(weights_t_ref[1], cells).astype(BF)
            self.value_t = dot_nt(weights_t_ref[2], cells).astype(BF)

        def project_rows(self):
            self.query = dot(cells_ref[self.u], w_q).astype(BF)
            self.grad = dot_nt(up_ref[self.u], w_o).astype(BF)

        def scores(self, h, q):
            columns = pl.ds(q, QUERIES)
            return (
                dot(self.key, query_m[self.slot, h, :, columns]),
                dot(self.value, grad_m[self.slot, h, :, columns]),
            )

        def softmax(self, h, q, score, dprob):
            rows = slice(h * GLOBALS, (h + 1) * GLOBALS)
            s_glob = self.s_global[rows, q : q + QUERIES]
            d_glob = self.d_global[rows, q : q + QUERIES]
            top = jnp.maximum(
                jnp.max(score, axis=0, keepdims=True), jnp.max(s_glob, axis=0, keepdims=True)
            )
            e_local = jnp.exp2((score - top) * (SCALE * LOG2E))
            e_global = jnp.exp2((s_glob - top) * (SCALE * LOG2E))
            total = jnp.sum(e_local, axis=0, keepdims=True) + jnp.sum(
                e_global, axis=0, keepdims=True
            )
            inv = 1.0 / total
            p_local = e_local * inv
            p_global = e_global * inv
            inner = jnp.sum(p_local * dprob, axis=0, keepdims=True) + jnp.sum(
                p_global * d_glob, axis=0, keepdims=True
            )
            self.rows["p"][h].append(p_global)
            self.rows["ds"][h].append(p_global * (d_glob - inner) * SCALE)
            return p_local.astype(BF), (p_local * (dprob - inner) * SCALE).astype(BF)

        def products(self, h, q, p_low, ds_low):
            part = heads(h)
            self.rows["out"][h].append(dot(self.value_t[part], p_low))
            self.rows["dq"][h].append(dot(self.key_t[part], ds_low))
            d_value = dot(p_low, self.grad[q : q + QUERIES])
            d_key = dot(ds_low, self.query[q : q + QUERIES])
            if q == 0:
                dv_ref[self.slot, :, part] = d_value[:, part]
                dk_ref[self.slot, :, part] = d_key[:, part]
            else:
                dv_ref[self.slot, :, part] += d_value[:, part]
                dk_ref[self.slot, :, part] += d_key[:, part]

        def whole(self, name):
            rows = [jnp.concatenate(row, axis=1) for row in self.rows[name]]
            return jnp.concatenate(rows, axis=0)

        def finish_queries(self):
            p_rows, ds_rows = self.whole("p").astype(BF), self.whole("ds").astype(BF)
            self.out_t = (self.whole("out") + dot(shared["gv_t"], p_rows)).astype(BF)
            self.dq_t = (self.whole("dq") + dot(shared["gk_t"], ds_rows)).astype(BF)
            g_sum[1] += dot(ds_rows, self.query)
            g_sum[2] += dot(p_rows, self.grad)

        def finish_global(self):
            score = dot(shared["gq_b"], self.key_t) * SCALE
            prob = jnp.exp(score - shared["g_top"]) * shared["g_inv"]
            dprob = dot(shared["gg_parts"], self.value_t)
            dprob = dprob[:PAIRS] + dprob[PAIRS : 2 * PAIRS] + dprob[2 * PAIRS :]
            dscore = prob * (dprob - shared["g_row"]) * SCALE
            none = jnp.zeros((PAIRS, TOKENS), BF)
            p_hi, p_mid, p_low = split3(prob)
            self.d_parts = jnp.concatenate([*split3(dscore), none], axis=0)
            self.p_parts = jnp.concatenate([p_hi, p_mid, p_low, p_hi], axis=0)
            self.p_more = jnp.concatenate([p_mid, p_hi, none, none], axis=0)
            g_query = dot(self.d_parts[: 3 * PAIRS], self.key)
            g_att = dot(self.p_parts[: 3 * PAIRS], self.value)
            g_sum[0] += g_query[:PAIRS] + g_query[PAIRS : 2 * PAIRS] + g_query[2 * PAIRS :]
            g_sum[3] += g_att[:PAIRS] + g_att[PAIRS : 2 * PAIRS] + g_att[2 * PAIRS :]

        def finish_keys(self):
            more = dot(shared["gq_t3"], self.d_parts)
            self.dk_t = (dk_ref[self.slot].T + more).astype(BF)

        def finish_values(self):
            more = dot(shared["gg_t6a"], self.p_parts) + dot(shared["gg_t6b"], self.p_more)
            self.dv_t = (dv_ref[self.slot].T + more).astype(BF)

        def finish_weights(self):
            cells = cells_ref[self.u]
            w_sum[0] += dot(self.dq_t, cells)
            w_sum[1] += dot(self.dk_t, cells)
            w_sum[2] += dot(self.dv_t, cells)
            w_sum[3] += dot(self.out_t, up_ref[self.u])

        def finish_cells(self):
            delta = dot(w_q, self.dq_t) + dot(w_k, self.dk_t) + dot(w_v, self.dv_t)
            delta_ref[self.u] = delta.T.astype(BF)

        def before(self):
            return [
                self.project_query,
                self.project_grad,
                self.project_global,
                self.project_transposed,
                self.project_rows,
            ]

        def after(self):
            return [
                self.finish_queries,
                self.finish_global,
                self.finish_keys,
                self.finish_values,
                self.finish_weights,
                self.finish_cells,
            ]

    cuboids = [Cuboid(u) for u in range(CUBOIDS)]
    for task in cuboids[0].before():
        task()
    order = [(c, h, q) for c in cuboids for h in range(HEADS) for q in range(0, TOKENS, QUERIES)]
    per_cuboid = len(order) // CUBOIDS
    ready = cuboids[0].scores(*order[0][1:])
    low = None
    for i, (cuboid, *step) in enumerate(order):
        place = i % per_cuboid
        u = cuboid.u
        if place == 0:
            early = cuboids[u + 1].before() if u + 1 < CUBOIDS else []
            late = cuboids[u - 1].after() if u > 0 else [global_operands, global_softmax]
        following = None
        if place + 1 == per_cuboid:
            for task in early + late:
                task()
        if i + 1 < len(order):
            following = order[i + 1][0].scores(*order[i + 1][1:])
        now = cuboid.softmax(*step, *ready)
        if low is not None:
            order[i - 1][0].products(*order[i - 1][1:], *low)
        if place > 0 and late:
            late.pop(0)()
        low = now
        if early:
            early.pop(0)()
        ready = following
    order[-1][0].products(*order[-1][1:], *low)
    for task in cuboids[-1].after():
        task()

    def outer(a, b):
        a = jnp.concatenate([a, jnp.zeros((CH - GLOBALS, CH), F32)], axis=0).T
        b = jnp.concatenate([b, jnp.zeros((CH - GLOBALS, CH), F32)], axis=0)
        return jnp.dot(a, b, precision=HIGHEST, preferred_element_type=F32)

    vec = jnp.zeros((GLOBALS, CH), F32)
    for i in range(4):
        g_part = head_diagonal(g_sum[i])
        if i < 3:
            total = w_sum[i].T + outer(vectors, g_part)
            hi, mid, low = split3(g_part)
            weight = weights_ref[i]
            vec += dot_nt(hi, weight) + dot_nt(mid, weight) + dot_nt(low, weight)
        else:
            total = w_sum[3] + outer(g_part, vup_ref[...])
        high = total.astype(BF)
        rows = pl.ds(i * CH, CH)
        part_ref[0, rows, :] = high
        low_ref[rows, :] = total - high.astype(F32)
    hi, mid, _ = split3(vec)
    vec_parts = jnp.concatenate(
        [hi.astype(F32), mid.astype(F32), jnp.zeros((CH - VEC_LANES, CH), F32)], axis=0
    ).T.astype(BF)
    row, slots = vec_slots(TOKENS)
    spread = (iota((TOKENS, CH), 0) // SPAN == iota((TOKENS, CH), 1)).astype(BF)
    part_ref[1] = jnp.where(slots, dot(spread, vec_parts), low_ref[...]).astype(BF)

    back = back_matrix()
    for i in range(PEERS // GROUP):
        tokens = pl.ds(i * group_tokens, group_tokens)
        rows = jnp.concatenate([delta_ref[u, tokens, :] for u in range(CUBOIDS)], axis=0)
        moved = dot(back, rows).astype(BF)
        msg_ref[pl.ds(i * GROUP, GROUP), 0:PEER_ROWS, :] = moved.reshape(GROUP, PEER_ROWS, CH)
    back = piece_matrix()
    for i in range(PEERS // PIECE_GROUP):
        tokens = pl.ds(i * CH, CH)
        rows = jnp.concatenate([part_ref[0, tokens, :], part_ref[1, tokens, :]], axis=0)
        moved = dot(back, rows).astype(BF)
        msg_ref[pl.ds(i * PIECE_GROUP, PIECE_GROUP), PEER_ROWS:, :] = moved.reshape(
            PIECE_GROUP, PIECE_ROWS, CH
        )


def sum_kernel(recv_ref, piece_ref):
    summed = jnp.sum(recv_ref[:, PEER_ROWS:, :].astype(F32), axis=0)
    row, slots = vec_slots(PIECE_ROWS)
    slots = slots & (row >= SPAN)
    vec = summed + pltpu.roll(summed, CH - GLOBALS, 1)
    low = jnp.where(slots, 0.0, summed)
    weight = summed[:SPAN] + low[SPAN:]
    high = weight.astype(BF).astype(F32)
    vec_high = vec.astype(BF).astype(F32)
    vec_low = pltpu.roll(vec - vec_high, GLOBALS, 1)
    vec = jnp.where(iota((PIECE_ROWS, CH), 1) < GLOBALS, vec_high, vec_low)
    piece = jnp.where(slots, vec, jnp.concatenate([high, weight - high], axis=0)).astype(BF)
    piece_ref[...] = jnp.broadcast_to(piece[None], piece_ref.shape)


def spread_kernel(recv_ref, weight_ref, vec_ref):
    rows = PIECE_GROUP * PIECE_ROWS
    row, slots = vec_slots(rows)
    slots = slots & (row % PIECE_ROWS >= SPAN)
    target, source = iota((CH, rows), 0), iota((CH, rows), 1)
    joins = (source // PIECE_ROWS == target // SPAN) & (source % SPAN == target % SPAN)
    joins = joins.astype(BF)
    target, source = iota((PIECE_GROUP, rows), 0), iota((PIECE_GROUP, rows), 1)
    last = (source == target * PIECE_ROWS + PIECE_ROWS - 1).astype(BF)
    vec = []
    for i in range(PEERS // PIECE_GROUP):
        piece = recv_ref[pl.ds(i * PIECE_GROUP, PIECE_GROUP)].reshape(rows, CH)
        vec.append(dot(last, piece))
        piece = jnp.where(slots, 0.0, piece.astype(F32)).astype(BF)
        weight_ref[i] = dot(joins, piece)
    vec = jnp.concatenate(vec, axis=0).T
    vec_ref[...] = vec[:GLOBALS] + vec[GLOBALS : 2 * GLOBALS]


def place_kernel(shift_ref, recv_ref, out_ref, held):
    for i in range(PEERS // GROUP):
        held[pl.ds(i * GROUP_ROWS, GROUP_ROWS), :] = recv_ref[
            pl.ds(i * GROUP, GROUP), 0:PEER_ROWS, :
        ].reshape(GROUP_ROWS, CH)
    held[CELLS_DEV:, :] = held[:WINDOW, :]
    offset = (CELLS_DEV - tile_offset(shift_ref)) % CELLS_DEV
    mover = shift_matrix(offset % 16)
    base = offset - offset % 16
    for i in range(CELLS_DEV // GROUP_ROWS):
        start = pl.multiple_of((base + i * GROUP_ROWS) % CELLS_DEV, 16)
        moved = dot(mover, held[pl.ds(start, WINDOW), :]).astype(BF)
        out_ref[pl.ds(i * GROUP_ROWS, GROUP_ROWS), :] = moved


VMEM = pl.BlockSpec(memory_space=pltpu.VMEM)
SMEM = pl.BlockSpec(memory_space=pltpu.SMEM)
HBM = pl.BlockSpec(memory_space=pltpu.HBM)
PACK_PARAMS = pltpu.CompilerParams(vmem_limit_bytes=58_000_000)
PARAMS = pltpu.CompilerParams(vmem_limit_bytes=48 * 1024 * 1024)


def exchange(rows):
    return lax.all_to_all(rows, ("tile", "frame"), split_axis=0, concat_axis=0, tiled=True)


def body(cells, vectors, weights, cuboid_shift, cell_upstream, vector_upstream):
    message = pl.pallas_call(
        pack_kernel,
        out_shape=pltpu.VMEM((PEERS, MSG_ROWS, CH), BF),
        in_specs=[SMEM] + [HBM] * 5,
        out_specs=VMEM,
        scratch_shapes=[
            pltpu.VMEM((CELLS_DEV + WINDOW, 2 * CH), BF),
            pltpu.VMEM((GLOBALS, CH), BF),
            pltpu.VMEM((4, CH, CH), BF),
            pltpu.VMEM((GLOBALS, CH), F32),
            pltpu.SemaphoreType.DMA((7,)),
        ],
        compiler_params=PACK_PARAMS,
        name="pack",
    )(cuboid_shift, cells[0], cell_upstream[0], vectors, weights, vector_upstream)
    received = exchange(message)
    message = pl.pallas_call(
        owner_kernel,
        out_shape=pltpu.VMEM((PEERS, PEER_ROWS + PIECE_ROWS, CH), BF),
        in_specs=[VMEM] * 4,
        out_specs=VMEM,
        scratch_shapes=[
            pltpu.VMEM((CUBOIDS, TOKENS, CH), BF),
            pltpu.VMEM((CUBOIDS, TOKENS, CH), BF),
            pltpu.VMEM((CUBOIDS, TOKENS, CH), BF),
            pltpu.VMEM((3, CH, CH), BF),
            pltpu.VMEM((2, HEADS, CH, TOKENS), BF),
            pltpu.VMEM((2, HEADS, CH, TOKENS), BF),
            pltpu.VMEM((4, CH, CH), F32),
            pltpu.VMEM((4, PAIRS, CH), F32),
            pltpu.VMEM((2, TOKENS, CH), BF),
            pltpu.VMEM((TOKENS, CH), F32),
            pltpu.VMEM((2, TOKENS, CH), F32),
            pltpu.VMEM((2, TOKENS, CH), F32),
        ],
        compiler_params=PARAMS,
        name="owner",
    )(received, vectors, weights, vector_upstream)
    received = exchange(message)
    pieces = pl.pallas_call(
        sum_kernel,
        out_shape=pltpu.VMEM((PEERS, PIECE_ROWS, CH), BF),
        in_specs=[VMEM],
        out_specs=VMEM,
        compiler_params=PARAMS,
        name="sum_pieces",
    )(received)
    pieces = exchange(pieces)
    cell_grad = pl.pallas_call(
        place_kernel,
        out_shape=jax.ShapeDtypeStruct((CELLS_DEV, CH), BF),
        in_specs=[SMEM, VMEM],
        out_specs=VMEM,
        scratch_shapes=[pltpu.VMEM((CELLS_DEV + WINDOW, CH), BF)],
        compiler_params=PARAMS,
        name="place",
    )(cuboid_shift, received)
    weight_grad, vector_grad = pl.pallas_call(
        spread_kernel,
        out_shape=[
            jax.ShapeDtypeStruct((4, CH, CH), F32),
            jax.ShapeDtypeStruct((GLOBALS, CH), F32),
        ],
        in_specs=[VMEM],
        out_specs=[VMEM, VMEM],
        compiler_params=PARAMS,
        name="spread",
    )(pieces)
    return cell_grad[None], weight_grad, vector_grad


def solution(mesh):
    in_specs = (P("frame", "tile", None), P(), P(), P(), P("frame", "tile", None), P())
    out_specs = (P("frame", "tile", None), P(), P())
    return jax.shard_map(body, mesh=mesh, in_specs=in_specs, out_specs=out_specs, check_vma=False)
```

```python
import math

import jax
import jax.numpy as jnp
from jax import lax
from jax.experimental import pallas as pl
from jax.experimental.pallas import tpu as pltpu
from jax.sharding import PartitionSpec as P

CH = 128
HEADS = 4
HDIM = 32
GLOBALS = 8
PAIRS = HEADS * GLOBALS
SPAN = 4
CELLS_DEV = 2048
PEERS = 128
PEER_ROWS = CELLS_DEV // PEERS
CUBOIDS = PEER_ROWS // SPAN
TOKENS = 512
QUERIES = 256
GROUP = 16
GROUP_ROWS = GROUP * PEER_ROWS
WINDOW = GROUP_ROWS + 16
MSG_ROWS = 40
PIECE_ROWS = 2 * SPAN
PIECE_GROUP = 32
VEC_LANES = 2 * GLOBALS
SCALE = HDIM**-0.5
LOG2E = math.log2(math.e)
BF = jnp.bfloat16
F32 = jnp.float32
HIGHEST = lax.Precision.HIGHEST
NT = (((1,), (1,)), ((), ()))


def dot(a, b):
    return jnp.dot(a, b, preferred_element_type=F32)


def dot_nt(a, b):
    return lax.dot_general(a, b, NT, preferred_element_type=F32)


def iota(shape, axis):
    return lax.broadcasted_iota(jnp.int32, shape, axis)


def split3(x):
    hi = x.astype(BF)
    rest = x - hi.astype(F32)
    mid = rest.astype(BF)
    low = (rest - mid.astype(F32)).astype(BF)
    return hi, mid, low


def head_blocks(rows):
    head = iota((GLOBALS, CH), 1) // HDIM
    return jnp.concatenate([jnp.where(head == h, rows, 0.0) for h in range(HEADS)], axis=0)


def head_diagonal(blocks):
    head = iota((GLOBALS, CH), 1) // HDIM
    total = jnp.zeros((GLOBALS, CH), F32)
    for h in range(HEADS):
        total += jnp.where(head == h, blocks[h * GLOBALS : (h + 1) * GLOBALS], 0.0)
    return total


def global_rows(vectors, weight):
    return dot(vectors.astype(BF), weight).astype(BF).astype(F32)


def global_upstream(vector_upstream, w_out):
    hi, mid, low = split3(vector_upstream)
    return dot_nt(hi, w_out) + dot_nt(mid, w_out) + dot_nt(low, w_out)


def tile_offset(shift_ref):
    return (shift_ref[0] * (lax.axis_index("tile") + 1)) % CELLS_DEV


def shift_matrix(step):
    return (iota((GROUP_ROWS, WINDOW), 1) == iota((GROUP_ROWS, WINDOW), 0) + step).astype(BF)


def pack_kernel(
    shift_hbm,
    cells_hbm,
    up_hbm,
    vectors_hbm,
    weights_hbm,
    vup_hbm,
    msg_ref,
    held,
    vectors_ref,
    weights_ref,
    vup_ref,
    shift_ref,
    sems,
):
    whole, wrap = pl.ds(0, CELLS_DEV), pl.ds(CELLS_DEV, WINDOW)
    left, right = pl.ds(0, CH), pl.ds(CH, CH)
    copies = [
        pltpu.make_async_copy(source, target, sems.at[i])
        for i, (source, target) in enumerate(
            [
                (vectors_hbm, vectors_ref),
                (weights_hbm, weights_ref),
                (vup_hbm, vup_ref),
                (cells_hbm, held.at[whole, left]),
                (cells_hbm.at[pl.ds(0, WINDOW)], held.at[wrap, left]),
                (up_hbm, held.at[whole, right]),
                (up_hbm.at[pl.ds(0, WINDOW)], held.at[wrap, right]),
                (shift_hbm, shift_ref),
            ]
        )
    ]
    for copy in copies:
        copy.start()
    for copy in copies[:5]:
        copy.wait()
    vectors = vectors_ref[...].astype(F32)
    cells = held[:CELLS_DEV, :CH]
    query = head_blocks(global_rows(vectors, weights_ref[0])).astype(BF)
    upstream = head_blocks(global_upstream(vup_ref[...], weights_ref[3]))
    up_parts = jnp.concatenate([part.astype(F32) for part in split3(upstream)], axis=0).astype(BF)
    keys = dot(cells, weights_ref[1]).astype(BF)
    values = dot(cells, weights_ref[2]).astype(BF)
    score = dot_nt(query, keys) * SCALE
    dprob = dot_nt(up_parts, values)
    dprob = dprob[:PAIRS] + dprob[PAIRS : 2 * PAIRS] + dprob[2 * PAIRS :]
    top = jnp.max(score, axis=1, keepdims=True)
    weight = jnp.exp(score - top)
    total = jnp.sum(weight, axis=1, keepdims=True)
    inner = jnp.sum(weight * dprob, axis=1, keepdims=True)
    lane = iota((PAIRS, CH), 1)
    stats = jnp.where(lane == 0, top, jnp.where(lane == 1, total, jnp.where(lane == 2, inner, 0.0)))
    parts = [part.astype(F32) for part in split3(stats)] + [jnp.zeros((PAIRS, CH), F32)]
    rows = jnp.concatenate(parts, axis=0).T[:GLOBALS].astype(BF)
    msg_ref[:, 2 * PEER_ROWS :, :] = jnp.broadcast_to(rows[None], (PEERS, GLOBALS, CH))
    for copy in copies[5:]:
        copy.wait()
    offset = tile_offset(shift_ref)
    mover = shift_matrix(offset % 16)
    base = offset - offset % 16
    for i in range(CELLS_DEV // GROUP_ROWS):
        start = pl.multiple_of((base + i * GROUP_ROWS) % CELLS_DEV, 16)
        moved = dot(mover, held[pl.ds(start, WINDOW), :]).astype(BF)
        peers = pl.ds(i * GROUP, GROUP)
        msg_ref[peers, 0:PEER_ROWS, :] = moved[:, :CH].reshape(GROUP, PEER_ROWS, CH)
        msg_ref[peers, PEER_ROWS : 2 * PEER_ROWS, :] = moved[:, CH:].reshape(GROUP, PEER_ROWS, CH)


def regroup_matrix():
    row = iota((GROUP_ROWS, GROUP_ROWS), 0)
    column = iota((GROUP_ROWS, GROUP_ROWS), 1)
    source = (row // SPAN) % GROUP * PEER_ROWS + row // (GROUP * SPAN) * SPAN + row % SPAN
    return (column == source).astype(BF)


def piece_matrix():
    rows = PIECE_GROUP * PIECE_ROWS
    row = iota((rows, rows), 0)
    source = row // SPAN % 2 * CH + row // PIECE_ROWS * SPAN + row % SPAN
    return (iota((rows, rows), 1) == source).astype(BF)


def vec_slots(rows):
    row, lane = iota((rows, CH), 0), iota((rows, CH), 1)
    return row, (row % SPAN == SPAN - 1) & (lane < VEC_LANES)


def back_matrix():
    row = iota((GROUP_ROWS, GROUP_ROWS), 0)
    column = iota((GROUP_ROWS, GROUP_ROWS), 1)
    source = (row // SPAN) % CUBOIDS * (GROUP * SPAN) + row // PEER_ROWS * SPAN + row % SPAN
    return (column == source).astype(BF)


def owner_kernel(
    recv_ref,
    vectors_ref,
    weights_ref,
    vup_ref,
    msg_ref,
    cells_ref,
    up_ref,
    delta_ref,
    query_m,
    grad_m,
    w_sum,
    g_sum,
    part_ref,
    low_ref,
    dk_ref,
    dv_ref,
):
    group_tokens = GROUP * SPAN
    mover = regroup_matrix()
    for i in range(PEERS // GROUP):
        peers = pl.ds(i * GROUP, GROUP)
        rows = jnp.concatenate(
            [
                recv_ref[peers, 0:PEER_ROWS, :].reshape(GROUP_ROWS, CH),
                recv_ref[peers, PEER_ROWS : 2 * PEER_ROWS, :].reshape(GROUP_ROWS, CH),
            ],
            axis=1,
        )
        moved = dot(mover, rows).astype(BF)
        for u in range(CUBOIDS):
            piece = moved[u * group_tokens : (u + 1) * group_tokens]
            cells_ref[u, pl.ds(i * group_tokens, group_tokens), :] = piece[:, :CH]
            up_ref[u, pl.ds(i * group_tokens, group_tokens), :] = piece[:, CH:]

    vectors = vectors_ref[...].astype(F32)
    w_q, w_k, w_v, w_o = (weights_ref[i] for i in range(4))
    w_qkv = jnp.concatenate([w_q, w_k, w_v], axis=1)
    w_q_t = w_q.T
    gk = head_blocks(global_rows(vectors, w_k))
    gv = head_blocks(global_rows(vectors, w_v))
    gk_b, gv_b = gk.astype(BF), gv.astype(BF)
    zero = jnp.zeros((PAIRS, CH), F32)
    shared = {}

    def global_operands():
        gq = head_blocks(global_rows(vectors, w_q))
        gg = head_blocks(global_upstream(vup_ref[...], w_o))
        gg3 = [part.astype(F32) for part in split3(gg)]
        shared["gq_b"] = gq.astype(BF)
        for name, blocks in (("gk_t", gk), ("gv_t", gv)):
            wide = jnp.concatenate([blocks, zero, zero, zero], axis=0)
            shared[name] = wide.T[:, :PAIRS].astype(BF)
        shared["gg_parts"] = jnp.concatenate(gg3, axis=0).astype(BF)
        shared["gq2"] = jnp.concatenate([gq, gq, zero, zero], axis=0).astype(BF)
        shared["gg3"] = jnp.concatenate([gg3[0], gg3[0], gg3[1], zero], axis=0).astype(BF)

    def global_softmax():
        stats = recv_ref[:, 2 * PEER_ROWS :, :].astype(F32).reshape(PEERS * GLOBALS, CH)
        stats = stats + pltpu.roll(stats, CH - PAIRS, 1) + pltpu.roll(stats, CH - 2 * PAIRS, 1)
        stats = stats.reshape(PEERS, GLOBALS, CH)
        tops = stats[:, 0:1, :]
        top = jnp.max(tops, axis=0)
        summed = jnp.sum(jnp.exp(tops - top[None]) * stats, axis=0)
        lanes = jnp.where(iota((GLOBALS, CH), 0) == 0, top, summed)
        columns = jnp.concatenate([lanes, jnp.zeros((CH - GLOBALS, CH), F32)], axis=0).T
        shared["g_top"] = columns[:PAIRS, 0:1]
        shared["g_inv"] = 1.0 / columns[:PAIRS, 1:2]
        shared["g_row"] = columns[:PAIRS, 2:3] * shared["g_inv"]

    query_m[...] = jnp.zeros_like(query_m)
    grad_m[...] = jnp.zeros_like(grad_m)
    w_sum[...] = jnp.zeros_like(w_sum)
    g_sum[...] = jnp.zeros_like(g_sum)

    def heads(h):
        return slice(h * HDIM, (h + 1) * HDIM)

    class Cuboid:
        def __init__(self, u):
            self.u, self.slot = u, u % 2
            self.low = []
            self.rows = {n: [[] for _ in range(HEADS)] for n in ("p", "ds", "out", "dq")}

        def project_query(self):
            cells = cells_ref[self.u]
            self.query_t = dot_nt(w_q_t, cells).astype(BF)
            for h in range(HEADS):
                query_m[self.slot, h, heads(h), :] = self.query_t[heads(h)]
            self.key = dot(cells, w_k).astype(BF)

        def project_grad(self):
            self.grad_t = dot_nt(w_o, up_ref[self.u]).astype(BF)
            for h in range(HEADS):
                grad_m[self.slot, h, heads(h), :] = self.grad_t[heads(h)]
            self.value = dot(cells_ref[self.u], w_v).astype(BF)

        def project_global(self):
            self.s_global = dot(gk_b, self.query_t)
            self.d_global = dot(gv_b, self.grad_t)

        def project_transposed(self):
            self.key_t = self.key.T
            self.value_t = self.value.T

        def project_rows(self):
            self.query = self.query_t.T
            self.grad = self.grad_t.T

        def scores(self, h, q):
            columns = pl.ds(q, QUERIES)
            return (
                dot(self.key, query_m[self.slot, h, :, columns]),
                dot(self.value, grad_m[self.slot, h, :, columns]),
            )

        def softmax(self, h, q, score, dprob):
            rows = slice(h * GLOBALS, (h + 1) * GLOBALS)
            s_glob = self.s_global[rows, q : q + QUERIES]
            d_glob = self.d_global[rows, q : q + QUERIES]
            top = jnp.maximum(
                jnp.max(score, axis=0, keepdims=True), jnp.max(s_glob, axis=0, keepdims=True)
            )
            e_local = jnp.exp2((score - top) * (SCALE * LOG2E))
            e_global = jnp.exp2((s_glob - top) * (SCALE * LOG2E))
            total = jnp.sum(e_local, axis=0, keepdims=True) + jnp.sum(
                e_global, axis=0, keepdims=True
            )
            inv = 1.0 / total
            p_local = e_local * inv
            p_global = e_global * inv
            inner = jnp.sum(p_local * dprob, axis=0, keepdims=True) + jnp.sum(
                p_global * d_glob, axis=0, keepdims=True
            )
            self.rows["p"][h].append(p_global)
            self.rows["ds"][h].append(p_global * (d_glob - inner) * SCALE)
            return p_local.astype(BF), (p_local * (dprob - inner) * SCALE).astype(BF)

        def products(self, h, q, p_low, ds_low):
            part = heads(h)
            self.rows["out"][h].append(dot(self.value_t[part], p_low))
            self.rows["dq"][h].append(dot(self.key_t[part], ds_low))
            self.low.append((p_low, ds_low))
            if q + QUERIES == TOKENS:
                p_low, ds_low = (jnp.concatenate(x, axis=1) for x in zip(*self.low))
                self.low = []
                dv_ref[self.slot, :, part] = dot(p_low, self.grad)[:, part]
                dk_ref[self.slot, :, part] = dot(ds_low, self.query)[:, part]

        def whole(self, name):
            rows = [jnp.concatenate(row, axis=1) for row in self.rows[name]]
            return jnp.concatenate(rows, axis=0)

        def finish_queries(self):
            p_rows, ds_rows = self.whole("p").astype(BF), self.whole("ds").astype(BF)
            self.out_t = (self.whole("out") + dot(shared["gv_t"], p_rows)).astype(BF)
            self.dq_t = (self.whole("dq") + dot(shared["gk_t"], ds_rows)).astype(BF)
            g_sum[1] += dot(ds_rows, self.query)
            g_sum[2] += dot(p_rows, self.grad)

        def finish_global(self):
            score = dot(shared["gq_b"], self.key_t) * SCALE
            prob = jnp.exp(score - shared["g_top"]) * shared["g_inv"]
            dprob = dot(shared["gg_parts"], self.value_t)
            dprob = dprob[:PAIRS] + dprob[PAIRS : 2 * PAIRS] + dprob[2 * PAIRS :]
            dscore = prob * (dprob - shared["g_row"]) * SCALE
            p_hi, p_mid, _ = split3(prob)
            d_hi, d_mid, _ = split3(dscore)
            none = jnp.zeros((PAIRS, TOKENS), BF)
            self.d_parts = jnp.concatenate([d_hi, d_mid, none, none], axis=0)
            self.p_parts = jnp.concatenate([p_hi, p_mid, p_hi, none], axis=0)
            g_query = dot(self.d_parts[: 2 * PAIRS], self.key)
            g_att = dot(self.p_parts[: 2 * PAIRS], self.value)
            g_sum[0] += g_query[:PAIRS] + g_query[PAIRS:]
            g_sum[3] += g_att[:PAIRS] + g_att[PAIRS:]

        def finish_keys(self):
            more = dot(self.d_parts.T, shared["gq2"])
            self.d_key = (dk_ref[self.slot] + more).astype(BF)

        def finish_values(self):
            more = dot(self.p_parts.T, shared["gg3"])
            self.d_value = (dv_ref[self.slot] + more).astype(BF)

        def finish_weights(self):
            self.grads = jnp.concatenate([self.dq_t.T, self.d_key, self.d_value], axis=1)
            w_sum[:, : 3 * CH] += dot(cells_ref[self.u].T, self.grads)
            w_sum[:, 3 * CH :] += dot(self.out_t, up_ref[self.u])

        def finish_cells(self):
            delta_ref[self.u] = dot_nt(self.grads, w_qkv).astype(BF)

        def before(self):
            return [
                self.project_query,
                self.project_grad,
                self.project_global,
                self.project_transposed,
                self.project_rows,
            ]

        def after(self):
            return [
                self.finish_queries,
                self.finish_global,
                self.finish_keys,
                self.finish_values,
                self.finish_weights,
                self.finish_cells,
            ]

    cuboids = [Cuboid(u) for u in range(CUBOIDS)]
    for task in cuboids[0].before():
        task()
    order = [(c, h, q) for c in cuboids for h in range(HEADS) for q in range(0, TOKENS, QUERIES)]
    per_cuboid = len(order) // CUBOIDS
    ready = cuboids[0].scores(*order[0][1:])
    low = None
    for i, (cuboid, *step) in enumerate(order):
        place = i % per_cuboid
        u = cuboid.u
        if place == 0:
            early = cuboids[u + 1].before() if u + 1 < CUBOIDS else []
            late = cuboids[u - 1].after() if u > 0 else [global_operands, global_softmax]
        following = None
        if place + 1 == per_cuboid:
            for task in early + late:
                task()
        if i + 1 < len(order):
            following = order[i + 1][0].scores(*order[i + 1][1:])
        now = cuboid.softmax(*step, *ready)
        if low is not None:
            order[i - 1][0].products(*order[i - 1][1:], *low)
        if place > 0 and late:
            late.pop(0)()
        low = now
        if early:
            early.pop(0)()
        ready = following
    order[-1][0].products(*order[-1][1:], *low)
    for task in cuboids[-1].after():
        task()

    def outer(a, b):
        a = jnp.concatenate([a, jnp.zeros((CH - GLOBALS, CH), F32)], axis=0).T
        b = jnp.concatenate([b, jnp.zeros((CH - GLOBALS, CH), F32)], axis=0)
        return jnp.dot(a, b, precision=HIGHEST, preferred_element_type=F32)

    vec = jnp.zeros((GLOBALS, CH), F32)
    for i in range(4):
        g_part = head_diagonal(g_sum[i])
        if i < 3:
            total = w_sum[:, i * CH : (i + 1) * CH] + outer(vectors, g_part)
            hi, mid, low = split3(g_part)
            weight = weights_ref[i]
            vec += dot_nt(hi, weight) + dot_nt(mid, weight) + dot_nt(low, weight)
        else:
            total = w_sum[:, 3 * CH :] + outer(g_part, vup_ref[...])
        high = total.astype(BF)
        rows = pl.ds(i * CH, CH)
        part_ref[0, rows, :] = high
        low_ref[rows, :] = total - high.astype(F32)
    hi, mid, _ = split3(vec)
    vec_parts = jnp.concatenate(
        [hi.astype(F32), mid.astype(F32), jnp.zeros((CH - VEC_LANES, CH), F32)], axis=0
    ).T.astype(BF)
    row, slots = vec_slots(TOKENS)
    spread = (iota((TOKENS, CH), 0) // SPAN == iota((TOKENS, CH), 1)).astype(BF)
    part_ref[1] = jnp.where(slots, dot(spread, vec_parts), low_ref[...]).astype(BF)

    back = back_matrix()
    for i in range(PEERS // GROUP):
        tokens = pl.ds(i * group_tokens, group_tokens)
        rows = jnp.concatenate([delta_ref[u, tokens, :] for u in range(CUBOIDS)], axis=0)
        moved = dot(back, rows).astype(BF)
        msg_ref[pl.ds(i * GROUP, GROUP), 0:PEER_ROWS, :] = moved.reshape(GROUP, PEER_ROWS, CH)
    back = piece_matrix()
    for i in range(PEERS // PIECE_GROUP):
        tokens = pl.ds(i * CH, CH)
        rows = jnp.concatenate([part_ref[0, tokens, :], part_ref[1, tokens, :]], axis=0)
        moved = dot(back, rows).astype(BF)
        msg_ref[pl.ds(i * PIECE_GROUP, PIECE_GROUP), PEER_ROWS:, :] = moved.reshape(
            PIECE_GROUP, PIECE_ROWS, CH
        )


def sum_kernel(recv_ref, piece_ref):
    summed = jnp.sum(recv_ref[:, PEER_ROWS:, :].astype(F32), axis=0)
    row, slots = vec_slots(PIECE_ROWS)
    slots = slots & (row >= SPAN)
    vec = summed + pltpu.roll(summed, CH - GLOBALS, 1)
    low = jnp.where(slots, 0.0, summed)
    weight = summed[:SPAN] + low[SPAN:]
    high = weight.astype(BF).astype(F32)
    vec_high = vec.astype(BF).astype(F32)
    vec_low = pltpu.roll(vec - vec_high, GLOBALS, 1)
    vec = jnp.where(iota((PIECE_ROWS, CH), 1) < GLOBALS, vec_high, vec_low)
    piece = jnp.where(slots, vec, jnp.concatenate([high, weight - high], axis=0)).astype(BF)
    piece_ref[...] = jnp.broadcast_to(piece[None], piece_ref.shape)


def spread_kernel(recv_ref, weight_ref, vec_ref):
    rows = PIECE_GROUP * PIECE_ROWS
    row, slots = vec_slots(rows)
    slots = slots & (row % PIECE_ROWS >= SPAN)
    target, source = iota((CH, rows), 0), iota((CH, rows), 1)
    joins = (source // PIECE_ROWS == target // SPAN) & (source % SPAN == target % SPAN)
    joins = joins.astype(BF)
    target, source = iota((PIECE_GROUP, rows), 0), iota((PIECE_GROUP, rows), 1)
    last = (source == target * PIECE_ROWS + PIECE_ROWS - 1).astype(BF)
    vec = []
    for i in range(PEERS // PIECE_GROUP):
        piece = recv_ref[pl.ds(i * PIECE_GROUP, PIECE_GROUP)].reshape(rows, CH)
        vec.append(dot(last, piece))
        piece = jnp.where(slots, 0.0, piece.astype(F32)).astype(BF)
        weight_ref[i] = dot(joins, piece)
    vec = jnp.concatenate(vec, axis=0).T
    vec_ref[...] = vec[:GLOBALS] + vec[GLOBALS : 2 * GLOBALS]


def place_kernel(shift_hbm, recv_ref, out_ref, held, shift_ref, sem):
    copy = pltpu.make_async_copy(shift_hbm, shift_ref, sem)
    copy.start()
    for i in range(PEERS // GROUP):
        held[pl.ds(i * GROUP_ROWS, GROUP_ROWS), :] = recv_ref[
            pl.ds(i * GROUP, GROUP), 0:PEER_ROWS, :
        ].reshape(GROUP_ROWS, CH)
    held[CELLS_DEV:, :] = held[:WINDOW, :]
    copy.wait()
    offset = (CELLS_DEV - tile_offset(shift_ref)) % CELLS_DEV
    mover = shift_matrix(offset % 16)
    base = offset - offset % 16
    for i in range(CELLS_DEV // GROUP_ROWS):
        start = pl.multiple_of((base + i * GROUP_ROWS) % CELLS_DEV, 16)
        moved = dot(mover, held[pl.ds(start, WINDOW), :]).astype(BF)
        out_ref[pl.ds(i * GROUP_ROWS, GROUP_ROWS), :] = moved


VMEM = pl.BlockSpec(memory_space=pltpu.VMEM)
HBM = pl.BlockSpec(memory_space=pltpu.HBM)
PACK_PARAMS = pltpu.CompilerParams(vmem_limit_bytes=58_000_000)
PARAMS = pltpu.CompilerParams(vmem_limit_bytes=48 * 1024 * 1024)


def exchange(rows):
    return lax.all_to_all(rows, ("tile", "frame"), split_axis=0, concat_axis=0, tiled=True)


def body(cells, vectors, weights, cuboid_shift, cell_upstream, vector_upstream):
    message = pl.pallas_call(
        pack_kernel,
        out_shape=pltpu.VMEM((PEERS, MSG_ROWS, CH), BF),
        in_specs=[HBM] * 6,
        out_specs=VMEM,
        scratch_shapes=[
            pltpu.VMEM((CELLS_DEV + WINDOW, 2 * CH), BF),
            pltpu.VMEM((GLOBALS, CH), BF),
            pltpu.VMEM((4, CH, CH), BF),
            pltpu.VMEM((GLOBALS, CH), F32),
            pltpu.SMEM((1,), jnp.int32),
            pltpu.SemaphoreType.DMA((8,)),
        ],
        compiler_params=PACK_PARAMS,
        name="pack",
    )(cuboid_shift, cells[0], cell_upstream[0], vectors, weights, vector_upstream)
    received = exchange(message)
    message = pl.pallas_call(
        owner_kernel,
        out_shape=pltpu.VMEM((PEERS, PEER_ROWS + PIECE_ROWS, CH), BF),
        in_specs=[VMEM] * 4,
        out_specs=VMEM,
        scratch_shapes=[
            pltpu.VMEM((CUBOIDS, TOKENS, CH), BF),
            pltpu.VMEM((CUBOIDS, TOKENS, CH), BF),
            pltpu.VMEM((CUBOIDS, TOKENS, CH), BF),
            pltpu.VMEM((2, HEADS, CH, TOKENS), BF),
            pltpu.VMEM((2, HEADS, CH, TOKENS), BF),
            pltpu.VMEM((CH, 4 * CH), F32),
            pltpu.VMEM((4, PAIRS, CH), F32),
            pltpu.VMEM((2, TOKENS, CH), BF),
            pltpu.VMEM((TOKENS, CH), F32),
            pltpu.VMEM((2, TOKENS, CH), F32),
            pltpu.VMEM((2, TOKENS, CH), F32),
        ],
        compiler_params=PARAMS,
        name="owner",
    )(received, vectors, weights, vector_upstream)
    received = exchange(message)
    pieces = pl.pallas_call(
        sum_kernel,
        out_shape=pltpu.VMEM((PEERS, PIECE_ROWS, CH), BF),
        in_specs=[VMEM],
        out_specs=VMEM,
        compiler_params=PARAMS,
        name="sum_pieces",
    )(received)
    pieces = exchange(pieces)
    cell_grad = pl.pallas_call(
        place_kernel,
        out_shape=jax.ShapeDtypeStruct((CELLS_DEV, CH), BF),
        in_specs=[HBM, VMEM],
        out_specs=VMEM,
        scratch_shapes=[
            pltpu.VMEM((CELLS_DEV + WINDOW, CH), BF),
            pltpu.SMEM((1,), jnp.int32),
            pltpu.SemaphoreType.DMA,
        ],
        compiler_params=PARAMS,
        name="place",
    )(cuboid_shift, received)
    weight_grad, vector_grad = pl.pallas_call(
        spread_kernel,
        out_shape=[
            jax.ShapeDtypeStruct((4, CH, CH), F32),
            jax.ShapeDtypeStruct((GLOBALS, CH), F32),
        ],
        in_specs=[VMEM],
        out_specs=[VMEM, VMEM],
        compiler_params=PARAMS,
        name="spread",
    )(pieces)
    return cell_grad[None], weight_grad, vector_grad


def solution(mesh):
    in_specs = (P("frame", "tile", None), P(), P(), P(), P("frame", "tile", None), P())
    out_specs = (P("frame", "tile", None), P(), P())
    return jax.shard_map(body, mesh=mesh, in_specs=in_specs, out_specs=out_specs, check_vma=False)
```

```python
import math

import jax
import jax.numpy as jnp
from jax import lax
from jax.experimental import pallas as pl
from jax.experimental.pallas import tpu as pltpu
from jax.sharding import PartitionSpec as P

CH = 128
HEADS = 4
HDIM = 32
GLOBALS = 8
PAIRS = HEADS * GLOBALS
SPAN = 4
CELLS_DEV = 2048
PEERS = 128
PEER_ROWS = CELLS_DEV // PEERS
CUBOIDS = PEER_ROWS // SPAN
TOKENS = 512
QUERIES = 256
GROUP = 16
GROUP_ROWS = GROUP * PEER_ROWS
WINDOW = GROUP_ROWS + 16
MSG_ROWS = 40
PIECE_ROWS = 2 * SPAN
PIECE_GROUP = 32
VEC_LANES = 2 * GLOBALS
SCALE = HDIM**-0.5
LOG2E = math.log2(math.e)
BF = jnp.bfloat16
F32 = jnp.float32
NT = (((1,), (1,)), ((), ()))


def dot(a, b):
    return jnp.dot(a, b, preferred_element_type=F32)


def dot_nt(a, b):
    return lax.dot_general(a, b, NT, preferred_element_type=F32)


def iota(shape, axis):
    return lax.broadcasted_iota(jnp.int32, shape, axis)


def split3(x):
    hi = x.astype(BF)
    rest = x - hi.astype(F32)
    mid = rest.astype(BF)
    low = (rest - mid.astype(F32)).astype(BF)
    return hi, mid, low


def head_blocks(rows):
    head = iota((GLOBALS, CH), 1) // HDIM
    return jnp.concatenate([jnp.where(head == h, rows, 0.0) for h in range(HEADS)], axis=0)


def diagonal(first, second):
    zero = jnp.zeros((CH, CH), F32)
    rows = [jnp.concatenate([first, zero], axis=1), jnp.concatenate([zero, second], axis=1)]
    return jnp.concatenate(rows, axis=0).astype(BF)


def head_diagonal(blocks):
    head = iota((GLOBALS, CH), 1) // HDIM
    total = jnp.zeros((GLOBALS, CH), F32)
    for h in range(HEADS):
        total += jnp.where(head == h, blocks[h * GLOBALS : (h + 1) * GLOBALS], 0.0)
    return total


def global_rows(vectors, weight):
    return dot(vectors.astype(BF), weight).astype(BF).astype(F32)


def global_upstream(vector_upstream, w_out):
    hi, mid, low = split3(vector_upstream)
    return dot_nt(hi, w_out) + dot_nt(mid, w_out) + dot_nt(low, w_out)


def tile_offset(shift_ref):
    return (shift_ref[0] * (lax.axis_index("tile") + 1)) % CELLS_DEV


def shift_matrix(step, rows, window):
    return (iota((rows, window), 1) == iota((rows, window), 0) + step).astype(BF)


def pack_kernel(
    shift_hbm,
    cells_hbm,
    up_hbm,
    vectors_hbm,
    weights_hbm,
    vup_hbm,
    msg_ref,
    held,
    vectors_ref,
    weights_ref,
    vup_ref,
    shift_ref,
    sems,
):
    whole, wrap = pl.ds(0, CELLS_DEV), pl.ds(CELLS_DEV, WINDOW)
    left, right = pl.ds(0, CH), pl.ds(CH, CH)
    copies = [
        pltpu.make_async_copy(source, target, sems.at[i])
        for i, (source, target) in enumerate(
            [
                (vectors_hbm, vectors_ref),
                (weights_hbm, weights_ref),
                (vup_hbm, vup_ref),
                (cells_hbm, held.at[whole, left]),
                (cells_hbm.at[pl.ds(0, WINDOW)], held.at[wrap, left]),
                (up_hbm, held.at[whole, right]),
                (up_hbm.at[pl.ds(0, WINDOW)], held.at[wrap, right]),
                (shift_hbm, shift_ref),
            ]
        )
    ]
    for copy in copies:
        copy.start()
    for copy in copies[:5]:
        copy.wait()
    vectors = vectors_ref[...].astype(F32)
    cells = held[:CELLS_DEV, :CH]
    query = head_blocks(global_rows(vectors, weights_ref[0])).astype(BF)
    upstream = head_blocks(global_upstream(vup_ref[...], weights_ref[3]))
    up_parts = jnp.concatenate([part.astype(F32) for part in split3(upstream)], axis=0).astype(BF)
    w_kv = jnp.concatenate([weights_ref[1], weights_ref[2]], axis=1)
    key_value = dot(cells, w_kv).astype(BF)
    score = dot_nt(query, key_value[:, :CH]) * SCALE
    dprob = dot_nt(up_parts, key_value[:, CH:])
    dprob = dprob[:PAIRS] + dprob[PAIRS : 2 * PAIRS] + dprob[2 * PAIRS :]
    top = jnp.max(score, axis=1, keepdims=True)
    weight = jnp.exp(score - top)
    total = jnp.sum(weight, axis=1, keepdims=True)
    inner = jnp.sum(weight * dprob, axis=1, keepdims=True)
    lane = iota((PAIRS, CH), 1)
    stats = jnp.where(lane == 0, top, jnp.where(lane == 1, total, jnp.where(lane == 2, inner, 0.0)))
    parts = [part.astype(F32) for part in split3(stats)] + [jnp.zeros((PAIRS, CH), F32)]
    rows = jnp.concatenate(parts, axis=0).T[:GLOBALS].astype(BF)
    msg_ref[:, 2 * PEER_ROWS :, :] = jnp.broadcast_to(rows[None], (PEERS, GLOBALS, CH))
    for copy in copies[5:]:
        copy.wait()
    offset = tile_offset(shift_ref)
    base = offset - offset % 16
    mover = shift_matrix(offset % 16, GROUP_ROWS - 16, GROUP_ROWS)
    for first in range(0, PEERS, GROUP - 1):
        count = min(GROUP - 1, PEERS - first)
        start = pl.multiple_of((base + first * PEER_ROWS) % CELLS_DEV, 16)
        rows = held[pl.ds(start, GROUP_ROWS), :]
        moved = dot(mover[: count * PEER_ROWS], rows).astype(BF)
        peers = pl.ds(first, count)
        msg_ref[peers, 0:PEER_ROWS, :] = moved[:, :CH].reshape(count, PEER_ROWS, CH)
        msg_ref[peers, PEER_ROWS : 2 * PEER_ROWS, :] = moved[:, CH:].reshape(count, PEER_ROWS, CH)


def regroup_matrix():
    row = iota((GROUP_ROWS, GROUP_ROWS), 0)
    column = iota((GROUP_ROWS, GROUP_ROWS), 1)
    source = (row // SPAN) % GROUP * PEER_ROWS + row // (GROUP * SPAN) * SPAN + row % SPAN
    return (column == source).astype(BF)


def piece_matrix():
    rows = PIECE_GROUP * PIECE_ROWS
    row = iota((rows, rows), 0)
    source = row // SPAN % 2 * CH + row // PIECE_ROWS * SPAN + row % SPAN
    return (iota((rows, rows), 1) == source).astype(BF)


def vec_slots(rows):
    row, lane = iota((rows, CH), 0), iota((rows, CH), 1)
    return row, (row % SPAN == SPAN - 1) & (lane < VEC_LANES)


def back_matrix():
    row = iota((GROUP_ROWS, GROUP_ROWS), 0)
    column = iota((GROUP_ROWS, GROUP_ROWS), 1)
    source = (row // SPAN) % CUBOIDS * (GROUP * SPAN) + row // PEER_ROWS * SPAN + row % SPAN
    return (column == source).astype(BF)


def owner_kernel(
    recv_ref,
    vectors_ref,
    weights_ref,
    vup_ref,
    msg_ref,
    cells_ref,
    up_ref,
    delta_ref,
    query_m,
    grad_m,
    w_sum,
    g_sum,
    part_ref,
    low_ref,
    dkv_ref,
):
    group_tokens = GROUP * SPAN
    mover = regroup_matrix()
    for i in range(PEERS // GROUP):
        peers = pl.ds(i * GROUP, GROUP)
        rows = jnp.concatenate(
            [
                recv_ref[peers, 0:PEER_ROWS, :].reshape(GROUP_ROWS, CH),
                recv_ref[peers, PEER_ROWS : 2 * PEER_ROWS, :].reshape(GROUP_ROWS, CH),
            ],
            axis=1,
        )
        moved = dot(mover, rows).astype(BF)
        for u in range(CUBOIDS):
            piece = moved[u * group_tokens : (u + 1) * group_tokens]
            cells_ref[u, pl.ds(i * group_tokens, group_tokens), :] = piece[:, :CH]
            up_ref[u, pl.ds(i * group_tokens, group_tokens), :] = piece[:, CH:]

    vectors = vectors_ref[...].astype(F32)
    w_q, w_k, w_v, w_o = (weights_ref[i] for i in range(4))
    w_kv = jnp.concatenate([w_k, w_v], axis=1)
    w_qkv = jnp.concatenate([w_q, w_kv], axis=1)
    w_q_t = w_q.T
    gk = head_blocks(global_rows(vectors, w_k))
    gv = head_blocks(global_rows(vectors, w_v))
    gk_b, gv_b = gk.astype(BF), gv.astype(BF)
    zero = jnp.zeros((PAIRS, CH), F32)
    shared = {}

    def global_operands():
        gq = head_blocks(global_rows(vectors, w_q))
        gg = head_blocks(global_upstream(vup_ref[...], w_o))
        gg3 = [part.astype(F32) for part in split3(gg)]
        shared["gq_b"] = gq.astype(BF)
        for name, blocks in (("gk_t", gk), ("gv_t", gv)):
            wide = jnp.concatenate([blocks, zero, zero, zero], axis=0)
            shared[name] = wide.T[:, :PAIRS].astype(BF)
        shared["gg_parts"] = jnp.concatenate(gg3, axis=0).astype(BF)
        shared["more"] = diagonal(
            jnp.concatenate([gq, gq, zero, zero], axis=0),
            jnp.concatenate([gg3[0], gg3[0], gg3[1], zero], axis=0),
        )

    def global_softmax():
        stats = recv_ref[:, 2 * PEER_ROWS :, :].astype(F32).reshape(PEERS * GLOBALS, CH)
        stats = stats + pltpu.roll(stats, CH - PAIRS, 1) + pltpu.roll(stats, CH - 2 * PAIRS, 1)
        stats = stats.reshape(PEERS, GLOBALS, CH)
        tops = stats[:, 0:1, :]
        top = jnp.max(tops, axis=0)
        summed = jnp.sum(jnp.exp(tops - top[None]) * stats, axis=0)
        lanes = jnp.where(iota((GLOBALS, CH), 0) == 0, top, summed)
        columns = jnp.concatenate([lanes, jnp.zeros((CH - GLOBALS, CH), F32)], axis=0).T
        shared["g_top"] = columns[:PAIRS, 0:1]
        shared["g_inv"] = 1.0 / columns[:PAIRS, 1:2]
        shared["g_row"] = columns[:PAIRS, 2:3] * shared["g_inv"]

    def clear(slot):
        query_m[slot] = jnp.zeros(query_m.shape[1:], BF)
        grad_m[slot] = jnp.zeros(grad_m.shape[1:], BF)

    clear(0)

    def heads(h):
        return slice(h * HDIM, (h + 1) * HDIM)

    class Cuboid:
        def __init__(self, u):
            self.u, self.slot = u, u % 2
            self.low = []
            self.rows = {n: [[] for _ in range(HEADS)] for n in ("p", "ds", "out", "dq")}

        def project_query(self):
            cells = cells_ref[self.u]
            self.query_t = dot_nt(w_q_t, cells).astype(BF)
            for h in range(HEADS):
                query_m[self.slot, h, heads(h), :] = self.query_t[heads(h)]

        def project_grad(self):
            self.grad_t = dot_nt(w_o, up_ref[self.u]).astype(BF)
            for h in range(HEADS):
                grad_m[self.slot, h, heads(h), :] = self.grad_t[heads(h)]

        def project_keys(self):
            self.key_value = dot(cells_ref[self.u], w_kv).astype(BF)
            self.key, self.value = self.key_value[:, :CH], self.key_value[:, CH:]

        def project_global(self):
            self.s_global = dot(gk_b, self.query_t)
            self.d_global = dot(gv_b, self.grad_t)

        def project_transposed(self):
            self.key_t = self.key.T
            self.value_t = self.value.T

        def project_rows(self):
            self.query = self.query_t.T
            self.grad = self.grad_t.T

        def scores(self, h, q):
            columns = pl.ds(q, QUERIES)
            return (
                dot(self.key, query_m[self.slot, h, :, columns]),
                dot(self.value, grad_m[self.slot, h, :, columns]),
            )

        def softmax(self, h, q, score, dprob):
            rows = slice(h * GLOBALS, (h + 1) * GLOBALS)
            s_glob = self.s_global[rows, q : q + QUERIES]
            d_glob = self.d_global[rows, q : q + QUERIES]
            top = jnp.maximum(
                jnp.max(score, axis=0, keepdims=True), jnp.max(s_glob, axis=0, keepdims=True)
            )
            e_local = jnp.exp2((score - top) * (SCALE * LOG2E))
            e_global = jnp.exp2((s_glob - top) * (SCALE * LOG2E))
            total = jnp.sum(e_local, axis=0, keepdims=True) + jnp.sum(
                e_global, axis=0, keepdims=True
            )
            inv = 1.0 / total
            p_local = e_local * inv
            p_global = e_global * inv
            inner = jnp.sum(p_local * dprob, axis=0, keepdims=True) + jnp.sum(
                p_global * d_glob, axis=0, keepdims=True
            )
            self.rows["p"][h].append(p_global)
            self.rows["ds"][h].append(p_global * (d_glob - inner) * SCALE)
            return p_local.astype(BF), (p_local * (dprob - inner) * SCALE).astype(BF)

        def products(self, h, q, p_low, ds_low):
            part = heads(h)
            self.rows["out"][h].append(dot(self.value_t[part], p_low))
            self.rows["dq"][h].append(dot(self.key_t[part], ds_low))
            self.low.append((p_low, ds_low))
            if q + QUERIES == TOKENS:
                p_low, ds_low = (jnp.concatenate(x, axis=1) for x in zip(*self.low))
                self.low = []
                dkv_ref[self.slot, :, part] = dot(ds_low, self.query)[:, part]
                lanes = slice(CH + part.start, CH + part.stop)
                dkv_ref[self.slot, :, lanes] = dot(p_low, self.grad)[:, part]

        def add(self, ref, where, value):
            ref[where] = value if self.u == 0 else ref[where] + value

        def whole(self, name):
            rows = [jnp.concatenate(row, axis=1) for row in self.rows[name]]
            return jnp.concatenate(rows, axis=0)

        def finish_queries(self):
            p_rows, ds_rows = self.whole("p").astype(BF), self.whole("ds").astype(BF)
            self.out_t = (self.whole("out") + dot(shared["gv_t"], p_rows)).astype(BF)
            self.dq_t = (self.whole("dq") + dot(shared["gk_t"], ds_rows)).astype(BF)
            rows = jnp.concatenate([ds_rows, p_rows], axis=0)
            g_both = dot(rows, jnp.concatenate([self.query, self.grad], axis=1))
            self.add(g_sum, 1, g_both[:PAIRS, :CH])
            self.add(g_sum, 2, g_both[PAIRS:, CH:])

        def finish_global(self):
            score = dot(shared["gq_b"], self.key_t) * SCALE
            prob = jnp.exp(score - shared["g_top"]) * shared["g_inv"]
            dprob = dot(shared["gg_parts"], self.value_t)
            dprob = dprob[:PAIRS] + dprob[PAIRS : 2 * PAIRS] + dprob[2 * PAIRS :]
            dscore = prob * (dprob - shared["g_row"]) * SCALE
            p_hi, p_mid, _ = split3(prob)
            d_hi, d_mid, _ = split3(dscore)
            none = jnp.zeros((PAIRS, TOKENS), BF)
            self.parts = jnp.concatenate(
                [d_hi, d_mid, none, none, p_hi, p_mid, p_hi, none], axis=0
            )
            g_both = dot(
                jnp.concatenate([d_hi, d_mid, p_hi, p_mid], axis=0), self.key_value
            )
            self.add(g_sum, 0, g_both[:PAIRS, :CH] + g_both[PAIRS : 2 * PAIRS, :CH])
            self.add(g_sum, 3, g_both[2 * PAIRS : 3 * PAIRS, CH:] + g_both[3 * PAIRS :, CH:])

        def finish_keys(self):
            more = dot(self.parts.T, shared["more"])
            self.d_key_value = (dkv_ref[self.slot] + more).astype(BF)

        def finish_weights(self):
            self.grads = jnp.concatenate([self.dq_t.T, self.d_key_value], axis=1)
            everything = slice(None)
            first, last = slice(0, 3 * CH), slice(3 * CH, 4 * CH)
            self.add(w_sum, (everything, first), dot(cells_ref[self.u].T, self.grads))
            self.add(w_sum, (everything, last), dot(self.out_t, up_ref[self.u]))

        def finish_cells(self):
            delta_ref[self.u] = dot_nt(self.grads, w_qkv).astype(BF)

        def before(self):
            return [
                self.project_query,
                self.project_grad,
                self.project_keys,
                self.project_global,
                self.project_transposed,
                self.project_rows,
            ]

        def after(self):
            return [
                self.finish_queries,
                self.finish_global,
                self.finish_keys,
                self.finish_weights,
                self.finish_cells,
            ]

    cuboids = [Cuboid(u) for u in range(CUBOIDS)]
    for task in cuboids[0].before():
        task()
    order = [(c, h, q) for c in cuboids for h in range(HEADS) for q in range(0, TOKENS, QUERIES)]
    per_cuboid = len(order) // CUBOIDS
    ready = cuboids[0].scores(*order[0][1:])
    low = None
    for i, (cuboid, *step) in enumerate(order):
        place = i % per_cuboid
        u = cuboid.u
        if place == 0:
            early = cuboids[u + 1].before() if u + 1 < CUBOIDS else []
            if u == 0:
                early.insert(0, lambda: clear(1))
            late = cuboids[u - 1].after() if u > 0 else [global_operands, global_softmax]
        following = None
        if place + 1 == per_cuboid:
            for task in early + late:
                task()
        if i + 1 < len(order):
            following = order[i + 1][0].scores(*order[i + 1][1:])
        now = cuboid.softmax(*step, *ready)
        if low is not None:
            order[i - 1][0].products(*order[i - 1][1:], *low)
        if place > 0 and late:
            late.pop(0)()
        low = now
        if early:
            early.pop(0)()
        ready = following
    order[-1][0].products(*order[-1][1:], *low)
    for task in cuboids[-1].after():
        task()

    def tall(pieces):
        rows = jnp.concatenate(pieces, axis=0)
        return jnp.concatenate([rows, jnp.zeros((CH - rows.shape[0], CH), F32)], axis=0)

    def parts_of(rows):
        return [part.astype(F32) for part in split3(rows)]

    g_parts = [parts_of(head_diagonal(g_sum[i])) for i in range(3)]
    g_tall = jnp.concatenate([tall(parts) for parts in g_parts], axis=1).astype(BF)
    w_sum[:, : 3 * CH] += dot(tall([vectors] * 3).T.astype(BF), g_tall)
    a_hi, a_mid, a_low = parts_of(head_diagonal(g_sum[3]))
    u_hi, u_mid, u_low = parts_of(vup_ref[...])
    left = tall([a_hi, a_hi, a_hi, a_mid, a_mid, a_low]).T.astype(BF)
    w_sum[:, 3 * CH :] += dot(left, tall([u_hi, u_mid, u_low, u_hi, u_mid, u_hi]).astype(BF))
    vec = dot_nt(g_tall[: 4 * GLOBALS], w_qkv)
    vec = vec[:GLOBALS] + vec[GLOBALS : 2 * GLOBALS] + vec[2 * GLOBALS : 3 * GLOBALS]
    for i in range(4):
        total = w_sum[:, i * CH : (i + 1) * CH]
        high = total.astype(BF)
        rows = pl.ds(i * CH, CH)
        part_ref[0, rows, :] = high
        low_ref[rows, :] = total - high.astype(F32)
    hi, mid, _ = split3(vec)
    vec_parts = jnp.concatenate(
        [hi.astype(F32), mid.astype(F32), jnp.zeros((CH - VEC_LANES, CH), F32)], axis=0
    ).T.astype(BF)
    row, slots = vec_slots(TOKENS)
    spread = (iota((TOKENS, CH), 0) // SPAN == iota((TOKENS, CH), 1)).astype(BF)
    part_ref[1] = jnp.where(slots, dot(spread, vec_parts), low_ref[...]).astype(BF)

    back = back_matrix()
    for i in range(PEERS // GROUP):
        tokens = pl.ds(i * group_tokens, group_tokens)
        rows = jnp.concatenate([delta_ref[u, tokens, :] for u in range(CUBOIDS)], axis=0)
        moved = dot(back, rows).astype(BF)
        msg_ref[pl.ds(i * GROUP, GROUP), 0:PEER_ROWS, :] = moved.reshape(GROUP, PEER_ROWS, CH)
    back = piece_matrix()
    for i in range(PEERS // PIECE_GROUP):
        tokens = pl.ds(i * CH, CH)
        rows = jnp.concatenate([part_ref[0, tokens, :], part_ref[1, tokens, :]], axis=0)
        moved = dot(back, rows).astype(BF)
        msg_ref[pl.ds(i * PIECE_GROUP, PIECE_GROUP), PEER_ROWS:, :] = moved.reshape(
            PIECE_GROUP, PIECE_ROWS, CH
        )


def sum_kernel(recv_ref, piece_ref):
    summed = jnp.sum(recv_ref[:, PEER_ROWS:, :].astype(F32), axis=0)
    row, slots = vec_slots(PIECE_ROWS)
    slots = slots & (row >= SPAN)
    vec = summed + pltpu.roll(summed, CH - GLOBALS, 1)
    low = jnp.where(slots, 0.0, summed)
    weight = summed[:SPAN] + low[SPAN:]
    high = weight.astype(BF).astype(F32)
    vec_high = vec.astype(BF).astype(F32)
    vec_low = pltpu.roll(vec - vec_high, GLOBALS, 1)
    vec = jnp.where(iota((PIECE_ROWS, CH), 1) < GLOBALS, vec_high, vec_low)
    piece = jnp.where(slots, vec, jnp.concatenate([high, weight - high], axis=0)).astype(BF)
    piece_ref[...] = jnp.broadcast_to(piece[None], piece_ref.shape)


def spread_kernel(recv_ref, weight_ref, vec_ref):
    rows = PIECE_GROUP * PIECE_ROWS
    row, slots = vec_slots(rows)
    slots = slots & (row % PIECE_ROWS >= SPAN)
    target, source = iota((CH, rows), 0), iota((CH, rows), 1)
    joins = (source // PIECE_ROWS == target // SPAN) & (source % SPAN == target % SPAN)
    joins = joins.astype(BF)
    target, source = iota((PIECE_GROUP, rows), 0), iota((PIECE_GROUP, rows), 1)
    last = (source == target * PIECE_ROWS + PIECE_ROWS - 1).astype(BF)
    vec = []
    for i in range(PEERS // PIECE_GROUP):
        piece = recv_ref[pl.ds(i * PIECE_GROUP, PIECE_GROUP)].reshape(rows, CH)
        vec.append(dot(last, piece))
        piece = jnp.where(slots, 0.0, piece.astype(F32)).astype(BF)
        weight_ref[i] = dot(joins, piece)
    vec = jnp.concatenate(vec, axis=0).T
    vec_ref[...] = vec[:GLOBALS] + vec[GLOBALS : 2 * GLOBALS]


def place_kernel(shift_hbm, recv_ref, out_ref, held, shift_ref, sem):
    copy = pltpu.make_async_copy(shift_hbm, shift_ref, sem)
    copy.start()
    for i in range(PEERS // GROUP):
        held[pl.ds(i * GROUP_ROWS, GROUP_ROWS), :] = recv_ref[
            pl.ds(i * GROUP, GROUP), 0:PEER_ROWS, :
        ].reshape(GROUP_ROWS, CH)
    held[CELLS_DEV:, :] = held[:WINDOW, :]
    copy.wait()
    offset = (CELLS_DEV - tile_offset(shift_ref)) % CELLS_DEV
    mover = shift_matrix(offset % 16, GROUP_ROWS, WINDOW)
    base = offset - offset % 16
    for i in range(CELLS_DEV // GROUP_ROWS):
        start = pl.multiple_of((base + i * GROUP_ROWS) % CELLS_DEV, 16)
        moved = dot(mover, held[pl.ds(start, WINDOW), :]).astype(BF)
        out_ref[pl.ds(i * GROUP_ROWS, GROUP_ROWS), :] = moved


VMEM = pl.BlockSpec(memory_space=pltpu.VMEM)
HBM = pl.BlockSpec(memory_space=pltpu.HBM)
PACK_PARAMS = pltpu.CompilerParams(vmem_limit_bytes=58_000_000)
PARAMS = pltpu.CompilerParams(vmem_limit_bytes=48 * 1024 * 1024)


def exchange(rows):
    return lax.all_to_all(rows, ("tile", "frame"), split_axis=0, concat_axis=0, tiled=True)


def body(cells, vectors, weights, cuboid_shift, cell_upstream, vector_upstream):
    message = pl.pallas_call(
        pack_kernel,
        out_shape=pltpu.VMEM((PEERS, MSG_ROWS, CH), BF),
        in_specs=[HBM] * 6,
        out_specs=VMEM,
        scratch_shapes=[
            pltpu.VMEM((CELLS_DEV + WINDOW, 2 * CH), BF),
            pltpu.VMEM((GLOBALS, CH), BF),
            pltpu.VMEM((4, CH, CH), BF),
            pltpu.VMEM((GLOBALS, CH), F32),
            pltpu.SMEM((1,), jnp.int32),
            pltpu.SemaphoreType.DMA((8,)),
        ],
        compiler_params=PACK_PARAMS,
        name="pack",
    )(cuboid_shift, cells[0], cell_upstream[0], vectors, weights, vector_upstream)
    received = exchange(message)
    message = pl.pallas_call(
        owner_kernel,
        out_shape=pltpu.VMEM((PEERS, PEER_ROWS + PIECE_ROWS, CH), BF),
        in_specs=[VMEM] * 4,
        out_specs=VMEM,
        scratch_shapes=[
            pltpu.VMEM((CUBOIDS, TOKENS, CH), BF),
            pltpu.VMEM((CUBOIDS, TOKENS, CH), BF),
            pltpu.VMEM((CUBOIDS, TOKENS, CH), BF),
            pltpu.VMEM((2, HEADS, CH, TOKENS), BF),
            pltpu.VMEM((2, HEADS, CH, TOKENS), BF),
            pltpu.VMEM((CH, 4 * CH), F32),
            pltpu.VMEM((4, PAIRS, CH), F32),
            pltpu.VMEM((2, TOKENS, CH), BF),
            pltpu.VMEM((TOKENS, CH), F32),
            pltpu.VMEM((2, TOKENS, 2 * CH), F32),
        ],
        compiler_params=PARAMS,
        name="owner",
    )(received, vectors, weights, vector_upstream)
    received = exchange(message)
    pieces = pl.pallas_call(
        sum_kernel,
        out_shape=pltpu.VMEM((PEERS, PIECE_ROWS, CH), BF),
        in_specs=[VMEM],
        out_specs=VMEM,
        compiler_params=PARAMS,
        name="sum_pieces",
    )(received)
    pieces = exchange(pieces)
    cell_grad = pl.pallas_call(
        place_kernel,
        out_shape=jax.ShapeDtypeStruct((CELLS_DEV, CH), BF),
        in_specs=[HBM, VMEM],
        out_specs=VMEM,
        scratch_shapes=[
            pltpu.VMEM((CELLS_DEV + WINDOW, CH), BF),
            pltpu.SMEM((1,), jnp.int32),
            pltpu.SemaphoreType.DMA,
        ],
        compiler_params=PARAMS,
        name="place",
    )(cuboid_shift, received)
    weight_grad, vector_grad = pl.pallas_call(
        spread_kernel,
        out_shape=[
            jax.ShapeDtypeStruct((4, CH, CH), F32),
            jax.ShapeDtypeStruct((GLOBALS, CH), F32),
        ],
        in_specs=[VMEM],
        out_specs=[VMEM, VMEM],
        compiler_params=PARAMS,
        name="spread",
    )(pieces)
    return cell_grad[None], weight_grad, vector_grad


def solution(mesh):
    in_specs = (P("frame", "tile", None), P(), P(), P(), P("frame", "tile", None), P())
    out_specs = (P("frame", "tile", None), P(), P())
    return jax.shard_map(body, mesh=mesh, in_specs=in_specs, out_specs=out_specs, check_vma=False)
```

```python
import math

import jax
import jax.numpy as jnp
from jax import lax
from jax.experimental import pallas as pl
from jax.experimental.pallas import tpu as pltpu
from jax.sharding import PartitionSpec as P

CH = 128
HEADS = 4
HDIM = 32
GLOBALS = 8
PAIRS = HEADS * GLOBALS
SPAN = 4
CELLS_DEV = 2048
PEERS = 128
PEER_ROWS = CELLS_DEV // PEERS
CUBOIDS = PEER_ROWS // SPAN
TOKENS = 512
QUERIES = 256
GROUP = 16
GROUP_ROWS = GROUP * PEER_ROWS
WINDOW = GROUP_ROWS + 16
MSG_SPANS = 9
PIECE_ROWS = 2 * SPAN
PIECE_GROUP = 32
VEC_LANES = 2 * GLOBALS
SCALE = HDIM**-0.5
LOG2E = math.log2(math.e)
BF = jnp.bfloat16
F32 = jnp.float32
NT = (((1,), (1,)), ((), ()))


def dot(a, b):
    return jnp.dot(a, b, preferred_element_type=F32)


def dot_nt(a, b):
    return lax.dot_general(a, b, NT, preferred_element_type=F32)


def iota(shape, axis):
    return lax.broadcasted_iota(jnp.int32, shape, axis)


def split3(x):
    hi = x.astype(BF)
    rest = x - hi.astype(F32)
    mid = rest.astype(BF)
    low = (rest - mid.astype(F32)).astype(BF)
    return hi, mid, low


def head_blocks(rows):
    head = iota((GLOBALS, CH), 1) // HDIM
    return jnp.concatenate([jnp.where(head == h, rows, 0.0) for h in range(HEADS)], axis=0)


def diagonal(first, second):
    zero = jnp.zeros((CH, CH), F32)
    rows = [jnp.concatenate([first, zero], axis=1), jnp.concatenate([zero, second], axis=1)]
    return jnp.concatenate(rows, axis=0).astype(BF)


def head_diagonal(blocks):
    head = iota((GLOBALS, CH), 1) // HDIM
    total = jnp.zeros((GLOBALS, CH), F32)
    for h in range(HEADS):
        total += jnp.where(head == h, blocks[h * GLOBALS : (h + 1) * GLOBALS], 0.0)
    return total


def global_rows(vectors, weight):
    return dot(vectors.astype(BF), weight).astype(BF).astype(F32)


def global_upstream(vector_upstream, w_out):
    hi, mid, low = split3(vector_upstream)
    return dot_nt(hi, w_out) + dot_nt(mid, w_out) + dot_nt(low, w_out)


def tile_offset(shift_ref):
    return (shift_ref[0] * (lax.axis_index("tile") + 1)) % CELLS_DEV


def shift_matrix(step, rows, window):
    return (iota((rows, window), 1) == iota((rows, window), 0) + step).astype(BF)


def pack_kernel(
    shift_hbm,
    cells_hbm,
    up_hbm,
    vectors_hbm,
    weights_hbm,
    vup_hbm,
    msg_ref,
    held,
    vectors_ref,
    weights_ref,
    vup_ref,
    shift_ref,
    sems,
):
    whole, wrap = pl.ds(0, CELLS_DEV), pl.ds(CELLS_DEV, WINDOW)
    left, right = pl.ds(0, CH), pl.ds(CH, CH)
    copies = [
        pltpu.make_async_copy(source, target, sems.at[i])
        for i, (source, target) in enumerate(
            [
                (vectors_hbm, vectors_ref),
                (weights_hbm, weights_ref),
                (vup_hbm, vup_ref),
                (cells_hbm, held.at[whole, left]),
                (cells_hbm.at[pl.ds(0, WINDOW)], held.at[wrap, left]),
                (up_hbm, held.at[whole, right]),
                (up_hbm.at[pl.ds(0, WINDOW)], held.at[wrap, right]),
                (shift_hbm, shift_ref),
            ]
        )
    ]
    for copy in copies:
        copy.start()
    for copy in copies[:5]:
        copy.wait()
    vectors = vectors_ref[...].astype(F32)
    cells = held[:CELLS_DEV, :CH]
    query = head_blocks(global_rows(vectors, weights_ref[0])).astype(BF)
    upstream = head_blocks(global_upstream(vup_ref[...], weights_ref[3]))
    up_parts = jnp.concatenate([part.astype(F32) for part in split3(upstream)], axis=0).astype(BF)
    w_kv = jnp.concatenate([weights_ref[1], weights_ref[2]], axis=1)
    key_value = dot(cells, w_kv).astype(BF)
    score = dot_nt(query, key_value[:, :CH]) * SCALE
    dprob = dot_nt(up_parts, key_value[:, CH:])
    dprob = dprob[:PAIRS] + dprob[PAIRS : 2 * PAIRS] + dprob[2 * PAIRS :]
    top = jnp.max(score, axis=1, keepdims=True)
    weight = jnp.exp(score - top)
    total = jnp.sum(weight, axis=1, keepdims=True)
    inner = jnp.sum(weight * dprob, axis=1, keepdims=True)
    lane = iota((PAIRS, CH), 1)
    stats = jnp.where(lane == 0, top, jnp.where(lane == 1, total, jnp.where(lane == 2, inner, 0.0)))
    parts = [part.astype(F32) for part in split3(stats)] + [jnp.zeros((PAIRS, CH), F32)]
    rows = jnp.concatenate(parts, axis=0).T[:GLOBALS].astype(BF)
    msg_ref[:, 2 * CUBOIDS] = jnp.broadcast_to(rows[None, :SPAN], (PEERS, SPAN, CH))
    for copy in copies[5:]:
        copy.wait()
    offset = tile_offset(shift_ref)
    base = offset - offset % 16
    mover = shift_matrix(offset % 16, GROUP_ROWS - 16, GROUP_ROWS)
    for first in range(0, PEERS, GROUP - 1):
        count = min(GROUP - 1, PEERS - first)
        start = pl.multiple_of((base + first * PEER_ROWS) % CELLS_DEV, 16)
        rows = held[pl.ds(start, GROUP_ROWS), :]
        moved = dot(mover[: count * PEER_ROWS], rows).astype(BF)
        peers = pl.ds(first, count)
        shape = (count, CUBOIDS, SPAN, CH)
        msg_ref[peers, 0:CUBOIDS] = moved[:, :CH].reshape(shape)
        msg_ref[peers, CUBOIDS : 2 * CUBOIDS] = moved[:, CH:].reshape(shape)


def piece_matrix():
    rows = PIECE_GROUP * PIECE_ROWS
    row = iota((rows, rows), 0)
    source = row // SPAN % 2 * CH + row // PIECE_ROWS * SPAN + row % SPAN
    return (iota((rows, rows), 1) == source).astype(BF)


def vec_slots(rows):
    row, lane = iota((rows, CH), 0), iota((rows, CH), 1)
    return row, (row % SPAN == SPAN - 1) & (lane < VEC_LANES)


def back_matrix():
    row = iota((GROUP_ROWS, GROUP_ROWS), 0)
    column = iota((GROUP_ROWS, GROUP_ROWS), 1)
    source = (row // SPAN) % CUBOIDS * (GROUP * SPAN) + row // PEER_ROWS * SPAN + row % SPAN
    return (column == source).astype(BF)


def owner_kernel(
    recv_ref,
    vectors_ref,
    weights_ref,
    vup_ref,
    msg_ref,
    cells_ref,
    up_ref,
    delta_ref,
    query_m,
    grad_m,
    w_sum,
    g_sum,
    part_ref,
    low_ref,
    dkv_ref,
):
    group_tokens = GROUP * SPAN
    for u in range(CUBOIDS):
        cells_ref[u] = recv_ref[:, u].reshape(TOKENS, CH)
        up_ref[u] = recv_ref[:, CUBOIDS + u].reshape(TOKENS, CH)

    vectors = vectors_ref[...].astype(F32)
    w_q, w_k, w_v, w_o = (weights_ref[i] for i in range(4))
    w_kv = jnp.concatenate([w_k, w_v], axis=1)
    w_qkv = jnp.concatenate([w_q, w_kv], axis=1)
    w_q_t = w_q.T
    gk = head_blocks(global_rows(vectors, w_k))
    gv = head_blocks(global_rows(vectors, w_v))
    gk_b, gv_b = gk.astype(BF), gv.astype(BF)
    zero = jnp.zeros((PAIRS, CH), F32)
    shared = {}

    def global_operands():
        gq = head_blocks(global_rows(vectors, w_q))
        gg = head_blocks(global_upstream(vup_ref[...], w_o))
        gg3 = [part.astype(F32) for part in split3(gg)]
        shared["gq_b"] = gq.astype(BF)
        for name, blocks in (("gk_t", gk), ("gv_t", gv)):
            wide = jnp.concatenate([blocks, zero, zero, zero], axis=0)
            shared[name] = wide.T[:, :PAIRS].astype(BF)
        shared["gg_parts"] = jnp.concatenate(gg3, axis=0).astype(BF)
        shared["more"] = diagonal(
            jnp.concatenate([gq, gq, zero, zero], axis=0),
            jnp.concatenate([gg3[0], gg3[0], gg3[1], zero], axis=0),
        )

    def global_softmax():
        stats = recv_ref[:, 2 * CUBOIDS].astype(F32).reshape(PEERS * SPAN, CH)
        stats = stats + pltpu.roll(stats, CH - PAIRS, 1) + pltpu.roll(stats, CH - 2 * PAIRS, 1)
        stats = stats.reshape(PEERS, SPAN, CH)
        tops = stats[:, 0:1, :]
        top = jnp.max(tops, axis=0)
        summed = jnp.sum(jnp.exp(tops - top[None]) * stats, axis=0)
        lanes = jnp.where(iota((SPAN, CH), 0) == 0, top, summed)
        columns = jnp.concatenate([lanes, jnp.zeros((CH - SPAN, CH), F32)], axis=0).T
        shared["g_top"] = columns[:PAIRS, 0:1]
        shared["g_inv"] = 1.0 / columns[:PAIRS, 1:2]
        shared["g_row"] = columns[:PAIRS, 2:3] * shared["g_inv"]

    def clear(slot):
        query_m[slot] = jnp.zeros(query_m.shape[1:], BF)
        grad_m[slot] = jnp.zeros(grad_m.shape[1:], BF)

    clear(0)

    def heads(h):
        return slice(h * HDIM, (h + 1) * HDIM)

    class Cuboid:
        def __init__(self, u):
            self.u, self.slot = u, u % 2
            self.low = []
            self.rows = {n: [[] for _ in range(HEADS)] for n in ("p", "ds", "out", "dq")}

        def project_query(self):
            cells = cells_ref[self.u]
            self.query_t = dot_nt(w_q_t, cells).astype(BF)
            for h in range(HEADS):
                query_m[self.slot, h, heads(h), :] = self.query_t[heads(h)]

        def project_grad(self):
            self.grad_t = dot_nt(w_o, up_ref[self.u]).astype(BF)
            for h in range(HEADS):
                grad_m[self.slot, h, heads(h), :] = self.grad_t[heads(h)]

        def project_keys(self):
            self.key_value = dot(cells_ref[self.u], w_kv).astype(BF)
            self.key, self.value = self.key_value[:, :CH], self.key_value[:, CH:]

        def project_global(self):
            self.s_global = dot(gk_b, self.query_t)
            self.d_global = dot(gv_b, self.grad_t)

        def project_transposed(self):
            self.key_t = self.key.T
            self.value_t = self.value.T

        def project_rows(self):
            self.query = self.query_t.T
            self.grad = self.grad_t.T

        def scores(self, h, q):
            columns = pl.ds(q, QUERIES)
            return (
                dot(self.key, query_m[self.slot, h, :, columns]),
                dot(self.value, grad_m[self.slot, h, :, columns]),
            )

        def softmax(self, h, q, score, dprob):
            rows = slice(h * GLOBALS, (h + 1) * GLOBALS)
            s_glob = self.s_global[rows, q : q + QUERIES]
            d_glob = self.d_global[rows, q : q + QUERIES]
            top = jnp.maximum(
                jnp.max(score, axis=0, keepdims=True), jnp.max(s_glob, axis=0, keepdims=True)
            )
            e_local = jnp.exp2((score - top) * (SCALE * LOG2E))
            e_global = jnp.exp2((s_glob - top) * (SCALE * LOG2E))
            total = jnp.sum(e_local, axis=0, keepdims=True) + jnp.sum(
                e_global, axis=0, keepdims=True
            )
            inv = 1.0 / total
            p_local = e_local * inv
            p_global = e_global * inv
            inner = jnp.sum(p_local * dprob, axis=0, keepdims=True) + jnp.sum(
                p_global * d_glob, axis=0, keepdims=True
            )
            self.rows["p"][h].append(p_global)
            self.rows["ds"][h].append(p_global * (d_glob - inner) * SCALE)
            return p_local.astype(BF), (p_local * (dprob - inner) * SCALE).astype(BF)

        def products(self, h, q, p_low, ds_low):
            part = heads(h)
            self.rows["out"][h].append(dot(self.value_t[part], p_low))
            self.rows["dq"][h].append(dot(self.key_t[part], ds_low))
            self.low.append((p_low, ds_low))
            if q + QUERIES == TOKENS:
                p_low, ds_low = (jnp.concatenate(x, axis=1) for x in zip(*self.low))
                self.low = []
                dkv_ref[self.slot, :, part] = dot(ds_low, self.query)[:, part]
                lanes = slice(CH + part.start, CH + part.stop)
                dkv_ref[self.slot, :, lanes] = dot(p_low, self.grad)[:, part]

        def add(self, ref, where, value):
            ref[where] = value if self.u == 0 else ref[where] + value

        def whole(self, name):
            rows = [jnp.concatenate(row, axis=1) for row in self.rows[name]]
            return jnp.concatenate(rows, axis=0)

        def finish_queries(self):
            p_rows, ds_rows = self.whole("p").astype(BF), self.whole("ds").astype(BF)
            self.out_t = (self.whole("out") + dot(shared["gv_t"], p_rows)).astype(BF)
            self.dq_t = (self.whole("dq") + dot(shared["gk_t"], ds_rows)).astype(BF)
            rows = jnp.concatenate([ds_rows, p_rows], axis=0)
            g_both = dot(rows, jnp.concatenate([self.query, self.grad], axis=1))
            self.add(g_sum, 1, g_both[:PAIRS, :CH])
            self.add(g_sum, 2, g_both[PAIRS:, CH:])

        def finish_global(self):
            score = dot(shared["gq_b"], self.key_t) * SCALE
            prob = jnp.exp(score - shared["g_top"]) * shared["g_inv"]
            dprob = dot(shared["gg_parts"], self.value_t)
            dprob = dprob[:PAIRS] + dprob[PAIRS : 2 * PAIRS] + dprob[2 * PAIRS :]
            dscore = prob * (dprob - shared["g_row"]) * SCALE
            p_hi, p_mid, _ = split3(prob)
            d_hi, d_mid, _ = split3(dscore)
            none = jnp.zeros((PAIRS, TOKENS), BF)
            self.parts = jnp.concatenate(
                [d_hi, d_mid, none, none, p_hi, p_mid, p_hi, none], axis=0
            )
            g_both = dot(
                jnp.concatenate([d_hi, d_mid, p_hi, p_mid], axis=0), self.key_value
            )
            self.add(g_sum, 0, g_both[:PAIRS, :CH] + g_both[PAIRS : 2 * PAIRS, :CH])
            self.add(g_sum, 3, g_both[2 * PAIRS : 3 * PAIRS, CH:] + g_both[3 * PAIRS :, CH:])

        def finish_keys(self):
            more = dot(self.parts.T, shared["more"])
            self.d_key_value = (dkv_ref[self.slot] + more).astype(BF)

        def finish_weights(self):
            self.grads = jnp.concatenate([self.dq_t.T, self.d_key_value], axis=1)
            everything = slice(None)
            first, last = slice(0, 3 * CH), slice(3 * CH, 4 * CH)
            self.add(w_sum, (everything, first), dot(cells_ref[self.u].T, self.grads))
            self.add(w_sum, (everything, last), dot(self.out_t, up_ref[self.u]))

        def finish_cells(self):
            delta_ref[self.u] = dot_nt(self.grads, w_qkv).astype(BF)

        def before(self):
            return [
                self.project_query,
                self.project_grad,
                self.project_keys,
                self.project_global,
                self.project_transposed,
                self.project_rows,
            ]

        def after(self):
            return [
                self.finish_queries,
                self.finish_global,
                self.finish_keys,
                self.finish_weights,
                self.finish_cells,
            ]

    cuboids = [Cuboid(u) for u in range(CUBOIDS)]
    for task in cuboids[0].before():
        task()
    order = [(c, h, q) for c in cuboids for h in range(HEADS) for q in range(0, TOKENS, QUERIES)]
    per_cuboid = len(order) // CUBOIDS
    ready = cuboids[0].scores(*order[0][1:])
    low = None
    for i, (cuboid, *step) in enumerate(order):
        place = i % per_cuboid
        u = cuboid.u
        if place == 0:
            early = cuboids[u + 1].before() if u + 1 < CUBOIDS else []
            if u == 0:
                early.insert(0, lambda: clear(1))
            late = cuboids[u - 1].after() if u > 0 else [global_operands, global_softmax]
        following = None
        if place + 1 == per_cuboid:
            for task in early + late:
                task()
        if i + 1 < len(order):
            following = order[i + 1][0].scores(*order[i + 1][1:])
        now = cuboid.softmax(*step, *ready)
        if low is not None:
            order[i - 1][0].products(*order[i - 1][1:], *low)
        if place > 0 and late:
            late.pop(0)()
        low = now
        if early:
            early.pop(0)()
        ready = following
    order[-1][0].products(*order[-1][1:], *low)
    for task in cuboids[-1].after():
        task()

    def tall(pieces):
        rows = jnp.concatenate(pieces, axis=0)
        return jnp.concatenate([rows, jnp.zeros((CH - rows.shape[0], CH), F32)], axis=0)

    def parts_of(rows):
        return [part.astype(F32) for part in split3(rows)]

    g_parts = [parts_of(head_diagonal(g_sum[i])) for i in range(3)]
    g_tall = jnp.concatenate([tall(parts) for parts in g_parts], axis=1).astype(BF)
    w_sum[:, : 3 * CH] += dot(tall([vectors] * 3).T.astype(BF), g_tall)
    a_hi, a_mid, a_low = parts_of(head_diagonal(g_sum[3]))
    u_hi, u_mid, u_low = parts_of(vup_ref[...])
    left = tall([a_hi, a_hi, a_hi, a_mid, a_mid, a_low]).T.astype(BF)
    w_sum[:, 3 * CH :] += dot(left, tall([u_hi, u_mid, u_low, u_hi, u_mid, u_hi]).astype(BF))
    vec = dot_nt(g_tall[: 4 * GLOBALS], w_qkv)
    vec = vec[:GLOBALS] + vec[GLOBALS : 2 * GLOBALS] + vec[2 * GLOBALS : 3 * GLOBALS]
    for i in range(4):
        total = w_sum[:, i * CH : (i + 1) * CH]
        high = total.astype(BF)
        rows = pl.ds(i * CH, CH)
        part_ref[0, rows, :] = high
        low_ref[rows, :] = total - high.astype(F32)
    hi, mid, _ = split3(vec)
    vec_parts = jnp.concatenate(
        [hi.astype(F32), mid.astype(F32), jnp.zeros((CH - VEC_LANES, CH), F32)], axis=0
    ).T.astype(BF)
    row, slots = vec_slots(TOKENS)
    spread = (iota((TOKENS, CH), 0) // SPAN == iota((TOKENS, CH), 1)).astype(BF)
    part_ref[1] = jnp.where(slots, dot(spread, vec_parts), low_ref[...]).astype(BF)

    back = back_matrix()
    for i in range(PEERS // GROUP):
        tokens = pl.ds(i * group_tokens, group_tokens)
        rows = jnp.concatenate([delta_ref[u, tokens, :] for u in range(CUBOIDS)], axis=0)
        moved = dot(back, rows).astype(BF)
        msg_ref[pl.ds(i * GROUP, GROUP), 0:PEER_ROWS, :] = moved.reshape(GROUP, PEER_ROWS, CH)
    back = piece_matrix()
    for i in range(PEERS // PIECE_GROUP):
        tokens = pl.ds(i * CH, CH)
        rows = jnp.concatenate([part_ref[0, tokens, :], part_ref[1, tokens, :]], axis=0)
        moved = dot(back, rows).astype(BF)
        msg_ref[pl.ds(i * PIECE_GROUP, PIECE_GROUP), PEER_ROWS:, :] = moved.reshape(
            PIECE_GROUP, PIECE_ROWS, CH
        )


def sum_kernel(recv_ref, piece_ref):
    summed = jnp.sum(recv_ref[:, PEER_ROWS:, :].astype(F32), axis=0)
    row, slots = vec_slots(PIECE_ROWS)
    slots = slots & (row >= SPAN)
    vec = summed + pltpu.roll(summed, CH - GLOBALS, 1)
    low = jnp.where(slots, 0.0, summed)
    weight = summed[:SPAN] + low[SPAN:]
    high = weight.astype(BF).astype(F32)
    vec_high = vec.astype(BF).astype(F32)
    vec_low = pltpu.roll(vec - vec_high, GLOBALS, 1)
    vec = jnp.where(iota((PIECE_ROWS, CH), 1) < GLOBALS, vec_high, vec_low)
    piece = jnp.where(slots, vec, jnp.concatenate([high, weight - high], axis=0)).astype(BF)
    piece_ref[...] = jnp.broadcast_to(piece[None], piece_ref.shape)


def spread_kernel(recv_ref, weight_ref, vec_ref):
    rows = PIECE_GROUP * PIECE_ROWS
    row, slots = vec_slots(rows)
    slots = slots & (row % PIECE_ROWS >= SPAN)
    target, source = iota((CH, rows), 0), iota((CH, rows), 1)
    joins = (source // PIECE_ROWS == target // SPAN) & (source % SPAN == target % SPAN)
    joins = joins.astype(BF)
    target, source = iota((PIECE_GROUP, rows), 0), iota((PIECE_GROUP, rows), 1)
    last = (source == target * PIECE_ROWS + PIECE_ROWS - 1).astype(BF)
    vec = []
    for i in range(PEERS // PIECE_GROUP):
        piece = recv_ref[pl.ds(i * PIECE_GROUP, PIECE_GROUP)].reshape(rows, CH)
        vec.append(dot(last, piece))
        piece = jnp.where(slots, 0.0, piece.astype(F32)).astype(BF)
        weight_ref[i] = dot(joins, piece)
    vec = jnp.concatenate(vec, axis=0).T
    vec_ref[...] = vec[:GLOBALS] + vec[GLOBALS : 2 * GLOBALS]


def place_kernel(shift_hbm, recv_ref, out_ref, held, shift_ref, sem):
    copy = pltpu.make_async_copy(shift_hbm, shift_ref, sem)
    copy.start()
    for i in range(PEERS // GROUP):
        held[pl.ds(i * GROUP_ROWS, GROUP_ROWS), :] = recv_ref[
            pl.ds(i * GROUP, GROUP), 0:PEER_ROWS, :
        ].reshape(GROUP_ROWS, CH)
    held[CELLS_DEV:, :] = held[:WINDOW, :]
    copy.wait()
    offset = (CELLS_DEV - tile_offset(shift_ref)) % CELLS_DEV
    mover = shift_matrix(offset % 16, GROUP_ROWS, WINDOW)
    base = offset - offset % 16
    for i in range(CELLS_DEV // GROUP_ROWS):
        start = pl.multiple_of((base + i * GROUP_ROWS) % CELLS_DEV, 16)
        moved = dot(mover, held[pl.ds(start, WINDOW), :]).astype(BF)
        out_ref[pl.ds(i * GROUP_ROWS, GROUP_ROWS), :] = moved


VMEM = pl.BlockSpec(memory_space=pltpu.VMEM)
HBM = pl.BlockSpec(memory_space=pltpu.HBM)
PACK_PARAMS = pltpu.CompilerParams(vmem_limit_bytes=58_000_000)
PARAMS = pltpu.CompilerParams(vmem_limit_bytes=48 * 1024 * 1024)


def exchange(rows):
    return lax.all_to_all(rows, ("tile", "frame"), split_axis=0, concat_axis=0, tiled=True)


def body(cells, vectors, weights, cuboid_shift, cell_upstream, vector_upstream):
    message = pl.pallas_call(
        pack_kernel,
        out_shape=pltpu.VMEM((PEERS, MSG_SPANS, SPAN, CH), BF),
        in_specs=[HBM] * 6,
        out_specs=VMEM,
        scratch_shapes=[
            pltpu.VMEM((CELLS_DEV + WINDOW, 2 * CH), BF),
            pltpu.VMEM((GLOBALS, CH), BF),
            pltpu.VMEM((4, CH, CH), BF),
            pltpu.VMEM((GLOBALS, CH), F32),
            pltpu.SMEM((1,), jnp.int32),
            pltpu.SemaphoreType.DMA((8,)),
        ],
        compiler_params=PACK_PARAMS,
        name="pack",
    )(cuboid_shift, cells[0], cell_upstream[0], vectors, weights, vector_upstream)
    received = exchange(message)
    message = pl.pallas_call(
        owner_kernel,
        out_shape=pltpu.VMEM((PEERS, PEER_ROWS + PIECE_ROWS, CH), BF),
        in_specs=[VMEM] * 4,
        out_specs=VMEM,
        scratch_shapes=[
            pltpu.VMEM((CUBOIDS, TOKENS, CH), BF),
            pltpu.VMEM((CUBOIDS, TOKENS, CH), BF),
            pltpu.VMEM((CUBOIDS, TOKENS, CH), BF),
            pltpu.VMEM((2, HEADS, CH, TOKENS), BF),
            pltpu.VMEM((2, HEADS, CH, TOKENS), BF),
            pltpu.VMEM((CH, 4 * CH), F32),
            pltpu.VMEM((4, PAIRS, CH), F32),
            pltpu.VMEM((2, TOKENS, CH), BF),
            pltpu.VMEM((TOKENS, CH), F32),
            pltpu.VMEM((2, TOKENS, 2 * CH), F32),
        ],
        compiler_params=PARAMS,
        name="owner",
    )(received, vectors, weights, vector_upstream)
    received = exchange(message)
    pieces = pl.pallas_call(
        sum_kernel,
        out_shape=pltpu.VMEM((PEERS, PIECE_ROWS, CH), BF),
        in_specs=[VMEM],
        out_specs=VMEM,
        compiler_params=PARAMS,
        name="sum_pieces",
    )(received)
    pieces = exchange(pieces)
    cell_grad = pl.pallas_call(
        place_kernel,
        out_shape=jax.ShapeDtypeStruct((CELLS_DEV, CH), BF),
        in_specs=[HBM, VMEM],
        out_specs=VMEM,
        scratch_shapes=[
            pltpu.VMEM((CELLS_DEV + WINDOW, CH), BF),
            pltpu.SMEM((1,), jnp.int32),
            pltpu.SemaphoreType.DMA,
        ],
        compiler_params=PARAMS,
        name="place",
    )(cuboid_shift, received)
    weight_grad, vector_grad = pl.pallas_call(
        spread_kernel,
        out_shape=[
            jax.ShapeDtypeStruct((4, CH, CH), F32),
            jax.ShapeDtypeStruct((GLOBALS, CH), F32),
        ],
        in_specs=[VMEM],
        out_specs=[VMEM, VMEM],
        compiler_params=PARAMS,
        name="spread",
    )(pieces)
    return cell_grad[None], weight_grad, vector_grad


def solution(mesh):
    in_specs = (P("frame", "tile", None), P(), P(), P(), P("frame", "tile", None), P())
    out_specs = (P("frame", "tile", None), P(), P())
    return jax.shard_map(body, mesh=mesh, in_specs=in_specs, out_specs=out_specs, check_vma=False)
```

```python
import math

import jax
import jax.numpy as jnp
from jax import lax
from jax.experimental import pallas as pl
from jax.experimental.pallas import tpu as pltpu
from jax.sharding import PartitionSpec as P

CH = 128
HEADS = 4
HDIM = 32
GLOBALS = 8
PAIRS = HEADS * GLOBALS
SPAN = 4
CELLS_DEV = 2048
PEERS = 128
PEER_ROWS = CELLS_DEV // PEERS
CUBOIDS = PEER_ROWS // SPAN
TOKENS = 512
QUERIES = 256
GROUP = 16
GROUP_ROWS = GROUP * PEER_ROWS
WINDOW = GROUP_ROWS + 16
MSG_SPANS = 9
PIECE_ROWS = 2 * SPAN
PIECE_GROUP = 32
VEC_LANES = 2 * GLOBALS
SCALE = HDIM**-0.5
LOG2E = math.log2(math.e)
BF = jnp.bfloat16
F32 = jnp.float32
NT = (((1,), (1,)), ((), ()))


def dot(a, b):
    return jnp.dot(a, b, preferred_element_type=F32)


def dot_nt(a, b):
    return lax.dot_general(a, b, NT, preferred_element_type=F32)


def iota(shape, axis):
    return lax.broadcasted_iota(jnp.int32, shape, axis)


def split3(x):
    hi = x.astype(BF)
    rest = x - hi.astype(F32)
    mid = rest.astype(BF)
    low = (rest - mid.astype(F32)).astype(BF)
    return hi, mid, low


def head_blocks(rows):
    head = iota((GLOBALS, CH), 1) // HDIM
    return jnp.concatenate([jnp.where(head == h, rows, 0.0) for h in range(HEADS)], axis=0)


def diagonal(first, second):
    zero = jnp.zeros((CH, CH), F32)
    rows = [jnp.concatenate([first, zero], axis=1), jnp.concatenate([zero, second], axis=1)]
    return jnp.concatenate(rows, axis=0).astype(BF)


def head_diagonal(blocks):
    head = iota((GLOBALS, CH), 1) // HDIM
    total = jnp.zeros((GLOBALS, CH), F32)
    for h in range(HEADS):
        total += jnp.where(head == h, blocks[h * GLOBALS : (h + 1) * GLOBALS], 0.0)
    return total


def global_rows(vectors, weight):
    return dot(vectors.astype(BF), weight).astype(BF).astype(F32)


def global_upstream(vector_upstream, w_out):
    hi, mid, low = split3(vector_upstream)
    return dot_nt(hi, w_out) + dot_nt(mid, w_out) + dot_nt(low, w_out)


def tile_offset(shift_ref):
    return (shift_ref[0] * (lax.axis_index("tile") + 1)) % CELLS_DEV


def shift_matrix(step, rows, window):
    return (iota((rows, window), 1) == iota((rows, window), 0) + step).astype(BF)


def pack_kernel(
    shift_hbm,
    cells_hbm,
    up_hbm,
    vectors_hbm,
    weights_hbm,
    vup_hbm,
    msg_ref,
    held,
    vectors_ref,
    weights_ref,
    vup_ref,
    shift_ref,
    sems,
):
    whole, wrap = pl.ds(0, CELLS_DEV), pl.ds(CELLS_DEV, WINDOW)
    left, right = pl.ds(0, CH), pl.ds(CH, CH)
    copies = [
        pltpu.make_async_copy(source, target, sems.at[i])
        for i, (source, target) in enumerate(
            [
                (vectors_hbm, vectors_ref),
                (weights_hbm, weights_ref),
                (vup_hbm, vup_ref),
                (cells_hbm, held.at[whole, left]),
                (cells_hbm.at[pl.ds(0, WINDOW)], held.at[wrap, left]),
                (up_hbm, held.at[whole, right]),
                (up_hbm.at[pl.ds(0, WINDOW)], held.at[wrap, right]),
                (shift_hbm, shift_ref),
            ]
        )
    ]
    for copy in copies:
        copy.start()
    for copy in copies[:5]:
        copy.wait()
    vectors = vectors_ref[...].astype(F32)
    cells = held[:CELLS_DEV, :CH]
    query = head_blocks(global_rows(vectors, weights_ref[0])).astype(BF)
    upstream = head_blocks(global_upstream(vup_ref[...], weights_ref[3]))
    up_parts = jnp.concatenate([part.astype(F32) for part in split3(upstream)], axis=0).astype(BF)
    w_kv = jnp.concatenate([weights_ref[1], weights_ref[2]], axis=1)
    key_value = dot(cells, w_kv).astype(BF)
    score = dot_nt(query, key_value[:, :CH]) * SCALE
    dprob = dot_nt(up_parts, key_value[:, CH:])
    dprob = dprob[:PAIRS] + dprob[PAIRS : 2 * PAIRS] + dprob[2 * PAIRS :]
    top = jnp.max(score, axis=1, keepdims=True)
    weight = jnp.exp(score - top)
    total = jnp.sum(weight, axis=1, keepdims=True)
    inner = jnp.sum(weight * dprob, axis=1, keepdims=True)
    lane = iota((PAIRS, CH), 1)
    stats = jnp.where(lane == 0, top, jnp.where(lane == 1, total, jnp.where(lane == 2, inner, 0.0)))
    parts = [part.astype(F32) for part in split3(stats)] + [jnp.zeros((PAIRS, CH), F32)]
    rows = jnp.concatenate(parts, axis=0).T[:GLOBALS].astype(BF)
    msg_ref[:, 2 * CUBOIDS] = jnp.broadcast_to(rows[None, :SPAN], (PEERS, SPAN, CH))
    for copy in copies[5:]:
        copy.wait()
    offset = tile_offset(shift_ref)
    base = offset - offset % 16
    mover = shift_matrix(offset % 16, GROUP_ROWS - 16, GROUP_ROWS)
    for first in range(0, PEERS, GROUP - 1):
        count = min(GROUP - 1, PEERS - first)
        start = pl.multiple_of((base + first * PEER_ROWS) % CELLS_DEV, 16)
        rows = held[pl.ds(start, GROUP_ROWS), :]
        moved = dot(mover[: count * PEER_ROWS], rows).astype(BF)
        peers = pl.ds(first, count)
        shape = (count, CUBOIDS, SPAN, CH)
        msg_ref[peers, 0:CUBOIDS] = moved[:, :CH].reshape(shape)
        msg_ref[peers, CUBOIDS : 2 * CUBOIDS] = moved[:, CH:].reshape(shape)


def piece_matrix():
    rows = PIECE_GROUP * PIECE_ROWS
    row = iota((rows, rows), 0)
    source = row // SPAN % 2 * CH + row // PIECE_ROWS * SPAN + row % SPAN
    return (iota((rows, rows), 1) == source).astype(BF)


def vec_slots(rows):
    row, lane = iota((rows, CH), 0), iota((rows, CH), 1)
    return row, (row % SPAN == SPAN - 1) & (lane < VEC_LANES)


def back_matrix():
    row = iota((GROUP_ROWS, GROUP_ROWS), 0)
    column = iota((GROUP_ROWS, GROUP_ROWS), 1)
    source = (row // SPAN) % CUBOIDS * (GROUP * SPAN) + row // PEER_ROWS * SPAN + row % SPAN
    return (column == source).astype(BF)


def owner_kernel(
    recv_ref,
    vectors_ref,
    weights_ref,
    vup_ref,
    msg_ref,
    cells_ref,
    up_ref,
    delta_ref,
    query_m,
    grad_m,
    w_sum,
    g_sum,
    part_ref,
    low_ref,
    dkv_ref,
):
    group_tokens = GROUP * SPAN
    vectors = vectors_ref[...].astype(F32)
    w_q, w_k, w_v, w_o = (weights_ref[i] for i in range(4))
    w_kv = jnp.concatenate([w_k, w_v], axis=1)
    w_qkv = jnp.concatenate([w_q, w_kv], axis=1)
    w_q_t = w_q.T
    gk = head_blocks(global_rows(vectors, w_k))
    gv = head_blocks(global_rows(vectors, w_v))
    gk_b, gv_b = gk.astype(BF), gv.astype(BF)
    zero = jnp.zeros((PAIRS, CH), F32)
    shared = {}

    def global_operands():
        gq = head_blocks(global_rows(vectors, w_q))
        gg = head_blocks(global_upstream(vup_ref[...], w_o))
        gg3 = [part.astype(F32) for part in split3(gg)]
        shared["gq_b"] = gq.astype(BF)
        for name, blocks in (("gk_t", gk), ("gv_t", gv)):
            wide = jnp.concatenate([blocks, zero, zero, zero], axis=0)
            shared[name] = wide.T[:, :PAIRS].astype(BF)
        shared["gg_parts"] = jnp.concatenate(gg3, axis=0).astype(BF)
        shared["more"] = diagonal(
            jnp.concatenate([gq, gq, zero, zero], axis=0),
            jnp.concatenate([gg3[0], gg3[0], gg3[1], zero], axis=0),
        )

    def global_softmax():
        stats = recv_ref[:, 2 * CUBOIDS].astype(F32).reshape(PEERS * SPAN, CH)
        stats = stats + pltpu.roll(stats, CH - PAIRS, 1) + pltpu.roll(stats, CH - 2 * PAIRS, 1)
        stats = stats.reshape(PEERS, SPAN, CH)
        tops = stats[:, 0:1, :]
        top = jnp.max(tops, axis=0)
        summed = jnp.sum(jnp.exp(tops - top[None]) * stats, axis=0)
        lanes = jnp.where(iota((SPAN, CH), 0) == 0, top, summed)
        columns = jnp.concatenate([lanes, jnp.zeros((CH - SPAN, CH), F32)], axis=0).T
        shared["g_top"] = columns[:PAIRS, 0:1]
        shared["g_inv"] = 1.0 / columns[:PAIRS, 1:2]
        shared["g_row"] = columns[:PAIRS, 2:3] * shared["g_inv"]

    def clear(slot):
        query_m[slot] = jnp.zeros(query_m.shape[1:], BF)
        grad_m[slot] = jnp.zeros(grad_m.shape[1:], BF)

    clear(0)

    def heads(h):
        return slice(h * HDIM, (h + 1) * HDIM)

    class Cuboid:
        def __init__(self, u):
            self.u, self.slot = u, u % 2
            self.low = []
            self.rows = {n: [[] for _ in range(HEADS)] for n in ("p", "ds", "out", "dq")}

        def project_query(self):
            cells = recv_ref[:, self.u].reshape(TOKENS, CH)
            cells_ref[self.u] = cells
            self.query_t = dot_nt(w_q_t, cells).astype(BF)
            for h in range(HEADS):
                query_m[self.slot, h, heads(h), :] = self.query_t[heads(h)]

        def project_grad(self):
            upstream = recv_ref[:, CUBOIDS + self.u].reshape(TOKENS, CH)
            up_ref[self.u] = upstream
            self.grad_t = dot_nt(w_o, upstream).astype(BF)
            for h in range(HEADS):
                grad_m[self.slot, h, heads(h), :] = self.grad_t[heads(h)]

        def project_keys(self):
            self.key_value = dot(cells_ref[self.u], w_kv).astype(BF)
            self.key, self.value = self.key_value[:, :CH], self.key_value[:, CH:]

        def project_global(self):
            self.s_global = dot(gk_b, self.query_t)
            self.d_global = dot(gv_b, self.grad_t)

        def project_transposed(self):
            self.key_t = self.key.T
            self.value_t = self.value.T

        def project_rows(self):
            self.query = self.query_t.T
            self.grad = self.grad_t.T

        def scores(self, h, q):
            columns = pl.ds(q, QUERIES)
            return (
                dot(self.key, query_m[self.slot, h, :, columns]),
                dot(self.value, grad_m[self.slot, h, :, columns]),
            )

        def softmax(self, h, q, score, dprob):
            rows = slice(h * GLOBALS, (h + 1) * GLOBALS)
            s_glob = self.s_global[rows, q : q + QUERIES]
            d_glob = self.d_global[rows, q : q + QUERIES]
            top = jnp.maximum(
                jnp.max(score, axis=0, keepdims=True), jnp.max(s_glob, axis=0, keepdims=True)
            )
            e_local = jnp.exp2((score - top) * (SCALE * LOG2E))
            e_global = jnp.exp2((s_glob - top) * (SCALE * LOG2E))
            total = jnp.sum(e_local, axis=0, keepdims=True) + jnp.sum(
                e_global, axis=0, keepdims=True
            )
            inv = 1.0 / total
            p_local = e_local * inv
            p_global = e_global * inv
            inner = jnp.sum(p_local * dprob, axis=0, keepdims=True) + jnp.sum(
                p_global * d_glob, axis=0, keepdims=True
            )
            self.rows["p"][h].append(p_global)
            self.rows["ds"][h].append(p_global * (d_glob - inner) * SCALE)
            return p_local.astype(BF), (p_local * (dprob - inner) * SCALE).astype(BF)

        def products(self, h, q, p_low, ds_low):
            part = heads(h)
            self.rows["out"][h].append(dot(self.value_t[part], p_low))
            self.rows["dq"][h].append(dot(self.key_t[part], ds_low))
            self.low.append((p_low, ds_low))
            if q + QUERIES == TOKENS:
                p_low, ds_low = (jnp.concatenate(x, axis=1) for x in zip(*self.low))
                self.low = []
                dkv_ref[self.slot, :, part] = dot(ds_low, self.query)[:, part]
                lanes = slice(CH + part.start, CH + part.stop)
                dkv_ref[self.slot, :, lanes] = dot(p_low, self.grad)[:, part]

        def add(self, ref, where, value):
            ref[where] = value if self.u == 0 else ref[where] + value

        def whole(self, name):
            rows = [jnp.concatenate(row, axis=1) for row in self.rows[name]]
            return jnp.concatenate(rows, axis=0)

        def finish_queries(self):
            p_rows, ds_rows = self.whole("p").astype(BF), self.whole("ds").astype(BF)
            self.out_t = (self.whole("out") + dot(shared["gv_t"], p_rows)).astype(BF)
            self.dq_t = (self.whole("dq") + dot(shared["gk_t"], ds_rows)).astype(BF)
            rows = jnp.concatenate([ds_rows, p_rows], axis=0)
            g_both = dot(rows, jnp.concatenate([self.query, self.grad], axis=1))
            self.add(g_sum, 1, g_both[:PAIRS, :CH])
            self.add(g_sum, 2, g_both[PAIRS:, CH:])

        def finish_global(self):
            score = dot(shared["gq_b"], self.key_t) * SCALE
            prob = jnp.exp(score - shared["g_top"]) * shared["g_inv"]
            dprob = dot(shared["gg_parts"], self.value_t)
            dprob = dprob[:PAIRS] + dprob[PAIRS : 2 * PAIRS] + dprob[2 * PAIRS :]
            dscore = prob * (dprob - shared["g_row"]) * SCALE
            p_hi, p_mid, _ = split3(prob)
            d_hi, d_mid, _ = split3(dscore)
            none = jnp.zeros((PAIRS, TOKENS), BF)
            self.parts = jnp.concatenate(
                [d_hi, d_mid, none, none, p_hi, p_mid, p_hi, none], axis=0
            )
            g_both = dot(
                jnp.concatenate([d_hi, d_mid, p_hi, p_mid], axis=0), self.key_value
            )
            self.add(g_sum, 0, g_both[:PAIRS, :CH] + g_both[PAIRS : 2 * PAIRS, :CH])
            self.add(g_sum, 3, g_both[2 * PAIRS : 3 * PAIRS, CH:] + g_both[3 * PAIRS :, CH:])

        def finish_keys(self):
            more = dot(self.parts.T, shared["more"])
            self.d_key_value = (dkv_ref[self.slot] + more).astype(BF)

        def finish_weights(self):
            self.grads = jnp.concatenate([self.dq_t.T, self.d_key_value], axis=1)
            everything = slice(None)
            first, last = slice(0, 3 * CH), slice(3 * CH, 4 * CH)
            self.add(w_sum, (everything, first), dot(cells_ref[self.u].T, self.grads))
            self.add(w_sum, (everything, last), dot(self.out_t, up_ref[self.u]))

        def finish_cells(self):
            delta_ref[self.u] = dot_nt(self.grads, w_qkv).astype(BF)

        def before(self):
            return [
                self.project_query,
                self.project_grad,
                self.project_keys,
                self.project_global,
                self.project_transposed,
                self.project_rows,
            ]

        def after(self):
            return [
                self.finish_queries,
                self.finish_global,
                self.finish_keys,
                self.finish_weights,
                self.finish_cells,
            ]

    cuboids = [Cuboid(u) for u in range(CUBOIDS)]
    for task in cuboids[0].before():
        task()
    order = [(c, h, q) for c in cuboids for h in range(HEADS) for q in range(0, TOKENS, QUERIES)]
    per_cuboid = len(order) // CUBOIDS
    ready = cuboids[0].scores(*order[0][1:])
    low = None
    for i, (cuboid, *step) in enumerate(order):
        place = i % per_cuboid
        u = cuboid.u
        if place == 0:
            early = cuboids[u + 1].before() if u + 1 < CUBOIDS else []
            if u == 0:
                early.insert(0, lambda: clear(1))
            late = cuboids[u - 1].after() if u > 0 else [global_operands, global_softmax]
        following = None
        if place + 1 == per_cuboid:
            for task in early + late:
                task()
        if i + 1 < len(order):
            following = order[i + 1][0].scores(*order[i + 1][1:])
        now = cuboid.softmax(*step, *ready)
        if low is not None:
            order[i - 1][0].products(*order[i - 1][1:], *low)
        if place > 0 and late:
            late.pop(0)()
        low = now
        if early:
            early.pop(0)()
        ready = following
    order[-1][0].products(*order[-1][1:], *low)
    for task in cuboids[-1].after():
        task()

    def tall(pieces):
        rows = jnp.concatenate(pieces, axis=0)
        return jnp.concatenate([rows, jnp.zeros((CH - rows.shape[0], CH), F32)], axis=0)

    def parts_of(rows):
        return [part.astype(F32) for part in split3(rows)]

    g_parts = [parts_of(head_diagonal(g_sum[i])) for i in range(3)]
    g_tall = jnp.concatenate([tall(parts) for parts in g_parts], axis=1).astype(BF)
    w_sum[:, : 3 * CH] += dot(tall([vectors] * 3).T.astype(BF), g_tall)
    a_hi, a_mid, a_low = parts_of(head_diagonal(g_sum[3]))
    u_hi, u_mid, u_low = parts_of(vup_ref[...])
    left = tall([a_hi, a_hi, a_hi, a_mid, a_mid, a_low]).T.astype(BF)
    w_sum[:, 3 * CH :] += dot(left, tall([u_hi, u_mid, u_low, u_hi, u_mid, u_hi]).astype(BF))
    vec = dot_nt(g_tall[: 4 * GLOBALS], w_qkv)
    vec = vec[:GLOBALS] + vec[GLOBALS : 2 * GLOBALS] + vec[2 * GLOBALS : 3 * GLOBALS]
    for i in range(4):
        total = w_sum[:, i * CH : (i + 1) * CH]
        high = total.astype(BF)
        rows = pl.ds(i * CH, CH)
        part_ref[0, rows, :] = high
        low_ref[rows, :] = total - high.astype(F32)
    hi, mid, _ = split3(vec)
    vec_parts = jnp.concatenate(
        [hi.astype(F32), mid.astype(F32), jnp.zeros((CH - VEC_LANES, CH), F32)], axis=0
    ).T.astype(BF)
    row, slots = vec_slots(TOKENS)
    spread = (iota((TOKENS, CH), 0) // SPAN == iota((TOKENS, CH), 1)).astype(BF)
    part_ref[1] = jnp.where(slots, dot(spread, vec_parts), low_ref[...]).astype(BF)

    back = back_matrix()
    for i in range(PEERS // GROUP):
        tokens = pl.ds(i * group_tokens, group_tokens)
        rows = jnp.concatenate([delta_ref[u, tokens, :] for u in range(CUBOIDS)], axis=0)
        moved = dot(back, rows).astype(BF)
        msg_ref[pl.ds(i * GROUP, GROUP), 0:PEER_ROWS, :] = moved.reshape(GROUP, PEER_ROWS, CH)
    back = piece_matrix()
    for i in range(PEERS // PIECE_GROUP):
        tokens = pl.ds(i * CH, CH)
        rows = jnp.concatenate([part_ref[0, tokens, :], part_ref[1, tokens, :]], axis=0)
        moved = dot(back, rows).astype(BF)
        msg_ref[pl.ds(i * PIECE_GROUP, PIECE_GROUP), PEER_ROWS:, :] = moved.reshape(
            PIECE_GROUP, PIECE_ROWS, CH
        )


def sum_kernel(recv_ref, piece_ref):
    summed = jnp.sum(recv_ref[:, PEER_ROWS:, :].astype(F32), axis=0)
    row, slots = vec_slots(PIECE_ROWS)
    slots = slots & (row >= SPAN)
    vec = summed + pltpu.roll(summed, CH - GLOBALS, 1)
    low = jnp.where(slots, 0.0, summed)
    weight = summed[:SPAN] + low[SPAN:]
    high = weight.astype(BF).astype(F32)
    vec_high = vec.astype(BF).astype(F32)
    vec_low = pltpu.roll(vec - vec_high, GLOBALS, 1)
    vec = jnp.where(iota((PIECE_ROWS, CH), 1) < GLOBALS, vec_high, vec_low)
    piece = jnp.where(slots, vec, jnp.concatenate([high, weight - high], axis=0)).astype(BF)
    piece_ref[...] = jnp.broadcast_to(piece[None], piece_ref.shape)


def spread_kernel(recv_ref, weight_ref, vec_ref):
    rows = PIECE_GROUP * PIECE_ROWS
    row, slots = vec_slots(rows)
    slots = slots & (row % PIECE_ROWS >= SPAN)
    target, source = iota((CH, rows), 0), iota((CH, rows), 1)
    joins = (source // PIECE_ROWS == target // SPAN) & (source % SPAN == target % SPAN)
    joins = joins.astype(BF)
    target, source = iota((PIECE_GROUP, rows), 0), iota((PIECE_GROUP, rows), 1)
    last = (source == target * PIECE_ROWS + PIECE_ROWS - 1).astype(BF)
    vec = []
    for i in range(PEERS // PIECE_GROUP):
        piece = recv_ref[pl.ds(i * PIECE_GROUP, PIECE_GROUP)].reshape(rows, CH)
        vec.append(dot(last, piece))
        piece = jnp.where(slots, 0.0, piece.astype(F32)).astype(BF)
        weight_ref[i] = dot(joins, piece)
    vec = jnp.concatenate(vec, axis=0).T
    vec_ref[...] = vec[:GLOBALS] + vec[GLOBALS : 2 * GLOBALS]


def place_kernel(shift_hbm, recv_ref, out_ref, held, shift_ref, sem):
    copy = pltpu.make_async_copy(shift_hbm, shift_ref, sem)
    copy.start()
    for i in range(PEERS // GROUP):
        held[pl.ds(i * GROUP_ROWS, GROUP_ROWS), :] = recv_ref[
            pl.ds(i * GROUP, GROUP), 0:PEER_ROWS, :
        ].reshape(GROUP_ROWS, CH)
    held[CELLS_DEV:, :] = held[:WINDOW, :]
    copy.wait()
    offset = (CELLS_DEV - tile_offset(shift_ref)) % CELLS_DEV
    mover = shift_matrix(offset % 16, GROUP_ROWS, WINDOW)
    base = offset - offset % 16
    for i in range(CELLS_DEV // GROUP_ROWS):
        start = pl.multiple_of((base + i * GROUP_ROWS) % CELLS_DEV, 16)
        moved = dot(mover, held[pl.ds(start, WINDOW), :]).astype(BF)
        out_ref[pl.ds(i * GROUP_ROWS, GROUP_ROWS), :] = moved


VMEM = pl.BlockSpec(memory_space=pltpu.VMEM)
HBM = pl.BlockSpec(memory_space=pltpu.HBM)
PACK_PARAMS = pltpu.CompilerParams(vmem_limit_bytes=58_000_000)
PARAMS = pltpu.CompilerParams(vmem_limit_bytes=48 * 1024 * 1024)


def exchange(rows):
    return lax.all_to_all(rows, ("tile", "frame"), split_axis=0, concat_axis=0, tiled=True)


def body(cells, vectors, weights, cuboid_shift, cell_upstream, vector_upstream):
    message = pl.pallas_call(
        pack_kernel,
        out_shape=pltpu.VMEM((PEERS, MSG_SPANS, SPAN, CH), BF),
        in_specs=[HBM] * 6,
        out_specs=VMEM,
        scratch_shapes=[
            pltpu.VMEM((CELLS_DEV + WINDOW, 2 * CH), BF),
            pltpu.VMEM((GLOBALS, CH), BF),
            pltpu.VMEM((4, CH, CH), BF),
            pltpu.VMEM((GLOBALS, CH), F32),
            pltpu.SMEM((1,), jnp.int32),
            pltpu.SemaphoreType.DMA((8,)),
        ],
        compiler_params=PACK_PARAMS,
        name="pack",
    )(cuboid_shift, cells[0], cell_upstream[0], vectors, weights, vector_upstream)
    received = exchange(message)
    message = pl.pallas_call(
        owner_kernel,
        out_shape=pltpu.VMEM((PEERS, PEER_ROWS + PIECE_ROWS, CH), BF),
        in_specs=[VMEM] * 4,
        out_specs=VMEM,
        scratch_shapes=[
            pltpu.VMEM((CUBOIDS, TOKENS, CH), BF),
            pltpu.VMEM((CUBOIDS, TOKENS, CH), BF),
            pltpu.VMEM((CUBOIDS, TOKENS, CH), BF),
            pltpu.VMEM((2, HEADS, CH, TOKENS), BF),
            pltpu.VMEM((2, HEADS, CH, TOKENS), BF),
            pltpu.VMEM((CH, 4 * CH), F32),
            pltpu.VMEM((4, PAIRS, CH), F32),
            pltpu.VMEM((2, TOKENS, CH), BF),
            pltpu.VMEM((TOKENS, CH), F32),
            pltpu.VMEM((2, TOKENS, 2 * CH), F32),
        ],
        compiler_params=PARAMS,
        name="owner",
    )(received, vectors, weights, vector_upstream)
    received = exchange(message)
    pieces = pl.pallas_call(
        sum_kernel,
        out_shape=pltpu.VMEM((PEERS, PIECE_ROWS, CH), BF),
        in_specs=[VMEM],
        out_specs=VMEM,
        compiler_params=PARAMS,
        name="sum_pieces",
    )(received)
    pieces = exchange(pieces)
    cell_grad = pl.pallas_call(
        place_kernel,
        out_shape=jax.ShapeDtypeStruct((CELLS_DEV, CH), BF),
        in_specs=[HBM, VMEM],
        out_specs=VMEM,
        scratch_shapes=[
            pltpu.VMEM((CELLS_DEV + WINDOW, CH), BF),
            pltpu.SMEM((1,), jnp.int32),
            pltpu.SemaphoreType.DMA,
        ],
        compiler_params=PARAMS,
        name="place",
    )(cuboid_shift, received)
    weight_grad, vector_grad = pl.pallas_call(
        spread_kernel,
        out_shape=[
            jax.ShapeDtypeStruct((4, CH, CH), F32),
            jax.ShapeDtypeStruct((GLOBALS, CH), F32),
        ],
        in_specs=[VMEM],
        out_specs=[VMEM, VMEM],
        compiler_params=PARAMS,
        name="spread",
    )(pieces)
    return cell_grad[None], weight_grad, vector_grad


def solution(mesh):
    in_specs = (P("frame", "tile", None), P(), P(), P(), P("frame", "tile", None), P())
    out_specs = (P("frame", "tile", None), P(), P())
    return jax.shard_map(body, mesh=mesh, in_specs=in_specs, out_specs=out_specs, check_vma=False)
```

```python
import math

import jax
import jax.numpy as jnp
from jax import lax
from jax.experimental import pallas as pl
from jax.experimental.pallas import tpu as pltpu
from jax.sharding import PartitionSpec as P

CH = 128
HEADS = 4
HDIM = 32
GLOBALS = 8
PAIRS = HEADS * GLOBALS
SPAN = 4
CELLS_DEV = 2048
PEERS = 128
PEER_ROWS = CELLS_DEV // PEERS
CUBOIDS = PEER_ROWS // SPAN
TOKENS = 512
QUERIES = 256
GROUP = 16
GROUP_ROWS = GROUP * PEER_ROWS
WINDOW = GROUP_ROWS + 16
MSG_SPANS = 9
PIECE_ROWS = 2 * SPAN
PIECE_GROUP = 32
VEC_LANES = 2 * GLOBALS
SCALE = HDIM**-0.5
LOG2E = math.log2(math.e)
BF = jnp.bfloat16
F32 = jnp.float32
NT = (((1,), (1,)), ((), ()))


def dot(a, b):
    return jnp.dot(a, b, preferred_element_type=F32)


def dot_nt(a, b):
    return lax.dot_general(a, b, NT, preferred_element_type=F32)


def iota(shape, axis):
    return lax.broadcasted_iota(jnp.int32, shape, axis)


def split3(x):
    hi = x.astype(BF)
    rest = x - hi.astype(F32)
    mid = rest.astype(BF)
    low = (rest - mid.astype(F32)).astype(BF)
    return hi, mid, low


def head_blocks(rows):
    head = iota((GLOBALS, CH), 1) // HDIM
    return jnp.concatenate([jnp.where(head == h, rows, 0.0) for h in range(HEADS)], axis=0)


def diagonal(first, second):
    zero = jnp.zeros((CH, CH), F32)
    rows = [jnp.concatenate([first, zero], axis=1), jnp.concatenate([zero, second], axis=1)]
    return jnp.concatenate(rows, axis=0).astype(BF)


def head_diagonal(blocks):
    head = iota((GLOBALS, CH), 1) // HDIM
    total = jnp.zeros((GLOBALS, CH), F32)
    for h in range(HEADS):
        total += jnp.where(head == h, blocks[h * GLOBALS : (h + 1) * GLOBALS], 0.0)
    return total


def global_rows(vectors, weight):
    return dot(vectors.astype(BF), weight).astype(BF).astype(F32)


def global_upstream(vector_upstream, w_out):
    hi, mid, low = split3(vector_upstream)
    return dot_nt(hi, w_out) + dot_nt(mid, w_out) + dot_nt(low, w_out)


def tile_offset(shift_ref):
    return (shift_ref[0] * (lax.axis_index("tile") + 1)) % CELLS_DEV


def shift_matrix(step, rows, window):
    return (iota((rows, window), 1) == iota((rows, window), 0) + step).astype(BF)


def pack_kernel(
    shift_hbm,
    cells_hbm,
    up_hbm,
    vectors_hbm,
    weights_hbm,
    vup_hbm,
    msg_ref,
    held,
    vectors_ref,
    weights_ref,
    vup_ref,
    shift_ref,
    sems,
):
    whole, wrap = pl.ds(0, CELLS_DEV), pl.ds(CELLS_DEV, WINDOW)
    left, right = pl.ds(0, CH), pl.ds(CH, CH)
    copies = [
        pltpu.make_async_copy(source, target, sems.at[i])
        for i, (source, target) in enumerate(
            [
                (vectors_hbm, vectors_ref),
                (weights_hbm, weights_ref),
                (vup_hbm, vup_ref),
                (cells_hbm, held.at[whole, left]),
                (cells_hbm.at[pl.ds(0, WINDOW)], held.at[wrap, left]),
                (up_hbm, held.at[whole, right]),
                (up_hbm.at[pl.ds(0, WINDOW)], held.at[wrap, right]),
                (shift_hbm, shift_ref),
            ]
        )
    ]
    for copy in copies:
        copy.start()
    for copy in copies[:5]:
        copy.wait()
    vectors = vectors_ref[...].astype(F32)
    cells = held[:CELLS_DEV, :CH]
    query = head_blocks(global_rows(vectors, weights_ref[0])).astype(BF)
    upstream = head_blocks(global_upstream(vup_ref[...], weights_ref[3]))
    up_parts = jnp.concatenate([part.astype(F32) for part in split3(upstream)], axis=0).astype(BF)
    w_kv = jnp.concatenate([weights_ref[1], weights_ref[2]], axis=1)
    key_value = dot(cells, w_kv).astype(BF)
    score = dot_nt(query, key_value[:, :CH]) * SCALE
    dprob = dot_nt(up_parts, key_value[:, CH:])
    dprob = dprob[:PAIRS] + dprob[PAIRS : 2 * PAIRS] + dprob[2 * PAIRS :]
    top = jnp.max(score, axis=1, keepdims=True)
    weight = jnp.exp(score - top)
    total = jnp.sum(weight, axis=1, keepdims=True)
    inner = jnp.sum(weight * dprob, axis=1, keepdims=True)
    lane = iota((PAIRS, CH), 1)
    stats = jnp.where(lane == 0, top, jnp.where(lane == 1, total, jnp.where(lane == 2, inner, 0.0)))
    parts = [part.astype(F32) for part in split3(stats)] + [jnp.zeros((PAIRS, CH), F32)]
    rows = jnp.concatenate(parts, axis=0).T[:GLOBALS].astype(BF)
    msg_ref[:, 2 * CUBOIDS] = jnp.broadcast_to(rows[None, :SPAN], (PEERS, SPAN, CH))
    for copy in copies[5:]:
        copy.wait()
    offset = tile_offset(shift_ref)
    base = offset - offset % 16
    mover = shift_matrix(offset % 16, GROUP_ROWS - 16, GROUP_ROWS)
    for first in range(0, PEERS, GROUP - 1):
        count = min(GROUP - 1, PEERS - first)
        start = pl.multiple_of((base + first * PEER_ROWS) % CELLS_DEV, 16)
        rows = held[pl.ds(start, GROUP_ROWS), :]
        moved = dot(mover[: count * PEER_ROWS], rows).astype(BF)
        peers = pl.ds(first, count)
        shape = (count, CUBOIDS, SPAN, CH)
        msg_ref[peers, 0:CUBOIDS] = moved[:, :CH].reshape(shape)
        msg_ref[peers, CUBOIDS : 2 * CUBOIDS] = moved[:, CH:].reshape(shape)


def vec_slots(rows):
    row, lane = iota((rows, CH), 0), iota((rows, CH), 1)
    return row, (row % SPAN == SPAN - 1) & (lane < VEC_LANES)


def owner_kernel(
    recv_ref,
    vectors_ref,
    weights_ref,
    vup_ref,
    msg_ref,
    cells_ref,
    up_ref,
    query_m,
    grad_m,
    w_sum,
    g_sum,
    low_ref,
    dkv_ref,
):
    vectors = vectors_ref[...].astype(F32)
    w_q, w_k, w_v, w_o = (weights_ref[i] for i in range(4))
    w_kv = jnp.concatenate([w_k, w_v], axis=1)
    w_qkv = jnp.concatenate([w_q, w_kv], axis=1)
    w_q_t = w_q.T
    gk = head_blocks(global_rows(vectors, w_k))
    gv = head_blocks(global_rows(vectors, w_v))
    gk_b, gv_b = gk.astype(BF), gv.astype(BF)
    zero = jnp.zeros((PAIRS, CH), F32)
    shared = {}

    def global_operands():
        gq = head_blocks(global_rows(vectors, w_q))
        gg = head_blocks(global_upstream(vup_ref[...], w_o))
        gg3 = [part.astype(F32) for part in split3(gg)]
        shared["gq_b"] = gq.astype(BF)
        for name, blocks in (("gk_t", gk), ("gv_t", gv)):
            wide = jnp.concatenate([blocks, zero, zero, zero], axis=0)
            shared[name] = wide.T[:, :PAIRS].astype(BF)
        shared["gg_parts"] = jnp.concatenate(gg3, axis=0).astype(BF)
        shared["more"] = diagonal(
            jnp.concatenate([gq, gq, zero, zero], axis=0),
            jnp.concatenate([gg3[0], gg3[0], gg3[1], zero], axis=0),
        )

    def global_softmax():
        stats = recv_ref[:, 2 * CUBOIDS].astype(F32).reshape(PEERS * SPAN, CH)
        stats = stats + pltpu.roll(stats, CH - PAIRS, 1) + pltpu.roll(stats, CH - 2 * PAIRS, 1)
        stats = stats.reshape(PEERS, SPAN, CH)
        tops = stats[:, 0:1, :]
        top = jnp.max(tops, axis=0)
        summed = jnp.sum(jnp.exp(tops - top[None]) * stats, axis=0)
        lanes = jnp.where(iota((SPAN, CH), 0) == 0, top, summed)
        columns = jnp.concatenate([lanes, jnp.zeros((CH - SPAN, CH), F32)], axis=0).T
        shared["g_top"] = columns[:PAIRS, 0:1]
        shared["g_inv"] = 1.0 / columns[:PAIRS, 1:2]
        shared["g_row"] = columns[:PAIRS, 2:3] * shared["g_inv"]

    def clear(slot):
        query_m[slot] = jnp.zeros(query_m.shape[1:], BF)
        grad_m[slot] = jnp.zeros(grad_m.shape[1:], BF)

    clear(0)

    def heads(h):
        return slice(h * HDIM, (h + 1) * HDIM)

    class Cuboid:
        def __init__(self, u):
            self.u, self.slot = u, u % 2
            self.low = []
            self.rows = {n: [[] for _ in range(HEADS)] for n in ("p", "ds", "out", "dq")}

        def project_query(self):
            cells = recv_ref[:, self.u].reshape(TOKENS, CH)
            cells_ref[self.u] = cells
            self.query_t = dot_nt(w_q_t, cells).astype(BF)
            for h in range(HEADS):
                query_m[self.slot, h, heads(h), :] = self.query_t[heads(h)]

        def project_grad(self):
            upstream = recv_ref[:, CUBOIDS + self.u].reshape(TOKENS, CH)
            up_ref[self.u] = upstream
            self.grad_t = dot_nt(w_o, upstream).astype(BF)
            for h in range(HEADS):
                grad_m[self.slot, h, heads(h), :] = self.grad_t[heads(h)]

        def project_keys(self):
            self.key_value = dot(cells_ref[self.u], w_kv).astype(BF)
            self.key, self.value = self.key_value[:, :CH], self.key_value[:, CH:]

        def project_global(self):
            self.s_global = dot(gk_b, self.query_t)
            self.d_global = dot(gv_b, self.grad_t)

        def project_transposed(self):
            self.key_t = self.key.T
            self.value_t = self.value.T

        def project_rows(self):
            self.query = self.query_t.T
            self.grad = self.grad_t.T

        def scores(self, h, q):
            columns = pl.ds(q, QUERIES)
            return (
                dot(self.key, query_m[self.slot, h, :, columns]),
                dot(self.value, grad_m[self.slot, h, :, columns]),
            )

        def softmax(self, h, q, score, dprob):
            rows = slice(h * GLOBALS, (h + 1) * GLOBALS)
            s_glob = self.s_global[rows, q : q + QUERIES]
            d_glob = self.d_global[rows, q : q + QUERIES]
            top = jnp.maximum(
                jnp.max(score, axis=0, keepdims=True), jnp.max(s_glob, axis=0, keepdims=True)
            )
            e_local = jnp.exp2((score - top) * (SCALE * LOG2E))
            e_global = jnp.exp2((s_glob - top) * (SCALE * LOG2E))
            total = jnp.sum(e_local, axis=0, keepdims=True) + jnp.sum(
                e_global, axis=0, keepdims=True
            )
            inv = 1.0 / total
            p_local = e_local * inv
            p_global = e_global * inv
            inner = jnp.sum(p_local * dprob, axis=0, keepdims=True) + jnp.sum(
                p_global * d_glob, axis=0, keepdims=True
            )
            self.rows["p"][h].append(p_global)
            self.rows["ds"][h].append(p_global * (d_glob - inner) * SCALE)
            return p_local.astype(BF), (p_local * (dprob - inner) * SCALE).astype(BF)

        def products(self, h, q, p_low, ds_low):
            part = heads(h)
            self.rows["out"][h].append(dot(self.value_t[part], p_low))
            self.rows["dq"][h].append(dot(self.key_t[part], ds_low))
            self.low.append((p_low, ds_low))
            if q + QUERIES == TOKENS:
                p_low, ds_low = (jnp.concatenate(x, axis=1) for x in zip(*self.low))
                self.low = []
                dkv_ref[self.slot, :, part] = dot(ds_low, self.query)[:, part]
                lanes = slice(CH + part.start, CH + part.stop)
                dkv_ref[self.slot, :, lanes] = dot(p_low, self.grad)[:, part]

        def add(self, ref, where, value):
            ref[where] = value if self.u == 0 else ref[where] + value

        def whole(self, name):
            rows = [jnp.concatenate(row, axis=1) for row in self.rows[name]]
            return jnp.concatenate(rows, axis=0)

        def finish_queries(self):
            p_rows, ds_rows = self.whole("p").astype(BF), self.whole("ds").astype(BF)
            self.out_t = (self.whole("out") + dot(shared["gv_t"], p_rows)).astype(BF)
            self.dq_t = (self.whole("dq") + dot(shared["gk_t"], ds_rows)).astype(BF)
            rows = jnp.concatenate([ds_rows, p_rows], axis=0)
            g_both = dot(rows, jnp.concatenate([self.query, self.grad], axis=1))
            self.add(g_sum, 1, g_both[:PAIRS, :CH])
            self.add(g_sum, 2, g_both[PAIRS:, CH:])

        def finish_global(self):
            score = dot(shared["gq_b"], self.key_t) * SCALE
            prob = jnp.exp(score - shared["g_top"]) * shared["g_inv"]
            dprob = dot(shared["gg_parts"], self.value_t)
            dprob = dprob[:PAIRS] + dprob[PAIRS : 2 * PAIRS] + dprob[2 * PAIRS :]
            dscore = prob * (dprob - shared["g_row"]) * SCALE
            p_hi, p_mid, _ = split3(prob)
            d_hi, d_mid, _ = split3(dscore)
            none = jnp.zeros((PAIRS, TOKENS), BF)
            self.parts = jnp.concatenate(
                [d_hi, d_mid, none, none, p_hi, p_mid, p_hi, none], axis=0
            )
            g_both = dot(
                jnp.concatenate([d_hi, d_mid, p_hi, p_mid], axis=0), self.key_value
            )
            self.add(g_sum, 0, g_both[:PAIRS, :CH] + g_both[PAIRS : 2 * PAIRS, :CH])
            self.add(g_sum, 3, g_both[2 * PAIRS : 3 * PAIRS, CH:] + g_both[3 * PAIRS :, CH:])

        def finish_keys(self):
            more = dot(self.parts.T, shared["more"])
            self.d_key_value = (dkv_ref[self.slot] + more).astype(BF)

        def finish_weights(self):
            self.grads = jnp.concatenate([self.dq_t.T, self.d_key_value], axis=1)
            everything = slice(None)
            first, last = slice(0, 3 * CH), slice(3 * CH, 4 * CH)
            self.add(w_sum, (everything, first), dot(cells_ref[self.u].T, self.grads))
            self.add(w_sum, (everything, last), dot(self.out_t, up_ref[self.u]))

        def finish_cells(self):
            delta = dot_nt(self.grads, w_qkv).astype(BF)
            msg_ref[:, self.u] = delta.reshape(PEERS, SPAN, CH)

        def before(self):
            return [
                self.project_query,
                self.project_grad,
                self.project_keys,
                self.project_global,
                self.project_transposed,
                self.project_rows,
            ]

        def after(self):
            return [
                self.finish_queries,
                self.finish_global,
                self.finish_keys,
                self.finish_weights,
                self.finish_cells,
            ]

    cuboids = [Cuboid(u) for u in range(CUBOIDS)]
    for task in cuboids[0].before():
        task()
    order = [(c, h, q) for c in cuboids for h in range(HEADS) for q in range(0, TOKENS, QUERIES)]
    per_cuboid = len(order) // CUBOIDS
    ready = cuboids[0].scores(*order[0][1:])
    low = None
    for i, (cuboid, *step) in enumerate(order):
        place = i % per_cuboid
        u = cuboid.u
        if place == 0:
            early = cuboids[u + 1].before() if u + 1 < CUBOIDS else []
            if u == 0:
                early.insert(0, lambda: clear(1))
            late = cuboids[u - 1].after() if u > 0 else [global_operands, global_softmax]
        following = None
        if place + 1 == per_cuboid:
            for task in early + late:
                task()
        if i + 1 < len(order):
            following = order[i + 1][0].scores(*order[i + 1][1:])
        now = cuboid.softmax(*step, *ready)
        if low is not None:
            order[i - 1][0].products(*order[i - 1][1:], *low)
        if place > 0 and late:
            late.pop(0)()
        low = now
        if early:
            early.pop(0)()
        ready = following
    order[-1][0].products(*order[-1][1:], *low)
    for task in cuboids[-1].after():
        task()

    def tall(pieces):
        rows = jnp.concatenate(pieces, axis=0)
        return jnp.concatenate([rows, jnp.zeros((CH - rows.shape[0], CH), F32)], axis=0)

    def parts_of(rows):
        return [part.astype(F32) for part in split3(rows)]

    g_parts = [parts_of(head_diagonal(g_sum[i])) for i in range(3)]
    g_tall = jnp.concatenate([tall(parts) for parts in g_parts], axis=1).astype(BF)
    w_sum[:, : 3 * CH] += dot(tall([vectors] * 3).T.astype(BF), g_tall)
    a_hi, a_mid, a_low = parts_of(head_diagonal(g_sum[3]))
    u_hi, u_mid, u_low = parts_of(vup_ref[...])
    left = tall([a_hi, a_hi, a_hi, a_mid, a_mid, a_low]).T.astype(BF)
    w_sum[:, 3 * CH :] += dot(left, tall([u_hi, u_mid, u_low, u_hi, u_mid, u_hi]).astype(BF))
    vec = dot_nt(g_tall[: 4 * GLOBALS], w_qkv)
    vec = vec[:GLOBALS] + vec[GLOBALS : 2 * GLOBALS] + vec[2 * GLOBALS : 3 * GLOBALS]
    for i in range(4):
        total = w_sum[:, i * CH : (i + 1) * CH]
        high = total.astype(BF)
        peers = pl.ds(i * PIECE_GROUP, PIECE_GROUP)
        msg_ref[peers, CUBOIDS] = high.reshape(PIECE_GROUP, SPAN, CH)
        low_ref[pl.ds(i * CH, CH), :] = total - high.astype(F32)
    hi, mid, _ = split3(vec)
    vec_parts = jnp.concatenate(
        [hi.astype(F32), mid.astype(F32), jnp.zeros((CH - VEC_LANES, CH), F32)], axis=0
    ).T.astype(BF)
    row, slots = vec_slots(TOKENS)
    spread = (iota((TOKENS, CH), 0) // SPAN == iota((TOKENS, CH), 1)).astype(BF)
    low_rows = jnp.where(slots, dot(spread, vec_parts), low_ref[...]).astype(BF)
    msg_ref[:, CUBOIDS + 1] = low_rows.reshape(PEERS, SPAN, CH)


def sum_kernel(recv_ref, piece_ref):
    summed = jnp.sum(recv_ref[:, CUBOIDS:].astype(F32), axis=0)
    summed = jnp.concatenate([summed[0], summed[1]], axis=0)
    row, slots = vec_slots(PIECE_ROWS)
    slots = slots & (row >= SPAN)
    vec = summed + pltpu.roll(summed, CH - GLOBALS, 1)
    low = jnp.where(slots, 0.0, summed)
    weight = summed[:SPAN] + low[SPAN:]
    high = weight.astype(BF).astype(F32)
    vec_high = vec.astype(BF).astype(F32)
    vec_low = pltpu.roll(vec - vec_high, GLOBALS, 1)
    vec = jnp.where(iota((PIECE_ROWS, CH), 1) < GLOBALS, vec_high, vec_low)
    piece = jnp.where(slots, vec, jnp.concatenate([high, weight - high], axis=0))
    for i in range(2):
        rows = piece[i * SPAN : (i + 1) * SPAN].astype(BF)
        piece_ref[:, i] = jnp.broadcast_to(rows[None], (PEERS, SPAN, CH))


def spread_kernel(recv_ref, weight_ref, vec_ref):
    high = recv_ref[:, 0].reshape(TOKENS, CH)
    low = recv_ref[:, 1].reshape(TOKENS, CH)
    _, slots = vec_slots(TOKENS)
    weight = high.astype(F32) + jnp.where(slots, 0.0, low.astype(F32))
    weight_ref[...] = weight.reshape(4, CH, CH)
    target, source = iota((PEERS, TOKENS), 0), iota((PEERS, TOKENS), 1)
    vec = dot((source == target * SPAN + SPAN - 1).astype(BF), low).T
    vec_ref[...] = vec[:GLOBALS] + vec[GLOBALS : 2 * GLOBALS]


def place_kernel(shift_hbm, recv_ref, out_ref, held, shift_ref, sem):
    copy = pltpu.make_async_copy(shift_hbm, shift_ref, sem)
    copy.start()
    for i in range(PEERS // GROUP):
        held[pl.ds(i * GROUP_ROWS, GROUP_ROWS), :] = recv_ref[
            pl.ds(i * GROUP, GROUP), 0:CUBOIDS
        ].reshape(GROUP_ROWS, CH)
    held[CELLS_DEV:, :] = held[:WINDOW, :]
    copy.wait()
    offset = (CELLS_DEV - tile_offset(shift_ref)) % CELLS_DEV
    mover = shift_matrix(offset % 16, GROUP_ROWS, WINDOW)
    base = offset - offset % 16
    for i in range(CELLS_DEV // GROUP_ROWS):
        start = pl.multiple_of((base + i * GROUP_ROWS) % CELLS_DEV, 16)
        moved = dot(mover, held[pl.ds(start, WINDOW), :]).astype(BF)
        out_ref[pl.ds(i * GROUP_ROWS, GROUP_ROWS), :] = moved


VMEM = pl.BlockSpec(memory_space=pltpu.VMEM)
HBM = pl.BlockSpec(memory_space=pltpu.HBM)
PACK_PARAMS = pltpu.CompilerParams(vmem_limit_bytes=58_000_000)
PARAMS = pltpu.CompilerParams(vmem_limit_bytes=48 * 1024 * 1024)


def exchange(rows):
    return lax.all_to_all(rows, ("tile", "frame"), split_axis=0, concat_axis=0, tiled=True)


def body(cells, vectors, weights, cuboid_shift, cell_upstream, vector_upstream):
    message = pl.pallas_call(
        pack_kernel,
        out_shape=pltpu.VMEM((PEERS, MSG_SPANS, SPAN, CH), BF),
        in_specs=[HBM] * 6,
        out_specs=VMEM,
        scratch_shapes=[
            pltpu.VMEM((CELLS_DEV + WINDOW, 2 * CH), BF),
            pltpu.VMEM((GLOBALS, CH), BF),
            pltpu.VMEM((4, CH, CH), BF),
            pltpu.VMEM((GLOBALS, CH), F32),
            pltpu.SMEM((1,), jnp.int32),
            pltpu.SemaphoreType.DMA((8,)),
        ],
        compiler_params=PACK_PARAMS,
        name="pack",
    )(cuboid_shift, cells[0], cell_upstream[0], vectors, weights, vector_upstream)
    received = exchange(message)
    message = pl.pallas_call(
        owner_kernel,
        out_shape=pltpu.VMEM((PEERS, CUBOIDS + 2, SPAN, CH), BF),
        in_specs=[VMEM] * 4,
        out_specs=VMEM,
        scratch_shapes=[
            pltpu.VMEM((CUBOIDS, TOKENS, CH), BF),
            pltpu.VMEM((CUBOIDS, TOKENS, CH), BF),
            pltpu.VMEM((2, HEADS, CH, TOKENS), BF),
            pltpu.VMEM((2, HEADS, CH, TOKENS), BF),
            pltpu.VMEM((CH, 4 * CH), F32),
            pltpu.VMEM((4, PAIRS, CH), F32),
            pltpu.VMEM((TOKENS, CH), F32),
            pltpu.VMEM((2, TOKENS, 2 * CH), F32),
        ],
        compiler_params=PARAMS,
        name="owner",
    )(received, vectors, weights, vector_upstream)
    received = exchange(message)
    pieces = pl.pallas_call(
        sum_kernel,
        out_shape=pltpu.VMEM((PEERS, 2, SPAN, CH), BF),
        in_specs=[VMEM],
        out_specs=VMEM,
        compiler_params=PARAMS,
        name="sum_pieces",
    )(received)
    pieces = exchange(pieces)
    cell_grad = pl.pallas_call(
        place_kernel,
        out_shape=jax.ShapeDtypeStruct((CELLS_DEV, CH), BF),
        in_specs=[HBM, VMEM],
        out_specs=VMEM,
        scratch_shapes=[
            pltpu.VMEM((CELLS_DEV + WINDOW, CH), BF),
            pltpu.SMEM((1,), jnp.int32),
            pltpu.SemaphoreType.DMA,
        ],
        compiler_params=PARAMS,
        name="place",
    )(cuboid_shift, received)
    weight_grad, vector_grad = pl.pallas_call(
        spread_kernel,
        out_shape=[
            jax.ShapeDtypeStruct((4, CH, CH), F32),
            jax.ShapeDtypeStruct((GLOBALS, CH), F32),
        ],
        in_specs=[VMEM],
        out_specs=[VMEM, VMEM],
        compiler_params=PARAMS,
        name="spread",
    )(pieces)
    return cell_grad[None], weight_grad, vector_grad


def solution(mesh):
    in_specs = (P("frame", "tile", None), P(), P(), P(), P("frame", "tile", None), P())
    out_specs = (P("frame", "tile", None), P(), P())
    return jax.shard_map(body, mesh=mesh, in_specs=in_specs, out_specs=out_specs, check_vma=False)
```

```python
import math

import jax
import jax.numpy as jnp
from jax import lax
from jax.experimental import pallas as pl
from jax.experimental.pallas import tpu as pltpu
from jax.sharding import PartitionSpec as P

CH = 128
HEADS = 4
HDIM = 32
GLOBALS = 8
PAIRS = HEADS * GLOBALS
SPAN = 4
CELLS_DEV = 2048
PEERS = 128
PEER_ROWS = CELLS_DEV // PEERS
CUBOIDS = PEER_ROWS // SPAN
TOKENS = 512
QUERIES = 256
GROUP = 16
GROUP_ROWS = GROUP * PEER_ROWS
WINDOW = GROUP_ROWS + 16
MSG_SPANS = 9
PIECE_ROWS = 2 * SPAN
PIECE_GROUP = 32
VEC_LANES = 2 * GLOBALS
SCALE = HDIM**-0.5
LOG2E = math.log2(math.e)
BF = jnp.bfloat16
F32 = jnp.float32
NT = (((1,), (1,)), ((), ()))


def dot(a, b):
    return jnp.dot(a, b, preferred_element_type=F32)


def dot_nt(a, b):
    return lax.dot_general(a, b, NT, preferred_element_type=F32)


def iota(shape, axis):
    return lax.broadcasted_iota(jnp.int32, shape, axis)


def split3(x):
    hi = x.astype(BF)
    rest = x - hi.astype(F32)
    mid = rest.astype(BF)
    low = (rest - mid.astype(F32)).astype(BF)
    return hi, mid, low


def head_blocks(rows):
    head = iota((GLOBALS, CH), 1) // HDIM
    return jnp.concatenate([jnp.where(head == h, rows, 0.0) for h in range(HEADS)], axis=0)


def diagonal(first, second):
    zero = jnp.zeros((CH, CH), F32)
    rows = [jnp.concatenate([first, zero], axis=1), jnp.concatenate([zero, second], axis=1)]
    return jnp.concatenate(rows, axis=0).astype(BF)


def head_diagonal(blocks):
    head = iota((GLOBALS, CH), 1) // HDIM
    total = jnp.zeros((GLOBALS, CH), F32)
    for h in range(HEADS):
        total += jnp.where(head == h, blocks[h * GLOBALS : (h + 1) * GLOBALS], 0.0)
    return total


def global_rows(vectors, weight):
    return dot(vectors.astype(BF), weight).astype(BF).astype(F32)


def global_upstream(vector_upstream, w_out):
    hi, mid, low = split3(vector_upstream)
    return dot_nt(hi, w_out) + dot_nt(mid, w_out) + dot_nt(low, w_out)


def tile_offset(shift_ref):
    return (shift_ref[0] * (lax.axis_index("tile") + 1)) % CELLS_DEV


def shift_matrix(step, rows, window):
    return (iota((rows, window), 1) == iota((rows, window), 0) + step).astype(BF)


def pack_kernel(
    shift_hbm,
    cells_hbm,
    up_hbm,
    vectors_hbm,
    weights_hbm,
    vup_hbm,
    msg_ref,
    held,
    vectors_ref,
    weights_ref,
    vup_ref,
    shift_ref,
    sems,
):
    whole, wrap = pl.ds(0, CELLS_DEV), pl.ds(CELLS_DEV, WINDOW)
    left, right = pl.ds(0, CH), pl.ds(CH, CH)
    copies = [
        pltpu.make_async_copy(source, target, sems.at[i])
        for i, (source, target) in enumerate(
            [
                (vectors_hbm, vectors_ref),
                (weights_hbm, weights_ref),
                (vup_hbm, vup_ref),
                (cells_hbm, held.at[whole, left]),
                (cells_hbm.at[pl.ds(0, WINDOW)], held.at[wrap, left]),
                (up_hbm, held.at[whole, right]),
                (up_hbm.at[pl.ds(0, WINDOW)], held.at[wrap, right]),
                (shift_hbm, shift_ref),
            ]
        )
    ]
    for copy in copies:
        copy.start()
    for copy in copies[:5]:
        copy.wait()
    vectors = vectors_ref[...].astype(F32)
    cells = held[:CELLS_DEV, :CH]
    query = head_blocks(global_rows(vectors, weights_ref[0])).astype(BF)
    upstream = head_blocks(global_upstream(vup_ref[...], weights_ref[3]))
    up_parts = jnp.concatenate([part.astype(F32) for part in split3(upstream)], axis=0).astype(BF)
    w_kv = jnp.concatenate([weights_ref[1], weights_ref[2]], axis=1)
    key_value = dot(cells, w_kv).astype(BF)
    score = dot_nt(query, key_value[:, :CH]) * SCALE
    dprob = dot_nt(up_parts, key_value[:, CH:])
    dprob = dprob[:PAIRS] + dprob[PAIRS : 2 * PAIRS] + dprob[2 * PAIRS :]
    top = jnp.max(score, axis=1, keepdims=True)
    weight = jnp.exp(score - top)
    total = jnp.sum(weight, axis=1, keepdims=True)
    inner = jnp.sum(weight * dprob, axis=1, keepdims=True)
    lane = iota((PAIRS, CH), 1)
    stats = jnp.where(lane == 0, top, jnp.where(lane == 1, total, jnp.where(lane == 2, inner, 0.0)))
    parts = [part.astype(F32) for part in split3(stats)] + [jnp.zeros((PAIRS, CH), F32)]
    rows = jnp.concatenate(parts, axis=0).T[:GLOBALS].astype(BF)
    msg_ref[:, 2 * CUBOIDS] = jnp.broadcast_to(rows[None, :SPAN], (PEERS, SPAN, CH))
    for copy in copies[5:]:
        copy.wait()
    offset = tile_offset(shift_ref)
    base = offset - offset % 16
    mover = shift_matrix(offset % 16, GROUP_ROWS - 16, GROUP_ROWS)
    for first in range(0, PEERS, GROUP - 1):
        count = min(GROUP - 1, PEERS - first)
        start = pl.multiple_of((base + first * PEER_ROWS) % CELLS_DEV, 16)
        rows = held[pl.ds(start, GROUP_ROWS), :]
        moved = dot(mover[: count * PEER_ROWS], rows).astype(BF)
        peers = pl.ds(first, count)
        shape = (count, CUBOIDS, SPAN, CH)
        msg_ref[peers, 0:CUBOIDS] = moved[:, :CH].reshape(shape)
        msg_ref[peers, CUBOIDS : 2 * CUBOIDS] = moved[:, CH:].reshape(shape)


def vec_slots(rows):
    row, lane = iota((rows, CH), 0), iota((rows, CH), 1)
    return row, (row % SPAN == SPAN - 1) & (lane < VEC_LANES)


def owner_kernel(
    recv_ref,
    vectors_ref,
    weights_ref,
    vup_ref,
    msg_ref,
    cells_ref,
    up_ref,
    query_m,
    grad_m,
    w_sum,
    g_sum,
    low_ref,
    dkv_ref,
):
    vectors = vectors_ref[...].astype(F32)
    w_q, w_k, w_v, w_o = (weights_ref[i] for i in range(4))
    w_kv = jnp.concatenate([w_k, w_v], axis=1)
    w_qkv = jnp.concatenate([w_q, w_kv], axis=1)
    w_q_t = w_q.T
    gk = head_blocks(global_rows(vectors, w_k))
    gv = head_blocks(global_rows(vectors, w_v))
    gk_b, gv_b = gk.astype(BF), gv.astype(BF)
    zero = jnp.zeros((PAIRS, CH), F32)
    shared = {}

    def global_operands():
        gq = head_blocks(global_rows(vectors, w_q))
        gg = head_blocks(global_upstream(vup_ref[...], w_o))
        gg3 = [part.astype(F32) for part in split3(gg)]
        shared["gq_b"] = gq.astype(BF)
        for name, blocks in (("gk_t", gk), ("gv_t", gv)):
            wide = jnp.concatenate([blocks, zero, zero, zero], axis=0)
            shared[name] = wide.T[:, :PAIRS].astype(BF)
        shared["gg_parts"] = jnp.concatenate(gg3, axis=0).astype(BF)
        shared["more"] = diagonal(
            jnp.concatenate([gq, gq, zero, zero], axis=0),
            jnp.concatenate([gg3[0], gg3[0], gg3[1], zero], axis=0),
        )

    def global_softmax():
        stats = recv_ref[:, 2 * CUBOIDS].astype(F32).reshape(PEERS * SPAN, CH)
        stats = stats + pltpu.roll(stats, CH - PAIRS, 1) + pltpu.roll(stats, CH - 2 * PAIRS, 1)
        stats = stats.reshape(PEERS, SPAN, CH)
        tops = stats[:, 0:1, :]
        top = jnp.max(tops, axis=0)
        summed = jnp.sum(jnp.exp(tops - top[None]) * stats, axis=0)
        lanes = jnp.where(iota((SPAN, CH), 0) == 0, top, summed)
        columns = jnp.concatenate([lanes, jnp.zeros((CH - SPAN, CH), F32)], axis=0).T
        shared["g_top"] = columns[:PAIRS, 0:1]
        shared["g_inv"] = 1.0 / columns[:PAIRS, 1:2]
        shared["g_row"] = columns[:PAIRS, 2:3] * shared["g_inv"]

    def clear(slot):
        query_m[slot] = jnp.zeros(query_m.shape[1:], BF)
        grad_m[slot] = jnp.zeros(grad_m.shape[1:], BF)

    clear(0)

    def heads(h):
        return slice(h * HDIM, (h + 1) * HDIM)

    class Cuboid:
        def __init__(self, u):
            self.u, self.slot = u, u % 2
            self.low = []
            self.rows = {n: [[] for _ in range(HEADS)] for n in ("p", "ds", "out", "dq")}

        def project_query(self):
            cells = recv_ref[:, self.u].reshape(TOKENS, CH)
            cells_ref[self.u] = cells
            self.query_t = dot_nt(w_q_t, cells).astype(BF)
            for h in range(HEADS):
                query_m[self.slot, h, heads(h), :] = self.query_t[heads(h)]

        def project_grad(self):
            upstream = recv_ref[:, CUBOIDS + self.u].reshape(TOKENS, CH)
            up_ref[self.u] = upstream
            self.grad_t = dot_nt(w_o, upstream).astype(BF)
            for h in range(HEADS):
                grad_m[self.slot, h, heads(h), :] = self.grad_t[heads(h)]

        def project_keys(self):
            self.key_value = dot(cells_ref[self.u], w_kv).astype(BF)
            self.key, self.value = self.key_value[:, :CH], self.key_value[:, CH:]

        def project_global(self):
            self.s_global = dot(gk_b, self.query_t)
            self.d_global = dot(gv_b, self.grad_t)

        def project_transposed(self):
            self.key_t = self.key.T
            self.value_t = self.value.T

        def project_rows(self):
            self.query = self.query_t.T
            self.grad = self.grad_t.T

        def scores(self, h, q):
            columns = pl.ds(q, QUERIES)
            return (
                dot(self.key, query_m[self.slot, h, :, columns]),
                dot(self.value, grad_m[self.slot, h, :, columns]),
            )

        def softmax(self, h, q, score, dprob):
            rows = slice(h * GLOBALS, (h + 1) * GLOBALS)
            s_glob = self.s_global[rows, q : q + QUERIES]
            d_glob = self.d_global[rows, q : q + QUERIES]
            top = jnp.maximum(
                jnp.max(score, axis=0, keepdims=True), jnp.max(s_glob, axis=0, keepdims=True)
            )
            e_local = jnp.exp2((score - top) * (SCALE * LOG2E))
            e_global = jnp.exp2((s_glob - top) * (SCALE * LOG2E))
            total = jnp.sum(e_local, axis=0, keepdims=True) + jnp.sum(
                e_global, axis=0, keepdims=True
            )
            inv = 1.0 / total
            p_local = e_local * inv
            p_global = e_global * inv
            inner = jnp.sum(p_local * dprob, axis=0, keepdims=True) + jnp.sum(
                p_global * d_glob, axis=0, keepdims=True
            )
            self.rows["p"][h].append(p_global)
            self.rows["ds"][h].append(p_global * (d_glob - inner) * SCALE)
            return p_local.astype(BF), (p_local * (dprob - inner) * SCALE).astype(BF)

        def products(self, h, q, p_low, ds_low):
            part = heads(h)
            self.rows["out"][h].append(dot(self.value_t[part], p_low))
            self.rows["dq"][h].append(dot(self.key_t[part], ds_low))
            self.low.append((p_low, ds_low))
            if q + QUERIES == TOKENS:
                p_low, ds_low = (jnp.concatenate(x, axis=1) for x in zip(*self.low))
                self.low = []
                dkv_ref[self.slot, :, part] = dot(ds_low, self.query)[:, part]
                lanes = slice(CH + part.start, CH + part.stop)
                dkv_ref[self.slot, :, lanes] = dot(p_low, self.grad)[:, part]

        def add(self, ref, where, value):
            ref[where] = value if self.u == 0 else ref[where] + value

        def whole(self, name):
            rows = [jnp.concatenate(row, axis=1) for row in self.rows[name]]
            return jnp.concatenate(rows, axis=0)

        def finish_queries(self):
            p_rows, ds_rows = self.whole("p").astype(BF), self.whole("ds").astype(BF)
            self.out_t = (self.whole("out") + dot(shared["gv_t"], p_rows)).astype(BF)
            self.dq_t = (self.whole("dq") + dot(shared["gk_t"], ds_rows)).astype(BF)
            rows = jnp.concatenate([ds_rows, p_rows], axis=0)
            g_both = dot(rows, jnp.concatenate([self.query, self.grad], axis=1))
            self.add(g_sum, 1, g_both[:PAIRS, :CH])
            self.add(g_sum, 2, g_both[PAIRS:, CH:])

        def finish_global(self):
            score = dot(shared["gq_b"], self.key_t) * SCALE
            prob = jnp.exp(score - shared["g_top"]) * shared["g_inv"]
            dprob = dot(shared["gg_parts"], self.value_t)
            dprob = dprob[:PAIRS] + dprob[PAIRS : 2 * PAIRS] + dprob[2 * PAIRS :]
            dscore = prob * (dprob - shared["g_row"]) * SCALE
            p_hi, p_mid, _ = split3(prob)
            d_hi, d_mid, _ = split3(dscore)
            none = jnp.zeros((PAIRS, TOKENS), BF)
            self.parts = jnp.concatenate(
                [d_hi, d_mid, none, none, p_hi, p_mid, p_hi, none], axis=0
            )
            g_both = dot(
                jnp.concatenate([d_hi, d_mid, p_hi, p_mid], axis=0), self.key_value
            )
            self.add(g_sum, 0, g_both[:PAIRS, :CH] + g_both[PAIRS : 2 * PAIRS, :CH])
            self.add(g_sum, 3, g_both[2 * PAIRS : 3 * PAIRS, CH:] + g_both[3 * PAIRS :, CH:])

        def finish_keys(self):
            more = dot(self.parts.T, shared["more"])
            self.d_key_value = (dkv_ref[self.slot] + more).astype(BF)

        def finish_weights(self):
            self.grads = jnp.concatenate([self.dq_t.T, self.d_key_value], axis=1)
            everything = slice(None)
            first, last = slice(0, 3 * CH), slice(3 * CH, 4 * CH)
            self.add(w_sum, (everything, first), dot(cells_ref[self.u].T, self.grads))
            self.add(w_sum, (everything, last), dot(self.out_t, up_ref[self.u]))

        def finish_cells(self):
            delta = dot_nt(self.grads, w_qkv).astype(BF)
            msg_ref[:, self.u] = delta.reshape(PEERS, SPAN, CH)

        def before(self):
            return [
                self.project_query,
                self.project_grad,
                self.project_keys,
                self.project_global,
                self.project_transposed,
                self.project_rows,
            ]

        def after(self):
            return [
                self.finish_queries,
                self.finish_global,
                self.finish_keys,
                self.finish_weights,
                self.finish_cells,
            ]

    cuboids = [Cuboid(u) for u in range(CUBOIDS)]
    for task in cuboids[0].before():
        task()
    order = [(c, h, q) for c in cuboids for h in range(HEADS) for q in range(0, TOKENS, QUERIES)]
    per_cuboid = len(order) // CUBOIDS
    ready = cuboids[0].scores(*order[0][1:])
    low = None
    for i, (cuboid, *step) in enumerate(order):
        place = i % per_cuboid
        u = cuboid.u
        if place == 0:
            early = cuboids[u + 1].before() if u + 1 < CUBOIDS else []
            if u == 0:
                early.insert(0, lambda: clear(1))
            late = cuboids[u - 1].after() if u > 0 else [global_operands, global_softmax]
        following = None
        if place + 1 == per_cuboid:
            for task in early + late:
                task()
        if i + 1 < len(order):
            following = order[i + 1][0].scores(*order[i + 1][1:])
        now = cuboid.softmax(*step, *ready)
        if low is not None:
            order[i - 1][0].products(*order[i - 1][1:], *low)
        if place > 0 and late:
            late.pop(0)()
        low = now
        if early:
            early.pop(0)()
        ready = following
    order[-1][0].products(*order[-1][1:], *low)
    for task in cuboids[-1].after():
        task()

    def tall(pieces):
        rows = jnp.concatenate(pieces, axis=0)
        return jnp.concatenate([rows, jnp.zeros((CH - rows.shape[0], CH), F32)], axis=0)

    def parts_of(rows):
        return [part.astype(F32) for part in split3(rows)]

    g_parts = [parts_of(head_diagonal(g_sum[i])) for i in range(3)]
    g_tall = jnp.concatenate([tall(parts) for parts in g_parts], axis=1).astype(BF)
    w_sum[:, : 3 * CH] += dot(tall([vectors] * 3).T.astype(BF), g_tall)
    a_hi, a_mid, a_low = parts_of(head_diagonal(g_sum[3]))
    u_hi, u_mid, u_low = parts_of(vup_ref[...])
    left = tall([a_hi, a_hi, a_hi, a_mid, a_mid, a_low]).T.astype(BF)
    w_sum[:, 3 * CH :] += dot(left, tall([u_hi, u_mid, u_low, u_hi, u_mid, u_hi]).astype(BF))
    vec = dot_nt(g_tall[: 4 * GLOBALS], w_qkv)
    vec = vec[:GLOBALS] + vec[GLOBALS : 2 * GLOBALS] + vec[2 * GLOBALS : 3 * GLOBALS]
    for i in range(4):
        total = w_sum[:, i * CH : (i + 1) * CH]
        high = total.astype(BF)
        peers = pl.ds(i * PIECE_GROUP, PIECE_GROUP)
        msg_ref[peers, CUBOIDS] = high.reshape(PIECE_GROUP, SPAN, CH)
        low_ref[pl.ds(i * CH, CH), :] = total - high.astype(F32)
    hi, mid, _ = split3(vec)
    vec_parts = jnp.concatenate(
        [hi.astype(F32), mid.astype(F32), jnp.zeros((CH - VEC_LANES, CH), F32)], axis=0
    ).T.astype(BF)
    row, slots = vec_slots(TOKENS)
    spread = (iota((TOKENS, CH), 0) // SPAN == iota((TOKENS, CH), 1)).astype(BF)
    low_rows = jnp.where(slots, dot(spread, vec_parts), low_ref[...]).astype(BF)
    msg_ref[:, CUBOIDS + 1] = low_rows.reshape(PEERS, SPAN, CH)


def sum_kernel(recv_ref, piece_hbm, piece_ref, sems):
    summed = jnp.sum(recv_ref[:, CUBOIDS:].astype(F32), axis=0)
    summed = jnp.concatenate([summed[0], summed[1]], axis=0)
    row, slots = vec_slots(PIECE_ROWS)
    slots = slots & (row >= SPAN)
    vec = summed + pltpu.roll(summed, CH - GLOBALS, 1)
    low = jnp.where(slots, 0.0, summed)
    weight = summed[:SPAN] + low[SPAN:]
    high = weight.astype(BF).astype(F32)
    vec_high = vec.astype(BF).astype(F32)
    vec_low = pltpu.roll(vec - vec_high, GLOBALS, 1)
    vec = jnp.where(iota((PIECE_ROWS, CH), 1) < GLOBALS, vec_high, vec_low)
    piece = jnp.where(slots, vec, jnp.concatenate([high, weight - high], axis=0))
    for i in range(2):
        rows = piece[i * SPAN : (i + 1) * SPAN].astype(BF)
        piece_ref[:, i] = jnp.broadcast_to(rows[None], (PIECE_GROUP, SPAN, CH))
    copies = [
        pltpu.make_async_copy(
            piece_ref, piece_hbm.at[pl.ds(i * PIECE_GROUP, PIECE_GROUP)], sems.at[i]
        )
        for i in range(PEERS // PIECE_GROUP)
    ]
    for copy in copies:
        copy.start()
    for copy in copies:
        copy.wait()


def spread_kernel(recv_ref, weight_ref, vec_ref):
    high = recv_ref[:, 0].reshape(TOKENS, CH)
    low = recv_ref[:, 1].reshape(TOKENS, CH)
    _, slots = vec_slots(TOKENS)
    weight = high.astype(F32) + jnp.where(slots, 0.0, low.astype(F32))
    weight_ref[...] = weight.reshape(4, CH, CH)
    target, source = iota((PEERS, TOKENS), 0), iota((PEERS, TOKENS), 1)
    vec = dot((source == target * SPAN + SPAN - 1).astype(BF), low).T
    vec_ref[...] = vec[:GLOBALS] + vec[GLOBALS : 2 * GLOBALS]


def place_kernel(shift_hbm, recv_ref, out_ref, held, shift_ref, sem):
    copy = pltpu.make_async_copy(shift_hbm, shift_ref, sem)
    copy.start()
    for i in range(PEERS // GROUP):
        held[pl.ds(i * GROUP_ROWS, GROUP_ROWS), :] = recv_ref[
            pl.ds(i * GROUP, GROUP), 0:CUBOIDS
        ].reshape(GROUP_ROWS, CH)
    held[CELLS_DEV:, :] = held[:WINDOW, :]
    copy.wait()
    offset = (CELLS_DEV - tile_offset(shift_ref)) % CELLS_DEV
    mover = shift_matrix(offset % 16, GROUP_ROWS, WINDOW)
    base = offset - offset % 16
    for i in range(CELLS_DEV // GROUP_ROWS):
        start = pl.multiple_of((base + i * GROUP_ROWS) % CELLS_DEV, 16)
        moved = dot(mover, held[pl.ds(start, WINDOW), :]).astype(BF)
        out_ref[pl.ds(i * GROUP_ROWS, GROUP_ROWS), :] = moved


VMEM = pl.BlockSpec(memory_space=pltpu.VMEM)
HBM = pl.BlockSpec(memory_space=pltpu.HBM)
PACK_PARAMS = pltpu.CompilerParams(vmem_limit_bytes=58_000_000)
PARAMS = pltpu.CompilerParams(vmem_limit_bytes=48 * 1024 * 1024)


def exchange(rows):
    return lax.all_to_all(rows, ("tile", "frame"), split_axis=0, concat_axis=0, tiled=True)


def body(cells, vectors, weights, cuboid_shift, cell_upstream, vector_upstream):
    message = pl.pallas_call(
        pack_kernel,
        out_shape=pltpu.VMEM((PEERS, MSG_SPANS, SPAN, CH), BF),
        in_specs=[HBM] * 6,
        out_specs=VMEM,
        scratch_shapes=[
            pltpu.VMEM((CELLS_DEV + WINDOW, 2 * CH), BF),
            pltpu.VMEM((GLOBALS, CH), BF),
            pltpu.VMEM((4, CH, CH), BF),
            pltpu.VMEM((GLOBALS, CH), F32),
            pltpu.SMEM((1,), jnp.int32),
            pltpu.SemaphoreType.DMA((8,)),
        ],
        compiler_params=PACK_PARAMS,
        name="pack",
    )(cuboid_shift, cells[0], cell_upstream[0], vectors, weights, vector_upstream)
    received = exchange(message)
    message = pl.pallas_call(
        owner_kernel,
        out_shape=pltpu.VMEM((PEERS, CUBOIDS + 2, SPAN, CH), BF),
        in_specs=[VMEM] * 4,
        out_specs=VMEM,
        scratch_shapes=[
            pltpu.VMEM((CUBOIDS, TOKENS, CH), BF),
            pltpu.VMEM((CUBOIDS, TOKENS, CH), BF),
            pltpu.VMEM((2, HEADS, CH, TOKENS), BF),
            pltpu.VMEM((2, HEADS, CH, TOKENS), BF),
            pltpu.VMEM((CH, 4 * CH), F32),
            pltpu.VMEM((4, PAIRS, CH), F32),
            pltpu.VMEM((TOKENS, CH), F32),
            pltpu.VMEM((2, TOKENS, 2 * CH), F32),
        ],
        compiler_params=PARAMS,
        name="owner",
    )(received, vectors, weights, vector_upstream)
    received = exchange(message)
    pieces = pl.pallas_call(
        sum_kernel,
        out_shape=jax.ShapeDtypeStruct((PEERS, 2, SPAN, CH), BF),
        in_specs=[VMEM],
        out_specs=HBM,
        scratch_shapes=[
            pltpu.VMEM((PIECE_GROUP, 2, SPAN, CH), BF),
            pltpu.SemaphoreType.DMA((PEERS // PIECE_GROUP,)),
        ],
        compiler_params=PARAMS,
        name="sum_pieces",
    )(received)
    pieces = exchange(pieces)
    cell_grad = pl.pallas_call(
        place_kernel,
        out_shape=jax.ShapeDtypeStruct((CELLS_DEV, CH), BF),
        in_specs=[HBM, VMEM],
        out_specs=VMEM,
        scratch_shapes=[
            pltpu.VMEM((CELLS_DEV + WINDOW, CH), BF),
            pltpu.SMEM((1,), jnp.int32),
            pltpu.SemaphoreType.DMA,
        ],
        compiler_params=PARAMS,
        name="place",
    )(cuboid_shift, received)
    weight_grad, vector_grad = pl.pallas_call(
        spread_kernel,
        out_shape=[
            jax.ShapeDtypeStruct((4, CH, CH), F32),
            jax.ShapeDtypeStruct((GLOBALS, CH), F32),
        ],
        in_specs=[VMEM],
        out_specs=[VMEM, VMEM],
        compiler_params=PARAMS,
        name="spread",
    )(pieces)
    return cell_grad[None], weight_grad, vector_grad


def solution(mesh):
    in_specs = (P("frame", "tile", None), P(), P(), P(), P("frame", "tile", None), P())
    out_specs = (P("frame", "tile", None), P(), P())
    return jax.shard_map(body, mesh=mesh, in_specs=in_specs, out_specs=out_specs, check_vma=False)
```
